512 devices in a mesh: row: 32 (over x, y), col: 16 (over z, core).
Axes of the slice: x: 4, y: 8, z: 8, core: 2. Of those that a mesh axis runs over, the one named last changes fastest.
Arguments:
- activations: bfloat16 [6144, 49, 512], P(('row', 'col'))
- pre_activation: bfloat16 [6144, 49, 1024], P(('row', 'col')), may hold values from -6 to 6
- pooled_grad: float32 [6144, 1024], P(('row', 'col')), may hold values from -300 to 300
- weights: bfloat16 [512, 1024], replicated, as said below
- master: float32 [512, 1024], P('row', 'col')
- velocity: float32 [512, 1024], P('row', 'col'), may hold values from -0.6 to 0.6
- bn_params: float32 [2, 1024], replicated, may hold values from 0.5 to 1.5
- bn_velocity: float32 [2, 1024], replicated, may hold values from -0.6 to 0.6
Outputs:
- input_grad: bfloat16 [6144, 49, 512], P(('row', 'col'))
- new_master: float32 [512, 1024], P('row', 'col')
- new_velocity: float32 [512, 1024], P('row', 'col')
- new_weights: bfloat16 [512, 1024], replicated
- new_bn: float32 [2, 1024], replicated
- new_bn_velocity: float32 [2, 1024], replicated
The draws below stay inside these ranges and needn't reach their ends.
Inputs may be any that keep to these rules, and one draw needn't show every extreme that they name: weights lies within one bfloat16 rounding of master, entry by entry.
All inputs are finite; a program needn't handle non-finite values.
Results may differ from the reference program's by a relative error of at most 0.0045.
The reference program's roundings to bfloat16 on the way count: a program that leaves them out, or rounds other values in their place, can miss the bound.
Values may be sent and summed in bfloat16 or wider, within the bound.
No kernel may reach another device: no remote copies, remote signals or barrier semaphores. Data moves between devices by JAX's collectives and lax.ppermute only.
A program may use at most 64 MiB of HBM per device.

```python
import math
import jax
import jax.numpy as jnp
from jax import lax

CIN = 512
COUT = 1024
PIX = 49
IMG_DEV = 12
BATCH = 6144
N_ROW = 32
N_COL = 16


def weight_field(key, spread):
    base = jax.random.normal(key, (CIN, COUT), jnp.float32)
    row_frac = jnp.arange(CIN, dtype=jnp.float32) / max(CIN - 1, 1)
    col_frac = jnp.arange(COUT, dtype=jnp.float32) / max(COUT - 1, 1)
    ramp = jnp.exp(math.log(10.0) * spread * (row_frac[:, None] + col_frac[None, :] - 1.0))
    return 2.0 * base * ramp


def draw_master(key, part):
    spread = 0.5
    field = weight_field(key, spread)
    key = jax.random.fold_in(key, 3)
    jitter = jax.random.uniform(key, (CIN, COUT), jnp.float32, -1.0, 1.0)
    return field * (1.0 + 0.000244140625 * jitter)


def draw_weights(key, part):
    spread = 0.5
    field = weight_field(key, spread)
    key = jax.random.fold_in(key, 5)
    jitter = jax.random.uniform(key, (CIN, COUT), jnp.float32, -1.0, 1.0)
    return (field * (1.0 + 0.000244140625 * jitter)).astype(jnp.bfloat16)


def draw_activations(key, part):
    key = jax.random.fold_in(key, 7)
    noise_key, pair_key = jax.random.split(key)
    base = jax.random.normal(noise_key, (BATCH, PIX, CIN), jnp.float32)
    image = jnp.arange(BATCH) // IMG_DEV
    column = image % N_COL
    image_ramp = jnp.exp(math.log(3.0) * column.astype(jnp.float32) / max(N_COL - 1, 1))
    offset = jax.random.randint(pair_key, (), 0, N_ROW)
    block = (image + offset) % N_ROW
    chan_block = jnp.arange(CIN) // (CIN // N_ROW)
    boost = jnp.where(block[:, None] == chan_block[None, :], 3.0, 1.0)
    chan_ramp = jnp.exp(math.log(10.0) * jnp.arange(CIN, dtype=jnp.float32) / max(CIN - 1, 1))
    values = jnp.maximum(base, 0.0) * image_ramp[:, None, None] * (boost * chan_ramp[None, :])[:, None, :]
    return values.astype(jnp.bfloat16)


def steps_of(own_key, shape, cuts, least, largest):
    loudness = 1.0
    for position, blocks in cuts:
        heights = jax.random.uniform(jax.random.fold_in(jax.random.fold_in(own_key, 6), position), (blocks,), jnp.float32, least / len(cuts), largest / len(cuts))
        loudness = loudness * jnp.repeat(jnp.exp(heights), shape[position] // blocks).reshape((-1,) + (1,) * (len(shape) - 1 - position))
    return loudness


def bell_draw(own_key, shape, deviation, most, shards=(), kind=jnp.bfloat16):
    array = jax.random.normal(own_key, shape, jnp.float32) * deviation
    if len(shards) > 0:
        array = steps_of(own_key, shape, shards, -0.22, 0.18) * array
    return jnp.clip(array, min=-most, max=most).astype(kind)


def setup_inputs(seed: int = 0) -> dict:
    seeds = jax.random.split(jax.random.key(seed), 9)
    activations = draw_activations(jax.random.fold_in(seeds[8], 71), 0)
    pre_activation = bell_draw(seeds[1], (BATCH, PIX, COUT), 1.0, 6.0, ((0, 512),))
    pooled_grad = bell_draw(seeds[2], (BATCH, COUT), 50.0, 300.0, ((0, 512),), jnp.float32)
    weights = draw_weights(jax.random.fold_in(seeds[8], 71), 0)
    master = draw_master(jax.random.fold_in(seeds[8], 71), 0)
    velocity = bell_draw(seeds[5], (CIN, COUT), 0.1, 0.6, ((0, 32), (1, 16)), jnp.float32)
    bn_params = jnp.clip(1.0 + 0.1 * jax.random.normal(seeds[6], (2, COUT), jnp.float32), 0.5, 1.5)
    bn_velocity = bell_draw(seeds[7], (2, COUT), 0.1, 0.6, (), jnp.float32)
    return {"activations": activations, "pre_activation": pre_activation, "pooled_grad": pooled_grad, "weights": weights, "master": master, "velocity": velocity, "bn_params": bn_params, "bn_velocity": bn_velocity}


epsilon = 1e-05
trust_coef = 0.001
weight_decay = 0.0001
momentum = 0.9
learn_rate = 12.0

def reference(activations, pre_activation, pooled_grad, weights, master, velocity, bn_params, bn_velocity):
    group_images = N_COL * IMG_DEV
    element_count = group_images * PIX
    norm_scale_weight = bn_params[0]
    acts_grouped = activations.reshape(N_ROW, group_images, PIX, CIN)
    pre_grouped = pre_activation.reshape(N_ROW, group_images, PIX, COUT)
    pooled_grouped = pooled_grad.reshape(N_ROW, group_images, COUT)

    def group_step(carry, pieces):
        acts, preact, pooled = pieces
        flat_in = acts.reshape(element_count, CIN)
        conv_low = jnp.dot(flat_in, weights, preferred_element_type=jnp.float32).astype(jnp.bfloat16)
        expand_conv_output = lax.optimization_barrier(conv_low).astype(jnp.float32)
        group_mean_value = lax.optimization_barrier(jnp.sum(expand_conv_output, axis=0)) / element_count
        variance = lax.optimization_barrier(jnp.sum(expand_conv_output * expand_conv_output, axis=0)) / element_count - group_mean_value * group_mean_value
        inverse_deviation = lax.rsqrt(variance + epsilon)
        upstream_all = jnp.broadcast_to((pooled / PIX)[:, None, :], preact.shape).reshape(element_count, COUT)
        incoming_gradient = jnp.where(preact.reshape(element_count, COUT) > 0, upstream_all, jnp.zeros_like(upstream_all))
        normalized_input = (expand_conv_output - group_mean_value) * inverse_deviation
        upstream_sum_local = lax.optimization_barrier(jnp.sum(incoming_gradient, axis=0))
        upstream_normalized_sum = lax.optimization_barrier(jnp.sum(incoming_gradient * normalized_input, axis=0))
        expand_conv_gradient = (norm_scale_weight * inverse_deviation * (incoming_gradient - upstream_sum_local / element_count - normalized_input * upstream_normalized_sum / element_count)).astype(jnp.bfloat16)
        back = lax.dot_general(expand_conv_gradient, weights, (((1,), (1,)), ((), ())), preferred_element_type=jnp.float32).astype(jnp.bfloat16)
        wgrad = lax.dot_general(flat_in, expand_conv_gradient, (((0,), (0,)), ((), ())), preferred_element_type=jnp.float32)
        return ((carry[0] + wgrad, carry[1] + upstream_normalized_sum, carry[2] + upstream_sum_local), back)
    start = (jnp.zeros((CIN, COUT), jnp.float32), jnp.zeros((COUT,), jnp.float32), jnp.zeros((COUT,), jnp.float32))
    totals, backs = lax.scan(group_step, start, (acts_grouped, pre_grouped, pooled_grouped))
    input_grad = backs.reshape(BATCH, PIX, CIN)
    inv_batch = 1.0 / BATCH
    weight_grad = totals[0] * inv_batch
    bn_grad = jnp.stack([totals[1], totals[2]]) * inv_batch
    wnorm = jnp.sqrt(jnp.sum(master * master))
    gnorm = jnp.sqrt(jnp.sum(weight_grad * weight_grad))
    trust = trust_coef * wnorm / (gnorm + weight_decay * wnorm)
    new_velocity = momentum * velocity + learn_rate * trust * (weight_grad + weight_decay * master)
    new_master = master - new_velocity
    new_weights = new_master.astype(jnp.bfloat16)
    new_bn_velocity = momentum * bn_velocity + learn_rate * bn_grad
    new_bn = bn_params - new_bn_velocity
    return (input_grad, new_master, new_velocity, new_weights, new_bn, new_bn_velocity)
```

```python
import functools

import jax
import jax.numpy as jnp
import numpy as np
from jax import lax
from jax.experimental import pallas as pl
from jax.experimental.pallas import tpu as pltpu
from jax.sharding import Mesh, PartitionSpec as P

epsilon = 1e-05
trust_coef = 0.001
weight_decay = 0.0001
momentum = 0.9
learn_rate = 12.0

IMG, PIX, STRIDE = 12, 49, 64
CIN, COUT = 512, 1024
ROWS = IMG * STRIDE
HALF = CIN // 2
N_ROW, N_COL = 32, 16
M = PIX * IMG * N_COL
BATCH = IMG * N_ROW * N_COL
CHUNKS = COUT // 128
GROUP, PEERS, ALL = ("z", "core"), ("x", "y", "z"), ("x", "y", "z", "core")
STAT_ROWS = 48
SIDE_ROWS = 24
bf16, f32 = jnp.bfloat16, jnp.float32


def params(megabytes=48):
    return pltpu.CompilerParams(vmem_limit_bytes=megabytes << 20)


def fold(line):
    return jnp.concatenate([line[:, 128 * k : 128 * k + 128] for k in range(line.shape[1] // 128)], axis=0)


def unfold(block):
    return jnp.concatenate([block[k : k + 1] for k in range(block.shape[0])], axis=1)


def stats_kernel(act_ref, pre_ref, pool_ref, w_ref, master_ref, vel_ref, conv_ref, actp_ref, msg_ref):
    actp_ref[...] = jnp.zeros_like(actp_ref)
    for i in range(IMG):
        actp_ref[STRIDE * i : STRIDE * i + PIX, :] = act_ref[i]
    conv_ref[...] = jnp.dot(actp_ref[...], w_ref[...], preferred_element_type=f32).astype(bf16)
    total = jnp.zeros((1, COUT), f32)
    square = jnp.zeros((1, COUT), f32)
    up = jnp.zeros((1, COUT), f32)
    up_conv = jnp.zeros((1, COUT), f32)
    for i in range(IMG):
        conv = conv_ref[STRIDE * i : STRIDE * i + STRIDE, :].astype(f32)
        total += jnp.sum(conv, axis=0, keepdims=True)
        square += jnp.sum(conv * conv, axis=0, keepdims=True)
        passed = pre_ref[i].astype(f32) > 0
        share = pool_ref[i : i + 1, :] / PIX
        up += share * jnp.sum(jnp.where(passed, 1.0, 0.0), axis=0, keepdims=True)
        up_conv += share * jnp.sum(jnp.where(passed, conv[:PIX], 0.0), axis=0, keepdims=True)
    act_total = jnp.sum(actp_ref[...].astype(f32), axis=0, keepdims=True)
    master = master_ref[...]
    norm = jnp.sum(jnp.sum(master * master, axis=1, keepdims=True), axis=0, keepdims=True)
    decayed = master - momentum * vel_ref[...]
    msg = jnp.concatenate(
        [
            fold(total),
            fold(square),
            fold(up),
            fold(up_conv),
            fold(act_total),
            jnp.broadcast_to(norm, (4, 128)),
            jnp.concatenate([decayed[:8], decayed[8:]], axis=1),
        ],
        axis=0,
    )
    for p in range(N_COL):
        msg_ref[p] = msg


def split(line):
    high = line.astype(bf16)
    return [high, (line - high.astype(f32)).astype(bf16)]


def grad_kernel(core_ref, stat_ref, conv_ref, actp_ref, pre_ref, pool_ref, bn_ref, cg_ref, keep_ref, send_ref, side_ref, grad):
    core = core_ref[0]
    sums = jnp.sum(stat_ref[:, :40, :], axis=0)
    total = unfold(sums[0:8])
    square = unfold(sums[8:16])
    sum_up = unfold(sums[16:24])
    up_conv = unfold(sums[24:32])
    act_mean = sums[32:36] / M
    norm = jnp.concatenate([sums[36:37]] * CHUNKS, axis=1)
    mean = total / M
    variance = square / M - mean * mean
    rstd = lax.rsqrt(variance + epsilon)
    sum_upx = rstd * (up_conv - mean * sum_up)
    scale = bn_ref[0:1, :] * rstd
    shift = scale * (sum_up / M)
    slope = scale * (sum_upx / M) * rstd
    cg_ref[...] = jnp.zeros_like(cg_ref)
    cg_total = jnp.zeros((1, COUT), f32)
    for i in range(IMG):
        conv = conv_ref[STRIDE * i : STRIDE * i + STRIDE, :].astype(f32)[:PIX]
        on = scale * (pool_ref[i : i + 1, :] / PIX) - shift
        cg = jnp.where(pre_ref[i].astype(f32) > 0, on, -shift) - slope * (conv - mean)
        low = cg.astype(bf16)
        cg_ref[STRIDE * i : STRIDE * i + PIX, :] = low
        cg_total += jnp.sum(low.astype(f32), axis=0, keepdims=True)
    grad[...] = lax.dot_general(
        actp_ref[...], cg_ref[...], (((0,), (0,)), ((), ())), preferred_element_type=f32
    )
    column = jnp.transpose(jnp.concatenate([unfold(act_mean)] * 8, axis=0))[:, 0:1]
    grad[...] = grad[...] - column * cg_total
    keep_ref[...] = grad[pl.ds(pl.multiple_of(core * HALF, HALF), HALF), :]
    send_ref[...] = grad[pl.ds(pl.multiple_of((1 - core) * HALF, HALF), HALF), :].astype(bf16)
    tops, bottoms = [], []
    for k in range(N_COL):
        block = stat_ref[k, 40:48, :]
        tops.append(block[:, :64])
        bottoms.append(block[:, 64:])
    decayed = jnp.concatenate([jnp.concatenate(tops, axis=1), jnp.concatenate(bottoms, axis=1)], axis=0)
    norm_high = norm.astype(bf16)
    norm_rest = norm - norm_high.astype(f32)
    extra = [h.astype(f32) for h in split(sum_up) + split(sum_upx) + [norm_high] + split(norm_rest)]
    extra.append(jnp.zeros((1, COUT), f32))
    side_ref[...] = jnp.concatenate([decayed, jnp.concatenate(extra, axis=0)], axis=0).astype(bf16)


def back_kernel(cg_ref, w_ref, out_ref):
    back = lax.dot_general(cg_ref[...], w_ref[...], (((1,), (1,)), ((), ())), preferred_element_type=f32)
    for i in range(IMG):
        out_ref[i] = back[STRIDE * i : STRIDE * i + PIX].astype(bf16)


def pair_kernel(keep_ref, got_ref, out_ref):
    both = (keep_ref[...] + got_ref[...].astype(f32)).reshape(HALF // 8, 8, COUT)
    for j in range(CHUNKS):
        out_ref[:, j] = both[:, :, 128 * j : 128 * j + 128].astype(bf16)


def sum_kernel(got_ref, out_ref):
    total = jnp.sum(got_ref[...].astype(f32), axis=0) * (1.0 / BATCH)
    out_ref[...] = jnp.broadcast_to(total.astype(bf16)[None], out_ref.shape)


def update_kernel(
    place_ref, mine_ref, other_ref, side_ref, w_ref, master_ref, vel_ref, bn_ref, bnv_ref,
    new_master_ref, new_vel_ref, new_w_ref, new_bn_ref, new_bnv_ref, grad,
):
    core, row, col = place_ref[0], place_ref[1], place_ref[2]
    square = jnp.zeros((8, 128), f32)
    for part, start in ((mine_ref, core * HALF), (other_ref, (1 - core) * HALF)):
        for j in range(CHUNKS):
            block = part[:, j].astype(f32)
            square += jnp.sum(block * block, axis=0)
            grad[pl.ds(pl.multiple_of(start, HALF), HALF), 128 * j : 128 * j + 128] = block.reshape(HALF, 128)
    grad_total = jnp.sum(jnp.sum(square, axis=1, keepdims=True), axis=0, keepdims=True)
    side = side_ref[...].astype(f32).reshape(N_ROW, SIDE_ROWS, COUT)
    extra = jnp.sum(side[:, 16:24, :], axis=0)
    up_total = extra[0:1] + extra[1:2]
    upx_total = extra[2:3] + extra[3:4]
    master_total = (extra[4:5] + extra[5:6] + extra[6:7])[:, 0:1]
    wnorm = jnp.sqrt(master_total)
    gnorm = jnp.sqrt(grad_total)
    rate = learn_rate * (trust_coef * wnorm / (gnorm + weight_decay * wnorm))
    decayed = side[:, :16, :].reshape(CIN, COUT)
    new_w_ref[...] = (decayed - rate * (grad[...] + weight_decay * w_ref[...].astype(f32))).astype(bf16)
    pair = grad[pl.ds(pl.multiple_of(row * 16, 16), 16), pl.ds(pl.multiple_of((col // 2) * 128, 128), 128)]
    own = jnp.where(col % 2 == 0, pair[:, :64], pair[:, 64:])
    new_vel = momentum * vel_ref[...] + rate * (own + weight_decay * master_ref[...])
    new_vel_ref[...] = new_vel
    new_master_ref[...] = master_ref[...] - new_vel
    bn_grad = jnp.concatenate([upx_total, up_total], axis=0) * (1.0 / BATCH)
    new_bnv = momentum * bnv_ref[...] + learn_rate * bn_grad
    new_bnv_ref[...] = new_bnv
    new_bn_ref[...] = bn_ref[...] - new_bnv


def shape(dims, kind):
    return jax.ShapeDtypeStruct(dims, kind)


SMEM = pl.BlockSpec(memory_space=pltpu.SMEM)
VMEM = pl.BlockSpec(memory_space=pltpu.VMEM)


def body(activations, pre_activation, pooled_grad, weights, master, velocity, bn_params, bn_velocity):
    core = lax.axis_index("core").astype(jnp.int32)
    row = (lax.axis_index("x") * 8 + lax.axis_index("y")).astype(jnp.int32)
    col = (lax.axis_index("z") * 2 + lax.axis_index("core")).astype(jnp.int32)
    place = jnp.stack([core, row, col])
    conv, act, msg = pl.pallas_call(
        stats_kernel,
        out_shape=(shape((ROWS, COUT), bf16), shape((ROWS, CIN), bf16), shape((N_COL, STAT_ROWS, 128), f32)),
        in_specs=[VMEM] * 6,
        out_specs=(VMEM,) * 3,
        compiler_params=params(),
        name="conv_stats",
    )(activations, pre_activation, pooled_grad, weights, master, velocity)
    stats = lax.all_to_all(msg, GROUP, 0, 0)
    conv_grad, keep, send, side = pl.pallas_call(
        grad_kernel,
        out_shape=(
            shape((ROWS, COUT), bf16),
            shape((HALF, COUT), f32),
            shape((HALF, COUT), bf16),
            shape((SIDE_ROWS, COUT), bf16),
        ),
        in_specs=[SMEM] + [VMEM] * 6,
        out_specs=(VMEM,) * 4,
        scratch_shapes=[pltpu.VMEM((CIN, COUT), f32)],
        compiler_params=params(),
        name="conv_grad",
    )(place, stats, conv, act, pre_activation, pooled_grad, bn_params)
    side_all = lax.all_gather(side, ("x", "y"), axis=0, tiled=True)
    swap = [(0, 1), (1, 0)]
    got = lax.ppermute(send, "core", swap)
    input_grad = pl.pallas_call(
        back_kernel,
        out_shape=shape((IMG, PIX, CIN), bf16),
        in_specs=[VMEM] * 2,
        out_specs=VMEM,
        compiler_params=params(),
        cost_estimate=pl.CostEstimate(flops=2 * ROWS * CIN * COUT, bytes_accessed=4 << 20, transcendentals=0),
        name="input_grad",
    )(conv_grad, weights)
    blocks = pl.pallas_call(
        pair_kernel,
        out_shape=shape((HALF // 8, CHUNKS, 8, 128), bf16),
        in_specs=[VMEM] * 2,
        out_specs=VMEM,
        compiler_params=params(),
        name="pair_sum",
    )(keep, got)
    arrived = lax.all_to_all(blocks.reshape(256, 8, 128), PEERS, 0, 0)
    block = pl.pallas_call(
        sum_kernel,
        out_shape=shape((256, 8, 128), bf16),
        in_specs=[VMEM],
        out_specs=VMEM,
        compiler_params=params(),
        name="block_sum",
    )(arrived)
    mine = lax.all_to_all(block, PEERS, 0, 0)
    other = lax.ppermute(mine, "core", swap)
    tiles = (HALF // 8, CHUNKS, 8, 128)
    new_master, new_velocity, new_weights, new_bn, new_bn_velocity = pl.pallas_call(
        update_kernel,
        out_shape=(
            shape((16, 64), f32),
            shape((16, 64), f32),
            shape((CIN, COUT), bf16),
            shape((2, COUT), f32),
            shape((2, COUT), f32),
        ),
        in_specs=[SMEM] + [VMEM] * 8,
        out_specs=(VMEM,) * 5,
        scratch_shapes=[pltpu.VMEM((CIN, COUT), f32)],
        compiler_params=params(),
        name="update",
    )(place, mine.reshape(tiles), other.reshape(tiles), side_all, weights, master, velocity, bn_params, bn_velocity)
    return input_grad, new_master, new_velocity, new_weights, new_bn, new_bn_velocity


def solution(mesh):
    fine = Mesh(mesh.devices.reshape(4, 8, 8, 2), ALL)
    block = P(("x", "y"), ("z", "core"))
    return jax.shard_map(
        body,
        mesh=fine,
        in_specs=(P(ALL, None, None), P(ALL, None, None), P(ALL, None), P(), block, block, P(), P()),
        out_specs=(P(ALL, None, None), block, block, P(), P(), P()),
        check_vma=False,
    )
```

```python
import jax
import jax.numpy as jnp
from jax import lax
from jax.experimental import pallas as pl
from jax.experimental.pallas import tpu as pltpu
from jax.sharding import Mesh, PartitionSpec as P

epsilon = 1e-05
trust_coef = 0.001
weight_decay = 0.0001
momentum = 0.9
learn_rate = 12.0

IMG, PIX, STRIDE = 12, 49, 64
CIN, COUT = 512, 1024
ROWS = IMG * STRIDE
HALF = CIN // 2
N_ROW, N_COL, N_Z = 32, 16, 8
M = PIX * IMG * N_COL
BATCH = IMG * N_ROW * N_COL
CHUNKS = COUT // 128
GROUP, LAYER, PEERS, ALL = ("z", "core"), ("x", "y"), ("x", "y", "z"), ("x", "y", "z", "core")
STAT_ROWS = 40
SIDE_ROWS = 24
WIDE_ROWS = 528
PARTS = 4
bf16, f32 = jnp.bfloat16, jnp.float32


def params(megabytes=20):
    return pltpu.CompilerParams(vmem_limit_bytes=megabytes << 20)


def fold(line):
    return jnp.concatenate([line[:, 128 * k : 128 * k + 128] for k in range(line.shape[1] // 128)], axis=0)


def unfold(block):
    return jnp.concatenate([block[k : k + 1] for k in range(block.shape[0])], axis=1)


def split(line):
    high = line.astype(bf16).astype(f32)
    middle = (line - high).astype(bf16).astype(f32)
    return high, middle, line - high - middle


def rows_of(count, lines, dims):
    row = lax.broadcasted_iota(jnp.int32, dims, 0)
    block = jnp.zeros(dims, f32)
    for k in range(count):
        block = jnp.where(row == k, jnp.broadcast_to(lines[k], dims), block)
    return block


def stats_kernel(act_hbm, pre_hbm, pool_hbm, w_hbm, conv_hbm, msg_ref, act, pre, pool, w, actp, conv, sem_in, sem_out):
    step = IMG // PARTS
    loads = []
    for k in range(PARTS):
        part = pl.ds(step * k, step)
        strip = pl.ds(CIN // PARTS * k, CIN // PARTS)
        loads.append(pltpu.make_async_copy(w_hbm.at[strip], w.at[strip], sem_in.at[0, k]))
        loads.append(pltpu.make_async_copy(act_hbm.at[part], act.at[part], sem_in.at[1, k]))
    for copy in loads:
        copy.start()
    later = [pltpu.make_async_copy(pool_hbm, pool, sem_in.at[3, 0])]
    for k in range(PARTS):
        part = pl.ds(step * k, step)
        later.append(pltpu.make_async_copy(pre_hbm.at[part], pre.at[part], sem_in.at[2, k]))
    for copy in later:
        copy.start()
    actp[...] = jnp.zeros_like(actp)
    for copy in loads:
        copy.wait()
    for i in range(IMG):
        actp[STRIDE * i : STRIDE * i + PIX, :] = act[i]
    stores = []
    for k in range(2):
        strip = pl.ds(ROWS // 2 * k, ROWS // 2)
        conv[strip, :] = jnp.dot(actp[strip, :], w[...], preferred_element_type=f32).astype(bf16)
        stores.append(pltpu.make_async_copy(conv.at[strip], conv_hbm.at[strip], sem_out.at[k]))
        stores[-1].start()
    for copy in later:
        copy.wait()
    total = jnp.zeros((1, COUT), f32)
    square = jnp.zeros((1, COUT), f32)
    up = jnp.zeros((1, COUT), f32)
    up_conv = jnp.zeros((1, COUT), f32)
    for i in range(IMG):
        value = conv[STRIDE * i : STRIDE * i + STRIDE, :].astype(f32)
        total += jnp.sum(value, axis=0, keepdims=True)
        square += jnp.sum(value * value, axis=0, keepdims=True)
        passed = pre[i].astype(f32) > 0
        share = pool[i : i + 1, :] / PIX
        up += share * jnp.sum(jnp.where(passed, 1.0, 0.0), axis=0, keepdims=True)
        up_conv += share * jnp.sum(jnp.where(passed, value[:PIX], 0.0), axis=0, keepdims=True)
    act_total = jnp.sum(actp[...].astype(f32), axis=0, keepdims=True)
    msg = jnp.concatenate(
        [fold(total), fold(square), fold(up), fold(up_conv), fold(act_total), jnp.zeros((4, 128), f32)], axis=0
    )
    for p in range(N_COL):
        msg_ref[p] = msg
    for copy in stores:
        copy.wait()


def grad_kernel(
    place_ref, stat_ref, conv_ref, act_ref, pre_ref, pool_ref, bn_ref, cg_ref, keep_ref, send_ref, line_ref, actp, lines
):
    core, layer = place_ref[0], place_ref[3]
    sums = jnp.sum(stat_ref[...], axis=0)
    sum_up = sums[16:24]
    act_mean = (unfold(sums[32:36]) / M).astype(bf16).astype(f32)
    mean = sums[0:8] / M
    variance = sums[8:16] / M - mean * mean
    rstd = lax.rsqrt(variance + epsilon)
    sum_upx = rstd * (sums[24:32] - mean * sum_up)
    lines[0:8, :] = sum_up
    lines[8:16, :] = sum_upx
    line_ref[...] = jnp.broadcast_to(lines[pl.ds(core * 8 + layer, 1), :], (8, 128))
    scale = fold(bn_ref[0:1, :]) * rstd
    shift = unfold(scale * (sum_up / M))
    slope = unfold(scale * (sum_upx / M) * rstd)
    mean = unfold(mean)
    scale = unfold(scale)
    actp[...] = jnp.zeros_like(actp)
    for i in range(IMG):
        actp[STRIDE * i : STRIDE * i + PIX, :] = act_ref[i]
    cg_ref[...] = jnp.zeros_like(cg_ref)
    cg_total = jnp.zeros((1, COUT), f32)
    for i in range(IMG):
        conv = conv_ref[STRIDE * i : STRIDE * i + STRIDE, :].astype(f32)[:PIX]
        on = scale * (pool_ref[i : i + 1, :] / PIX) - shift
        low = (jnp.where(pre_ref[i].astype(f32) > 0, on, -shift) - slope * (conv - mean)).astype(bf16)
        cg_ref[STRIDE * i : STRIDE * i + PIX, :] = low
        cg_total += jnp.sum(low.astype(f32), axis=0, keepdims=True)
    edge = actp[48:64, :].astype(f32)
    row = lax.broadcasted_iota(jnp.int32, edge.shape, 0)
    actp[48:64, :] = jnp.where((row >= 1) & (row < 4), -act_mean, edge).astype(bf16)
    high, middle, rest = split(cg_total)
    edge = cg_ref[48:64, :].astype(f32)
    cg_ref[48:64, :] = (edge + rows_of(4, [jnp.zeros_like(high), high, middle, rest], edge.shape)).astype(bf16)
    for half, out_ref in ((1 - core, send_ref), (core, keep_ref)):
        columns = actp[:, pl.ds(pl.multiple_of(half * HALF, HALF), HALF)]
        part = lax.dot_general(columns, cg_ref[...], (((0,), (0,)), ((), ())), preferred_element_type=f32)
        out_ref[...] = part.astype(out_ref.dtype)


def back_kernel(cg_ref, w_ref, out_ref):
    back = lax.dot_general(cg_ref[...], w_ref[...], (((1,), (1,)), ((), ())), preferred_element_type=f32)
    for i in range(IMG):
        out_ref[i] = back[STRIDE * i : STRIDE * i + PIX].astype(bf16)


def pair_kernel(keep_ref, got_ref, out_ref):
    both = (keep_ref[...] + got_ref[...].astype(f32)).reshape(HALF // 8, 8, COUT)
    for j in range(CHUNKS):
        out_ref[:, j] = both[:, :, 128 * j : 128 * j + 128].astype(bf16)


def block_kernel(got_ref, line_ref, master_ref, vel_ref, out_ref):
    total = jnp.sum(got_ref[...].astype(f32), axis=0) * (1.0 / BATCH)
    master = master_ref[...]
    decayed = master - momentum * vel_ref[...]
    decayed = jnp.concatenate([decayed[:8], decayed[8:]], axis=1)
    norm = jnp.sum(jnp.sum(master * master, axis=1, keepdims=True), axis=0, keepdims=True)
    extra = rows_of(6, split(line_ref[...]) + split(jnp.broadcast_to(norm, (8, 128))), (8, 128))
    block = jnp.concatenate([total, decayed, extra], axis=0).astype(bf16)
    out_ref[...] = jnp.broadcast_to(block[None], out_ref.shape)


def layer_kernel(got_ref, out_ref):
    extra = jnp.sum(got_ref[:, 16:24, :].astype(f32), axis=0)
    line = extra[0:1] + extra[1:2] + extra[2:3]
    norm = extra[3:4] + extra[4:5] + extra[5:6]
    extra = rows_of(6, split(line) + split(norm), (16, 128)).astype(bf16)
    grad = got_ref[:, 0:8, :].astype(f32).reshape(HALF, 128).astype(bf16)
    decayed = got_ref[:, 8:16, :].astype(f32).reshape(HALF, 128).astype(bf16)
    for p in range(N_Z):
        out_ref[p, 0:256, :] = grad
        out_ref[p, 256:512, :] = decayed
        out_ref[p, 512:528, :] = extra


def update_kernel(
    place_ref, mine_ref, other_ref, w_ref, master_ref, vel_ref, bn_ref, bnv_ref,
    new_master_ref, new_vel_ref, new_w_hbm, new_bn_ref, new_bnv_ref, new_w, sems,
):
    core, row, col = place_ref[0], place_ref[1], place_ref[2]

    def run(parts):
        square = jnp.zeros((8, 128), f32)
        norm = jnp.zeros((1, 128), f32)
        totals = []
        for part in parts:
            line = []
            for z in range(N_Z):
                block = part[z, 0:256, :].astype(f32)
                square += jnp.sum((block * block).reshape(32, 8, 128), axis=0)
                extra = part[z, 512:528, :].astype(f32)
                line.append(extra[0:1] + extra[1:2] + extra[2:3])
                norm += extra[3:4] + extra[4:5] + extra[5:6]
            totals.append(jnp.concatenate(line, axis=1))
        grad_total = jnp.sum(jnp.sum(square, axis=1, keepdims=True), axis=0, keepdims=True)
        wnorm = jnp.sqrt(norm[:, 0:1])
        gnorm = jnp.sqrt(grad_total)
        rate = learn_rate * (trust_coef * wnorm / (gnorm + weight_decay * wnorm))
        stores = []
        for z in range(N_Z):
            even, odd = [part[z, 256:512, :].astype(f32).reshape(32, 8, 128) for part in parts]
            top = jnp.concatenate([even[:, :, :64], odd[:, :, :64]], axis=2)
            bottom = jnp.concatenate([even[:, :, 64:], odd[:, :, 64:]], axis=2)
            decayed = jnp.stack([top, bottom], axis=1).reshape(CIN, 128)
            columns = slice(128 * z, 128 * z + 128)
            for h in range(2):
                rows = slice(HALF * h, HALF * h + HALF)
                step = parts[h][z, 0:256, :].astype(f32) + weight_decay * w_ref[rows, columns].astype(f32)
                new_w[rows, columns] = (decayed[rows] - rate * step).astype(bf16)
            stores.append(pltpu.make_async_copy(new_w.at[:, columns], new_w_hbm.at[:, columns], sems.at[z]))
            stores[-1].start()
        bn_grad = jnp.concatenate([totals[1], totals[0]], axis=0) * (1.0 / BATCH)
        new_bnv = momentum * bnv_ref[...] + learn_rate * bn_grad
        new_bnv_ref[...] = new_bnv
        new_bn_ref[...] = bn_ref[...] - new_bnv
        for h in range(2):

            @pl.when(row // 16 == h)
            def _():
                pair = parts[h][col // 2, pl.ds(pl.multiple_of(row % 16 * 16, 16), 16), :].astype(f32)
                own = jnp.where(core == 0, pair[:, :64], pair[:, 64:])
                new_vel = momentum * vel_ref[...] + rate * (own + weight_decay * master_ref[...])
                new_vel_ref[...] = new_vel
                new_master_ref[...] = master_ref[...] - new_vel

        for copy in stores:
            copy.wait()

    @pl.when(core == 0)
    def _():
        run((mine_ref, other_ref))

    @pl.when(core == 1)
    def _():
        run((other_ref, mine_ref))


def shape(dims, kind):
    return jax.ShapeDtypeStruct(dims, kind)


SMEM = pl.BlockSpec(memory_space=pltpu.SMEM)
VMEM = pl.BlockSpec(memory_space=pltpu.VMEM)
HBM = pl.BlockSpec(memory_space=pltpu.HBM)


def body(activations, pre_activation, pooled_grad, weights, master, velocity, bn_params, bn_velocity):
    core = lax.axis_index("core").astype(jnp.int32)
    layer = lax.axis_index("z").astype(jnp.int32)
    row = (lax.axis_index("x") * 8 + lax.axis_index("y")).astype(jnp.int32)
    place = jnp.stack([core, row, layer * 2 + core, layer])
    conv, msg = pl.pallas_call(
        stats_kernel,
        out_shape=(shape((ROWS, COUT), bf16), shape((N_COL, STAT_ROWS, 128), f32)),
        in_specs=[HBM] * 4,
        out_specs=(HBM, VMEM),
        scratch_shapes=[
            pltpu.VMEM((IMG, PIX, CIN), bf16),
            pltpu.VMEM((IMG, PIX, COUT), bf16),
            pltpu.VMEM((IMG, COUT), f32),
            pltpu.VMEM((CIN, COUT), bf16),
            pltpu.VMEM((ROWS, CIN), bf16),
            pltpu.VMEM((ROWS, COUT), bf16),
            pltpu.SemaphoreType.DMA((4, PARTS)),
            pltpu.SemaphoreType.DMA((2,)),
        ],
        compiler_params=params(),
        name="conv_stats",
    )(activations, pre_activation, pooled_grad, weights)
    stats = lax.all_to_all(msg, GROUP, 0, 0)
    conv_grad, keep, send, line = pl.pallas_call(
        grad_kernel,
        out_shape=(
            shape((ROWS, COUT), bf16),
            shape((HALF, COUT), f32),
            shape((HALF, COUT), bf16),
            shape((8, 128), f32),
        ),
        in_specs=[SMEM] + [VMEM] * 6,
        out_specs=(VMEM,) * 4,
        scratch_shapes=[pltpu.VMEM((ROWS, CIN), bf16), pltpu.VMEM((16, 128), f32)],
        compiler_params=params(),
        name="conv_grad",
    )(place, stats, conv, activations, pre_activation, pooled_grad, bn_params)
    swap = [(0, 1), (1, 0)]
    got = lax.ppermute(send, "core", swap)
    input_grad = pl.pallas_call(
        back_kernel,
        out_shape=shape((IMG, PIX, CIN), bf16),
        in_specs=[VMEM] * 2,
        out_specs=VMEM,
        compiler_params=params(),
        cost_estimate=pl.CostEstimate(flops=2 * ROWS * CIN * COUT, bytes_accessed=4 << 20, transcendentals=0),
        name="input_grad",
    )(conv_grad, weights)
    blocks = pl.pallas_call(
        pair_kernel,
        out_shape=shape((HALF // 8, CHUNKS, 8, 128), bf16),
        in_specs=[VMEM] * 2,
        out_specs=VMEM,
        compiler_params=params(),
        name="pair_sum",
    )(keep, got)
    arrived = lax.all_to_all(blocks.reshape(256, 8, 128), PEERS, 0, 0)
    block = pl.pallas_call(
        block_kernel,
        out_shape=shape((N_ROW, SIDE_ROWS, 128), bf16),
        in_specs=[VMEM] * 4,
        out_specs=VMEM,
        compiler_params=params(),
        name="block_sum",
    )(arrived, line, master, velocity)
    wide = pl.pallas_call(
        layer_kernel,
        out_shape=shape((N_Z, WIDE_ROWS, 128), bf16),
        in_specs=[VMEM],
        out_specs=VMEM,
        compiler_params=params(),
        name="layer_join",
    )(lax.all_to_all(block, LAYER, 0, 0))
    mine = lax.all_to_all(wide, "z", 0, 0)
    other = lax.ppermute(mine, "core", swap)
    new_master, new_velocity, new_weights, new_bn, new_bn_velocity = pl.pallas_call(
        update_kernel,
        out_shape=(
            shape((16, 64), f32),
            shape((16, 64), f32),
            shape((CIN, COUT), bf16),
            shape((2, COUT), f32),
            shape((2, COUT), f32),
        ),
        in_specs=[SMEM] + [VMEM] * 7,
        out_specs=(VMEM, VMEM, HBM, VMEM, VMEM),
        scratch_shapes=[pltpu.VMEM((CIN, COUT), bf16), pltpu.SemaphoreType.DMA((N_Z,))],
        compiler_params=params(),
        name="update",
    )(place, mine, other, weights, master, velocity, bn_params, bn_velocity)
    return input_grad, new_master, new_velocity, new_weights, new_bn, new_bn_velocity


def solution(mesh):
    fine = Mesh(mesh.devices.reshape(4, 8, 8, 2), ALL)
    block = P(("x", "y"), ("z", "core"))
    return jax.shard_map(
        body,
        mesh=fine,
        in_specs=(P(ALL, None, None), P(ALL, None, None), P(ALL, None), P(), block, block, P(), P()),
        out_specs=(P(ALL, None, None), block, block, P(), P(), P()),
        check_vma=False,
    )
```

```python
import jax
import jax.numpy as jnp
from jax import lax
from jax.experimental import pallas as pl
from jax.experimental.pallas import tpu as pltpu
from jax.sharding import Mesh, PartitionSpec as P

epsilon = 1e-05
trust_coef = 0.001
weight_decay = 0.0001
momentum = 0.9
learn_rate = 12.0

IMG, PIX, STRIDE = 12, 49, 64
CIN, COUT = 512, 1024
ROWS = IMG * STRIDE
HALF = CIN // 2
N_ROW, N_COL, N_Z = 32, 16, 8
M = PIX * IMG * N_COL
BATCH = IMG * N_ROW * N_COL
CHUNKS = COUT // 128
GROUP, LAYER, PEERS, ALL = ("z", "core"), ("x", "y"), ("x", "y", "z"), ("x", "y", "z", "core")
STAT_ROWS = 40
SIDE_ROWS = 24
WIDE_ROWS = 528
PARTS = 4
bf16, f32 = jnp.bfloat16, jnp.float32


def params(megabytes=20):
    return pltpu.CompilerParams(vmem_limit_bytes=megabytes << 20)


def fold(line):
    return jnp.concatenate([line[:, 128 * k : 128 * k + 128] for k in range(line.shape[1] // 128)], axis=0)


def unfold(block):
    return jnp.concatenate([block[k : k + 1] for k in range(block.shape[0])], axis=1)


def split(line):
    high = line.astype(bf16).astype(f32)
    middle = (line - high).astype(bf16).astype(f32)
    return high, middle, line - high - middle


def rows_of(count, lines, dims):
    row = lax.broadcasted_iota(jnp.int32, dims, 0)
    block = jnp.zeros(dims, f32)
    for k in range(count):
        block = jnp.where(row == k, jnp.broadcast_to(lines[k], dims), block)
    return block


def stats_kernel(act_hbm, pre_hbm, pool_hbm, w_hbm, msg_ref, act, pre, pool, w, actp, conv, sem_in):
    step = IMG // PARTS
    loads = []
    for k in range(PARTS):
        part = pl.ds(step * k, step)
        strip = pl.ds(CIN // PARTS * k, CIN // PARTS)
        loads.append(pltpu.make_async_copy(w_hbm.at[strip], w.at[strip], sem_in.at[0, k]))
        loads.append(pltpu.make_async_copy(act_hbm.at[part], act.at[part], sem_in.at[1, k]))
    for copy in loads:
        copy.start()
    later = [pltpu.make_async_copy(pool_hbm, pool, sem_in.at[3, 0])]
    for k in range(PARTS):
        part = pl.ds(step * k, step)
        later.append(pltpu.make_async_copy(pre_hbm.at[part], pre.at[part], sem_in.at[2, k]))
    for copy in later:
        copy.start()
    actp[...] = jnp.zeros_like(actp)
    for copy in loads:
        copy.wait()
    for i in range(IMG):
        actp[STRIDE * i : STRIDE * i + PIX, :] = act[i]
    conv[...] = jnp.dot(actp[...], w[...], preferred_element_type=f32).astype(bf16)
    for copy in later:
        copy.wait()
    total = jnp.zeros((1, COUT), f32)
    square = jnp.zeros((1, COUT), f32)
    up = jnp.zeros((1, COUT), f32)
    up_conv = jnp.zeros((1, COUT), f32)
    for i in range(IMG):
        value = conv[STRIDE * i : STRIDE * i + STRIDE, :].astype(f32)
        total += jnp.sum(value, axis=0, keepdims=True)
        square += jnp.sum(value * value, axis=0, keepdims=True)
        passed = pre[i].astype(f32) > 0
        share = pool[i : i + 1, :] / PIX
        up += share * jnp.sum(jnp.where(passed, 1.0, 0.0), axis=0, keepdims=True)
        up_conv += share * jnp.sum(jnp.where(passed, value[:PIX], 0.0), axis=0, keepdims=True)
    act_total = jnp.sum(actp[...].astype(f32), axis=0, keepdims=True)
    msg = jnp.concatenate(
        [fold(total), fold(square), fold(up), fold(up_conv), fold(act_total), jnp.zeros((4, 128), f32)], axis=0
    )
    for p in range(N_COL):
        msg_ref[p] = msg


def grad_kernel(
    place_ref, stat_ref, w_ref, act_ref, pre_ref, pool_ref, bn_ref, cg_ref, keep_ref, send_ref, line_ref, actp, conv_ref, lines
):
    core, layer = place_ref[0], place_ref[3]
    sums = jnp.sum(stat_ref[...], axis=0)
    sum_up = sums[16:24]
    act_mean = (unfold(sums[32:36]) / M).astype(bf16).astype(f32)
    mean = sums[0:8] / M
    variance = sums[8:16] / M - mean * mean
    rstd = lax.rsqrt(variance + epsilon)
    sum_upx = rstd * (sums[24:32] - mean * sum_up)
    lines[0:8, :] = sum_up
    lines[8:16, :] = sum_upx
    line_ref[...] = jnp.broadcast_to(lines[pl.ds(core * 8 + layer, 1), :], (8, 128))
    scale = fold(bn_ref[0:1, :]) * rstd
    shift = unfold(scale * (sum_up / M))
    slope = unfold(scale * (sum_upx / M) * rstd)
    mean = unfold(mean)
    scale = unfold(scale)
    actp[...] = jnp.zeros_like(actp)
    for i in range(IMG):
        actp[STRIDE * i : STRIDE * i + PIX, :] = act_ref[i]
    conv_ref[...] = jnp.dot(actp[...], w_ref[...], preferred_element_type=f32).astype(bf16)
    cg_ref[...] = jnp.zeros_like(cg_ref)
    cg_total = jnp.zeros((1, COUT), f32)
    for i in range(IMG):
        conv = conv_ref[STRIDE * i : STRIDE * i + STRIDE, :].astype(f32)[:PIX]
        on = scale * (pool_ref[i : i + 1, :] / PIX) - shift
        low = (jnp.where(pre_ref[i].astype(f32) > 0, on, -shift) - slope * (conv - mean)).astype(bf16)
        cg_ref[STRIDE * i : STRIDE * i + PIX, :] = low
        cg_total += jnp.sum(low.astype(f32), axis=0, keepdims=True)
    edge = actp[48:64, :].astype(f32)
    row = lax.broadcasted_iota(jnp.int32, edge.shape, 0)
    actp[48:64, :] = jnp.where((row >= 1) & (row < 4), -act_mean, edge).astype(bf16)
    high, middle, rest = split(cg_total)
    edge = cg_ref[48:64, :].astype(f32)
    cg_ref[48:64, :] = (edge + rows_of(4, [jnp.zeros_like(high), high, middle, rest], edge.shape)).astype(bf16)
    for half, out_ref in ((1 - core, send_ref), (core, keep_ref)):
        columns = actp[:, pl.ds(pl.multiple_of(half * HALF, HALF), HALF)]
        part = lax.dot_general(columns, cg_ref[...], (((0,), (0,)), ((), ())), preferred_element_type=f32)
        out_ref[...] = part.astype(out_ref.dtype)


def back_kernel(cg_ref, w_ref, out_ref):
    back = lax.dot_general(cg_ref[...], w_ref[...], (((1,), (1,)), ((), ())), preferred_element_type=f32)
    for i in range(IMG):
        out_ref[i] = back[STRIDE * i : STRIDE * i + PIX].astype(bf16)


def pair_kernel(keep_ref, got_ref, out_ref):
    both = (keep_ref[...] + got_ref[...].astype(f32)).reshape(HALF // 8, 8, COUT)
    for j in range(CHUNKS):
        out_ref[:, j] = both[:, :, 128 * j : 128 * j + 128].astype(bf16)


def block_kernel(got_ref, line_ref, master_ref, vel_ref, out_ref):
    total = jnp.sum(got_ref[...].astype(f32), axis=0) * (1.0 / BATCH)
    master = master_ref[...]
    decayed = master - momentum * vel_ref[...]
    decayed = jnp.concatenate([decayed[:8], decayed[8:]], axis=1)
    norm = jnp.sum(jnp.sum(master * master, axis=1, keepdims=True), axis=0, keepdims=True)
    extra = rows_of(6, split(line_ref[...]) + split(jnp.broadcast_to(norm, (8, 128))), (8, 128))
    block = jnp.concatenate([total, decayed, extra], axis=0).astype(bf16)
    out_ref[...] = jnp.broadcast_to(block[None], out_ref.shape)


def layer_kernel(got_ref, out_ref):
    extra = jnp.sum(got_ref[:, 16:24, :].astype(f32), axis=0)
    line = extra[0:1] + extra[1:2] + extra[2:3]
    norm = extra[3:4] + extra[4:5] + extra[5:6]
    extra = rows_of(6, split(line) + split(norm), (16, 128)).astype(bf16)
    grad = got_ref[:, 0:8, :].astype(f32).reshape(HALF, 128).astype(bf16)
    decayed = got_ref[:, 8:16, :].astype(f32).reshape(HALF, 128).astype(bf16)
    for p in range(N_Z):
        out_ref[p, 0:256, :] = grad
        out_ref[p, 256:512, :] = decayed
        out_ref[p, 512:528, :] = extra


def update_kernel(
    place_ref, mine_ref, other_ref, w_ref, master_ref, vel_ref, bn_ref, bnv_ref,
    new_master_ref, new_vel_ref, new_w_hbm, new_bn_ref, new_bnv_ref, new_w, sems,
):
    core, row, col = place_ref[0], place_ref[1], place_ref[2]

    def run(parts):
        square = jnp.zeros((8, 128), f32)
        norm = jnp.zeros((1, 128), f32)
        totals = []
        for part in parts:
            line = []
            for z in range(N_Z):
                block = part[z, 0:256, :].astype(f32)
                square += jnp.sum((block * block).reshape(32, 8, 128), axis=0)
                extra = part[z, 512:528, :].astype(f32)
                line.append(extra[0:1] + extra[1:2] + extra[2:3])
                norm += extra[3:4] + extra[4:5] + extra[5:6]
            totals.append(jnp.concatenate(line, axis=1))
        grad_total = jnp.sum(jnp.sum(square, axis=1, keepdims=True), axis=0, keepdims=True)
        wnorm = jnp.sqrt(norm[:, 0:1])
        gnorm = jnp.sqrt(grad_total)
        rate = learn_rate * (trust_coef * wnorm / (gnorm + weight_decay * wnorm))
        stores = []
        for z in range(N_Z):
            even, odd = [part[z, 256:512, :].astype(f32).reshape(32, 8, 128) for part in parts]
            top = jnp.concatenate([even[:, :, :64], odd[:, :, :64]], axis=2)
            bottom = jnp.concatenate([even[:, :, 64:], odd[:, :, 64:]], axis=2)
            decayed = jnp.stack([top, bottom], axis=1).reshape(CIN, 128)
            columns = slice(128 * z, 128 * z + 128)
            for h in range(2):
                rows = slice(HALF * h, HALF * h + HALF)
                step = parts[h][z, 0:256, :].astype(f32) + weight_decay * w_ref[rows, columns].astype(f32)
                new_w[rows, columns] = (decayed[rows] - rate * step).astype(bf16)
            stores.append(pltpu.make_async_copy(new_w.at[:, columns], new_w_hbm.at[:, columns], sems.at[z]))
            stores[-1].start()
        bn_grad = jnp.concatenate([totals[1], totals[0]], axis=0) * (1.0 / BATCH)
        new_bnv = momentum * bnv_ref[...] + learn_rate * bn_grad
        new_bnv_ref[...] = new_bnv
        new_bn_ref[...] = bn_ref[...] - new_bnv
        for h in range(2):

            @pl.when(row // 16 == h)
            def _():
                pair = parts[h][col // 2, pl.ds(pl.multiple_of(row % 16 * 16, 16), 16), :].astype(f32)
                own = jnp.where(core == 0, pair[:, :64], pair[:, 64:])
                new_vel = momentum * vel_ref[...] + rate * (own + weight_decay * master_ref[...])
                new_vel_ref[...] = new_vel
                new_master_ref[...] = master_ref[...] - new_vel

        for copy in stores:
            copy.wait()

    @pl.when(core == 0)
    def _():
        run((mine_ref, other_ref))

    @pl.when(core == 1)
    def _():
        run((other_ref, mine_ref))


def shape(dims, kind):
    return jax.ShapeDtypeStruct(dims, kind)


SMEM = pl.BlockSpec(memory_space=pltpu.SMEM)
VMEM = pl.BlockSpec(memory_space=pltpu.VMEM)
HBM = pl.BlockSpec(memory_space=pltpu.HBM)


def body(activations, pre_activation, pooled_grad, weights, master, velocity, bn_params, bn_velocity):
    core = lax.axis_index("core").astype(jnp.int32)
    layer = lax.axis_index("z").astype(jnp.int32)
    row = (lax.axis_index("x") * 8 + lax.axis_index("y")).astype(jnp.int32)
    place = jnp.stack([core, row, layer * 2 + core, layer])
    msg = pl.pallas_call(
        stats_kernel,
        out_shape=shape((N_COL, STAT_ROWS, 128), f32),
        in_specs=[HBM] * 4,
        out_specs=VMEM,
        scratch_shapes=[
            pltpu.VMEM((IMG, PIX, CIN), bf16),
            pltpu.VMEM((IMG, PIX, COUT), bf16),
            pltpu.VMEM((IMG, COUT), f32),
            pltpu.VMEM((CIN, COUT), bf16),
            pltpu.VMEM((ROWS, CIN), bf16),
            pltpu.VMEM((ROWS, COUT), bf16),
            pltpu.SemaphoreType.DMA((4, PARTS)),
        ],
        compiler_params=params(60),
        name="conv_stats",
    )(activations, pre_activation, pooled_grad, weights)
    stats = lax.all_to_all(msg, GROUP, 0, 0)
    conv_grad, keep, send, line = pl.pallas_call(
        grad_kernel,
        out_shape=(
            shape((ROWS, COUT), bf16),
            shape((HALF, COUT), f32),
            shape((HALF, COUT), bf16),
            shape((8, 128), f32),
        ),
        in_specs=[SMEM] + [VMEM] * 6,
        out_specs=(VMEM,) * 4,
        scratch_shapes=[pltpu.VMEM((ROWS, CIN), bf16), pltpu.VMEM((ROWS, COUT), bf16), pltpu.VMEM((16, 128), f32)],
        compiler_params=params(),
        name="conv_grad",
    )(place, stats, weights, activations, pre_activation, pooled_grad, bn_params)
    swap = [(0, 1), (1, 0)]
    got = lax.ppermute(send, "core", swap)
    input_grad = pl.pallas_call(
        back_kernel,
        out_shape=shape((IMG, PIX, CIN), bf16),
        in_specs=[VMEM] * 2,
        out_specs=VMEM,
        compiler_params=params(),
        cost_estimate=pl.CostEstimate(flops=2 * ROWS * CIN * COUT, bytes_accessed=4 << 20, transcendentals=0),
        name="input_grad",
    )(conv_grad, weights)
    blocks = pl.pallas_call(
        pair_kernel,
        out_shape=shape((HALF // 8, CHUNKS, 8, 128), bf16),
        in_specs=[VMEM] * 2,
        out_specs=VMEM,
        compiler_params=params(),
        name="pair_sum",
    )(keep, got)
    arrived = lax.all_to_all(blocks.reshape(256, 8, 128), PEERS, 0, 0)
    block = pl.pallas_call(
        block_kernel,
        out_shape=shape((N_ROW, SIDE_ROWS, 128), bf16),
        in_specs=[VMEM] * 4,
        out_specs=VMEM,
        compiler_params=params(),
        name="block_sum",
    )(arrived, line, master, velocity)
    wide = pl.pallas_call(
        layer_kernel,
        out_shape=shape((N_Z, WIDE_ROWS, 128), bf16),
        in_specs=[VMEM],
        out_specs=VMEM,
        compiler_params=params(),
        name="layer_join",
    )(lax.all_to_all(block, LAYER, 0, 0))
    mine = lax.all_to_all(wide, "z", 0, 0)
    other = lax.ppermute(mine, "core", swap)
    new_master, new_velocity, new_weights, new_bn, new_bn_velocity = pl.pallas_call(
        update_kernel,
        out_shape=(
            shape((16, 64), f32),
            shape((16, 64), f32),
            shape((CIN, COUT), bf16),
            shape((2, COUT), f32),
            shape((2, COUT), f32),
        ),
        in_specs=[SMEM] + [VMEM] * 7,
        out_specs=(VMEM, VMEM, HBM, VMEM, VMEM),
        scratch_shapes=[pltpu.VMEM((CIN, COUT), bf16), pltpu.SemaphoreType.DMA((N_Z,))],
        compiler_params=params(),
        name="update",
    )(place, mine, other, weights, master, velocity, bn_params, bn_velocity)
    return input_grad, new_master, new_velocity, new_weights, new_bn, new_bn_velocity


def solution(mesh):
    fine = Mesh(mesh.devices.reshape(4, 8, 8, 2), ALL)
    block = P(("x", "y"), ("z", "core"))
    return jax.shard_map(
        body,
        mesh=fine,
        in_specs=(P(ALL, None, None), P(ALL, None, None), P(ALL, None), P(), block, block, P(), P()),
        out_specs=(P(ALL, None, None), block, block, P(), P(), P()),
        check_vma=False,
    )
```

```python
import jax
import jax.numpy as jnp
from jax import lax
from jax.experimental import pallas as pl
from jax.experimental.pallas import tpu as pltpu
from jax.sharding import Mesh, PartitionSpec as P

epsilon = 1e-05
trust_coef = 0.001
weight_decay = 0.0001
momentum = 0.9
learn_rate = 12.0

IMG, PIX, STRIDE = 12, 49, 64
CIN, COUT = 512, 1024
ROWS = IMG * STRIDE
HALF = CIN // 2
N_ROW, N_COL = 32, 16
N_X, N_Y, N_Z = 4, 8, 8
M = PIX * IMG * N_COL
BATCH = IMG * N_ROW * N_COL
CHUNKS = COUT // 128
GROUP, PLANE, ALL = ("z", "core"), ("y", "z"), ("x", "y", "z", "core")
STAT_ROWS = 40
SIDE_ROWS = 24
WIDE_ROWS = 1056
PARTS = 2
STRIP = 512
bf16, f32 = jnp.bfloat16, jnp.float32


def params(megabytes=20):
    return pltpu.CompilerParams(vmem_limit_bytes=megabytes << 20)


def fold(line):
    return jnp.concatenate([line[:, 128 * k : 128 * k + 128] for k in range(line.shape[1] // 128)], axis=0)


def unfold(block):
    return jnp.concatenate([block[k : k + 1] for k in range(block.shape[0])], axis=1)


def split(line):
    high = line.astype(bf16).astype(f32)
    middle = (line - high).astype(bf16).astype(f32)
    return high, middle, line - high - middle


def rows_of(count, lines, dims):
    row = lax.broadcasted_iota(jnp.int32, dims, 0)
    block = jnp.zeros(dims, f32)
    for k in range(count):
        block = jnp.where(row == k, jnp.broadcast_to(lines[k], dims), block)
    return block


def stats_kernel(act_hbm, pre_hbm, pool_hbm, w_hbm, msg_ref, act, pre, pool, w, actp, conv, sem_in):
    step = IMG // PARTS
    loads = []
    for k in range(PARTS):
        part = pl.ds(step * k, step)
        strip = pl.ds(CIN // PARTS * k, CIN // PARTS)
        loads.append(pltpu.make_async_copy(w_hbm.at[strip], w.at[strip], sem_in.at[0, k]))
        loads.append(pltpu.make_async_copy(act_hbm.at[part], act.at[part], sem_in.at[1, k]))
    for copy in loads:
        copy.start()
    later = [pltpu.make_async_copy(pool_hbm, pool, sem_in.at[3, 0])]
    for k in range(PARTS):
        part = pl.ds(step * k, step)
        later.append(pltpu.make_async_copy(pre_hbm.at[part], pre.at[part], sem_in.at[2, k]))
    for copy in later:
        copy.start()
    actp[...] = jnp.zeros_like(actp)
    for copy in loads:
        copy.wait()
    for i in range(IMG):
        actp[STRIDE * i : STRIDE * i + PIX, :] = act[i]
    act_total = jnp.sum(actp[...].astype(f32), axis=0, keepdims=True)
    strips = [slice(STRIP * k, STRIP * k + STRIP) for k in range(COUT // STRIP)]
    lines = []
    for strip in strips:
        value = jnp.dot(actp[...], w[:, strip], preferred_element_type=f32).astype(bf16)
        conv[:, strip] = value
        value = value.astype(f32)
        total = jnp.sum(value, axis=0, keepdims=True)
        square = jnp.sum(value * value, axis=0, keepdims=True)
        lines.append([total, square])
    for copy in later:
        copy.wait()
    for k, strip in enumerate(strips):
        up = jnp.zeros((1, STRIP), f32)
        up_conv = jnp.zeros((1, STRIP), f32)
        for i in range(IMG):
            value = conv[STRIDE * i : STRIDE * i + STRIDE, strip].astype(f32)[:PIX]
            passed = pre[i, :, strip].astype(f32) > 0
            share = pool[i : i + 1, strip] / PIX
            up += share * jnp.sum(jnp.where(passed, 1.0, 0.0), axis=0, keepdims=True)
            up_conv += share * jnp.sum(jnp.where(passed, value, 0.0), axis=0, keepdims=True)
        lines[k] += [up, up_conv]
    sums = [fold(jnp.concatenate([line[q] for line in lines], axis=1)) for q in range(4)]
    msg = jnp.concatenate(sums + [fold(act_total), jnp.zeros((4, 128), f32)], axis=0)
    for p in range(N_COL):
        msg_ref[p] = msg


def grad_kernel(
    place_ref, stat_ref, w_ref, act_ref, pre_ref, pool_ref, bn_ref, cg_ref, keep_ref, send_ref, line_ref, actp, conv_ref, lines
):
    core, layer = place_ref[0], place_ref[3]
    sums = jnp.sum(stat_ref[...], axis=0)
    sum_up = sums[16:24]
    act_mean = (unfold(sums[32:36]) / M).astype(bf16).astype(f32)
    mean = sums[0:8] / M
    variance = sums[8:16] / M - mean * mean
    rstd = lax.rsqrt(variance + epsilon)
    sum_upx = rstd * (sums[24:32] - mean * sum_up)
    lines[0:8, :] = sum_up
    lines[8:16, :] = sum_upx
    line_ref[...] = jnp.broadcast_to(lines[pl.ds(core * 8 + layer, 1), :], (8, 128))
    scale = fold(bn_ref[0:1, :]) * rstd
    shift = unfold(scale * (sum_up / M))
    slope = unfold(scale * (sum_upx / M) * rstd)
    mean = unfold(mean)
    scale = unfold(scale)
    actp[...] = jnp.zeros_like(actp)
    for i in range(IMG):
        actp[STRIDE * i : STRIDE * i + PIX, :] = act_ref[i]
    conv_ref[...] = jnp.dot(actp[...], w_ref[...], preferred_element_type=f32).astype(bf16)
    cg_ref[...] = jnp.zeros_like(cg_ref)
    cg_total = jnp.zeros((1, COUT), f32)
    for i in range(IMG):
        conv = conv_ref[STRIDE * i : STRIDE * i + STRIDE, :].astype(f32)[:PIX]
        on = scale * (pool_ref[i : i + 1, :] / PIX) - shift
        low = (jnp.where(pre_ref[i].astype(f32) > 0, on, -shift) - slope * (conv - mean)).astype(bf16)
        cg_ref[STRIDE * i : STRIDE * i + PIX, :] = low
        cg_total += jnp.sum(low.astype(f32), axis=0, keepdims=True)
    edge = actp[48:64, :].astype(f32)
    row = lax.broadcasted_iota(jnp.int32, edge.shape, 0)
    actp[48:64, :] = jnp.where((row >= 1) & (row < 4), -act_mean, edge).astype(bf16)
    high, middle, rest = split(cg_total)
    edge = cg_ref[48:64, :].astype(f32)
    cg_ref[48:64, :] = (edge + rows_of(4, [jnp.zeros_like(high), high, middle, rest], edge.shape)).astype(bf16)
    for half, out_ref in ((1 - core, send_ref), (core, keep_ref)):
        columns = actp[:, pl.ds(pl.multiple_of(half * HALF, HALF), HALF)]
        part = lax.dot_general(columns, cg_ref[...], (((0,), (0,)), ((), ())), preferred_element_type=f32)
        out_ref[...] = part.astype(out_ref.dtype)


def back_kernel(cg_ref, w_ref, out_ref):
    back = lax.dot_general(cg_ref[...], w_ref[...], (((1,), (1,)), ((), ())), preferred_element_type=f32)
    for i in range(IMG):
        out_ref[i] = back[STRIDE * i : STRIDE * i + PIX].astype(bf16)


def pair_kernel(keep_ref, got_ref, out_ref):
    out_ref[...] = (keep_ref[...] + got_ref[...].astype(f32)).astype(bf16)


def line_kernel(got_ref, out_ref):
    total = jnp.sum(got_ref[...].astype(f32), axis=0).reshape(N_Z, 8, COUT)
    for y in range(N_Y):
        out_ref[y] = total[:, :, 128 * y : 128 * y + 128].astype(bf16)


def block_kernel(got_ref, line_ref, master_ref, vel_ref, out_ref):
    total = jnp.sum(got_ref[...].astype(f32), axis=0) * (1.0 / BATCH)
    master = master_ref[...]
    decayed = master - momentum * vel_ref[...]
    decayed = jnp.concatenate([decayed[:8], decayed[8:]], axis=1)
    norm = jnp.sum(jnp.sum(master * master, axis=1, keepdims=True), axis=0, keepdims=True)
    extra = rows_of(6, split(line_ref[...]) + split(jnp.broadcast_to(norm, (8, 128))), (8, 128))
    block = jnp.concatenate([total, decayed, extra], axis=0).astype(bf16)
    out_ref[...] = jnp.broadcast_to(block[None], out_ref.shape)


def plane_kernel(got_ref, out_ref):
    extra = jnp.sum(got_ref[:, 16:24, :].astype(f32).reshape(N_Y, N_Z, 8, 128), axis=0)
    lines = []
    norm = jnp.zeros((1, 128), f32)
    for z in range(N_Z):
        lines += split(extra[z, 0:1] + extra[z, 1:2] + extra[z, 2:3])
        norm += extra[z, 3:4] + extra[z, 4:5] + extra[z, 5:6]
    lines += split(norm)
    extra = jnp.concatenate(lines + [jnp.zeros((5, 128), f32)], axis=0).astype(bf16)
    grad = got_ref[:, 0:8, :].astype(f32).reshape(512, 128).astype(bf16)
    decayed = got_ref[:, 8:16, :].astype(f32).reshape(512, 128).astype(bf16)
    for p in range(N_X):
        out_ref[p, 0:512, :] = grad
        out_ref[p, 512:1024, :] = decayed
        out_ref[p, 1024:1056, :] = extra


def update_kernel(
    place_ref, mine_ref, other_ref, w_ref, master_ref, vel_ref, bn_ref, bnv_ref,
    new_master_ref, new_vel_ref, new_w_hbm, new_bn_ref, new_bnv_ref, new_w, sems,
):
    core, row, layer = place_ref[0], place_ref[1], place_ref[3]

    def run(parts):
        square = jnp.zeros((8, 128), f32)
        norm = jnp.zeros((1, 128), f32)
        totals = []
        for part in parts:
            extra = jnp.zeros((32, 128), f32)
            for x in range(N_X):
                block = part[x, 0:512, :].astype(f32)
                square += jnp.sum((block * block).reshape(64, 8, 128), axis=0)
                extra += part[x, 1024:1056, :].astype(f32)
            line = [extra[3 * z : 3 * z + 1] + extra[3 * z + 1 : 3 * z + 2] + extra[3 * z + 2 : 3 * z + 3] for z in range(N_Z)]
            norm += extra[24:25] + extra[25:26] + extra[26:27]
            totals.append(jnp.concatenate(line, axis=1))
        grad_total = jnp.sum(jnp.sum(square, axis=1, keepdims=True), axis=0, keepdims=True)
        wnorm = jnp.sqrt(norm[:, 0:1])
        gnorm = jnp.sqrt(grad_total)
        rate = learn_rate * (trust_coef * wnorm / (gnorm + weight_decay * wnorm))
        stores = []
        for x in range(N_X):
            tiles = [part[x, 512:1024, :].astype(f32).reshape(N_Y, N_Z, 8, 128) for part in parts]
            rows = slice(128 * x, 128 * x + 128)
            h, strip = x // 2, x % 2 * 2
            for z in range(N_Z):
                columns = slice(128 * z, 128 * z + 128)
                even, odd = [tile[:, z] for tile in tiles]
                top = jnp.concatenate([even[:, :, :64], odd[:, :, :64]], axis=2)
                bottom = jnp.concatenate([even[:, :, 64:], odd[:, :, 64:]], axis=2)
                decayed = jnp.stack([top, bottom], axis=1).reshape(128, 128)
                lines = slice(64 * z, 64 * z + 64)
                step = jnp.concatenate([parts[h][strip, lines, :], parts[h][strip + 1, lines, :]], axis=0).astype(f32)
                step += weight_decay * w_ref[rows, columns].astype(f32)
                new_w[rows, columns] = (decayed - rate * step).astype(bf16)
            stores.append(pltpu.make_async_copy(new_w.at[rows], new_w_hbm.at[rows], sems.at[x]))
            stores[-1].start()
        bn_grad = jnp.concatenate([totals[1], totals[0]], axis=0) * (1.0 / BATCH)
        new_bnv = momentum * bnv_ref[...] + learn_rate * bn_grad
        new_bnv_ref[...] = new_bnv
        new_bn_ref[...] = bn_ref[...] - new_bnv
        for h in range(2):

            @pl.when(row // 16 == h)
            def _():
                start = pl.multiple_of(layer * 64 + row % 4 * 16, 16)
                pair = parts[h][row % 16 // 4, pl.ds(start, 16), :].astype(f32)
                own = jnp.where(core == 0, pair[:, :64], pair[:, 64:])
                new_vel = momentum * vel_ref[...] + rate * (own + weight_decay * master_ref[...])
                new_vel_ref[...] = new_vel
                new_master_ref[...] = master_ref[...] - new_vel

        for copy in stores:
            copy.wait()

    @pl.when(core == 0)
    def _():
        run((mine_ref, other_ref))

    @pl.when(core == 1)
    def _():
        run((other_ref, mine_ref))


def shape(dims, kind):
    return jax.ShapeDtypeStruct(dims, kind)


SMEM = pl.BlockSpec(memory_space=pltpu.SMEM)
VMEM = pl.BlockSpec(memory_space=pltpu.VMEM)
HBM = pl.BlockSpec(memory_space=pltpu.HBM)


def body(activations, pre_activation, pooled_grad, weights, master, velocity, bn_params, bn_velocity):
    core = lax.axis_index("core").astype(jnp.int32)
    layer = lax.axis_index("z").astype(jnp.int32)
    row = (lax.axis_index("x") * 8 + lax.axis_index("y")).astype(jnp.int32)
    place = jnp.stack([core, row, layer * 2 + core, layer])
    msg = pl.pallas_call(
        stats_kernel,
        out_shape=shape((N_COL, STAT_ROWS, 128), f32),
        in_specs=[HBM] * 4,
        out_specs=VMEM,
        scratch_shapes=[
            pltpu.VMEM((IMG, PIX, CIN), bf16),
            pltpu.VMEM((IMG, PIX, COUT), bf16),
            pltpu.VMEM((IMG, COUT), f32),
            pltpu.VMEM((CIN, COUT), bf16),
            pltpu.VMEM((ROWS, CIN), bf16),
            pltpu.VMEM((ROWS, COUT), bf16),
            pltpu.SemaphoreType.DMA((4, PARTS)),
        ],
        compiler_params=params(60),
        name="conv_stats",
    )(activations, pre_activation, pooled_grad, weights)
    stats = lax.all_to_all(msg, GROUP, 0, 0)
    conv_grad, keep, send, line = pl.pallas_call(
        grad_kernel,
        out_shape=(
            shape((ROWS, COUT), bf16),
            shape((HALF, COUT), f32),
            shape((HALF, COUT), bf16),
            shape((8, 128), f32),
        ),
        in_specs=[SMEM] + [VMEM] * 6,
        out_specs=(VMEM,) * 4,
        scratch_shapes=[pltpu.VMEM((ROWS, CIN), bf16), pltpu.VMEM((ROWS, COUT), bf16), pltpu.VMEM((16, 128), f32)],
        compiler_params=params(),
        name="conv_grad",
    )(place, stats, weights, activations, pre_activation, pooled_grad, bn_params)
    swap = [(0, 1), (1, 0)]
    got = lax.ppermute(send, "core", swap)
    input_grad = pl.pallas_call(
        back_kernel,
        out_shape=shape((IMG, PIX, CIN), bf16),
        in_specs=[VMEM] * 2,
        out_specs=VMEM,
        compiler_params=params(),
        cost_estimate=pl.CostEstimate(flops=2 * ROWS * CIN * COUT, bytes_accessed=4 << 20, transcendentals=0),
        name="input_grad",
    )(conv_grad, weights)
    halves = pl.pallas_call(
        pair_kernel,
        out_shape=shape((HALF, COUT), bf16),
        in_specs=[VMEM] * 2,
        out_specs=VMEM,
        compiler_params=params(),
        name="pair_sum",
    )(keep, got)
    arrived = lax.all_to_all(halves.reshape(N_X, HALF // N_X, COUT), "x", 0, 0)
    lines = pl.pallas_call(
        line_kernel,
        out_shape=shape((N_Y, N_Z, 8, 128), bf16),
        in_specs=[VMEM],
        out_specs=VMEM,
        compiler_params=params(),
        name="line_sum",
    )(arrived)
    arrived = lax.all_to_all(lines.reshape(N_Y * N_Z, 8, 128), PLANE, 0, 0)
    block = pl.pallas_call(
        block_kernel,
        out_shape=shape((N_Y * N_Z, SIDE_ROWS, 128), bf16),
        in_specs=[VMEM] * 4,
        out_specs=VMEM,
        compiler_params=params(),
        name="block_sum",
    )(arrived, line, master, velocity)
    wide = pl.pallas_call(
        plane_kernel,
        out_shape=shape((N_X, WIDE_ROWS, 128), bf16),
        in_specs=[VMEM],
        out_specs=VMEM,
        compiler_params=params(),
        name="plane_join",
    )(lax.all_to_all(block, PLANE, 0, 0))
    mine = lax.all_to_all(wide, "x", 0, 0)
    other = lax.ppermute(mine, "core", swap)
    new_master, new_velocity, new_weights, new_bn, new_bn_velocity = pl.pallas_call(
        update_kernel,
        out_shape=(
            shape((16, 64), f32),
            shape((16, 64), f32),
            shape((CIN, COUT), bf16),
            shape((2, COUT), f32),
            shape((2, COUT), f32),
        ),
        in_specs=[SMEM] + [VMEM] * 7,
        out_specs=(VMEM, VMEM, HBM, VMEM, VMEM),
        scratch_shapes=[pltpu.VMEM((CIN, COUT), bf16), pltpu.SemaphoreType.DMA((N_X,))],
        compiler_params=params(),
        name="update",
    )(place, mine, other, weights, master, velocity, bn_params, bn_velocity)
    return input_grad, new_master, new_velocity, new_weights, new_bn, new_bn_velocity


def solution(mesh):
    fine = Mesh(mesh.devices.reshape(4, 8, 8, 2), ALL)
    block = P(("x", "y"), ("z", "core"))
    return jax.shard_map(
        body,
        mesh=fine,
        in_specs=(P(ALL, None, None), P(ALL, None, None), P(ALL, None), P(), block, block, P(), P()),
        out_specs=(P(ALL, None, None), block, block, P(), P(), P()),
        check_vma=False,
    )
```

```python
import jax
import jax.numpy as jnp
from jax import lax
from jax.experimental import pallas as pl
from jax.experimental.pallas import tpu as pltpu
from jax.sharding import Mesh, PartitionSpec as P

epsilon = 1e-05
trust_coef = 0.001
weight_decay = 0.0001
momentum = 0.9
learn_rate = 12.0

IMG, PIX, STRIDE = 12, 49, 64
CIN, COUT = 512, 1024
ROWS = IMG * STRIDE
HALF = CIN // 2
N_ROW, N_COL = 32, 16
N_X, N_Y, N_Z = 4, 8, 8
M = PIX * IMG * N_COL
BATCH = IMG * N_ROW * N_COL
CHUNKS = COUT // 128
PLANE, ALL = ("y", "z"), ("x", "y", "z", "core")
STAT_ROWS = 40
SIDE_ROWS = 24
WIDE_ROWS = 1056
PARTS = 2
STRIP = 512
bf16, f32 = jnp.bfloat16, jnp.float32


def params(megabytes=20):
    return pltpu.CompilerParams(vmem_limit_bytes=megabytes << 20)


def fold(line):
    return jnp.concatenate([line[:, 128 * k : 128 * k + 128] for k in range(line.shape[1] // 128)], axis=0)


def unfold(block):
    return jnp.concatenate([block[k : k + 1] for k in range(block.shape[0])], axis=1)


def split(line):
    high = line.astype(bf16).astype(f32)
    middle = (line - high).astype(bf16).astype(f32)
    return high, middle, line - high - middle


def rows_of(count, lines, dims):
    row = lax.broadcasted_iota(jnp.int32, dims, 0)
    block = jnp.zeros(dims, f32)
    for k in range(count):
        block = jnp.where(row == k, jnp.broadcast_to(lines[k], dims), block)
    return block


def stats_kernel(act_hbm, pre_hbm, pool_hbm, w_hbm, msg_ref, act, pre, pool, w, actp, conv, sem_in):
    step = IMG // PARTS
    loads = []
    for k in range(PARTS):
        part = pl.ds(step * k, step)
        strip = pl.ds(CIN // PARTS * k, CIN // PARTS)
        loads.append(pltpu.make_async_copy(w_hbm.at[strip], w.at[strip], sem_in.at[0, k]))
        loads.append(pltpu.make_async_copy(act_hbm.at[part], act.at[part], sem_in.at[1, k]))
    for copy in loads:
        copy.start()
    later = [pltpu.make_async_copy(pool_hbm, pool, sem_in.at[3, 0])]
    for k in range(PARTS):
        part = pl.ds(step * k, step)
        later.append(pltpu.make_async_copy(pre_hbm.at[part], pre.at[part], sem_in.at[2, k]))
    for copy in later:
        copy.start()
    actp[...] = jnp.zeros_like(actp)
    for copy in loads:
        copy.wait()
    for i in range(IMG):
        actp[STRIDE * i : STRIDE * i + PIX, :] = act[i]
    act_total = jnp.sum(actp[...].astype(f32), axis=0, keepdims=True)
    strips = [slice(STRIP * k, STRIP * k + STRIP) for k in range(COUT // STRIP)]
    lines = []
    for strip in strips:
        value = jnp.dot(actp[...], w[:, strip], preferred_element_type=f32).astype(bf16)
        conv[:, strip] = value
        value = value.astype(f32)
        total = jnp.sum(value, axis=0, keepdims=True)
        square = jnp.sum(value * value, axis=0, keepdims=True)
        lines.append([total, square])
    for copy in later:
        copy.wait()
    for k, strip in enumerate(strips):
        up = jnp.zeros((1, STRIP), f32)
        up_conv = jnp.zeros((1, STRIP), f32)
        for i in range(IMG):
            value = conv[STRIDE * i : STRIDE * i + STRIDE, strip].astype(f32)[:PIX]
            passed = pre[i, :, strip].astype(f32) > 0
            share = pool[i : i + 1, strip] / PIX
            up += share * jnp.sum(jnp.where(passed, 1.0, 0.0), axis=0, keepdims=True)
            up_conv += share * jnp.sum(jnp.where(passed, value, 0.0), axis=0, keepdims=True)
        lines[k] += [up, up_conv]
    sums = [fold(jnp.concatenate([line[q] for line in lines], axis=1)) for q in range(4)]
    msg = jnp.concatenate(sums + [fold(act_total), jnp.zeros((4, 128), f32)], axis=0)
    msg_ref[...] = msg


def chip_kernel(got_ref, out_ref):
    out_ref[...] = jnp.broadcast_to((got_ref[0] + got_ref[1])[None], out_ref.shape)


def grad_kernel(
    place_ref, stat_ref, w_ref, act_ref, pre_ref, pool_ref, bn_ref, cg_ref, actp, send_ref, line_ref, conv_ref, lines
):
    core, layer = place_ref[0], place_ref[3]
    sums = jnp.sum(stat_ref[...], axis=0)
    sum_up = sums[16:24]
    act_mean = (unfold(sums[32:36]) / M).astype(bf16).astype(f32)
    mean = sums[0:8] / M
    variance = sums[8:16] / M - mean * mean
    rstd = lax.rsqrt(variance + epsilon)
    sum_upx = rstd * (sums[24:32] - mean * sum_up)
    lines[0:8, :] = sum_up
    lines[8:16, :] = sum_upx
    line_ref[...] = jnp.broadcast_to(lines[pl.ds(core * 8 + layer, 1), :], (8, 128))
    scale = fold(bn_ref[0:1, :]) * rstd
    shift = unfold(scale * (sum_up / M))
    slope = unfold(scale * (sum_upx / M) * rstd)
    mean = unfold(mean)
    scale = unfold(scale)
    actp[...] = jnp.zeros_like(actp)
    for i in range(IMG):
        actp[STRIDE * i : STRIDE * i + PIX, :] = act_ref[i]
    conv_ref[...] = jnp.dot(actp[...], w_ref[...], preferred_element_type=f32).astype(bf16)
    cg_ref[...] = jnp.zeros_like(cg_ref)
    cg_total = jnp.zeros((1, COUT), f32)
    for i in range(IMG):
        conv = conv_ref[STRIDE * i : STRIDE * i + STRIDE, :].astype(f32)[:PIX]
        on = scale * (pool_ref[i : i + 1, :] / PIX) - shift
        low = (jnp.where(pre_ref[i].astype(f32) > 0, on, -shift) - slope * (conv - mean)).astype(bf16)
        cg_ref[STRIDE * i : STRIDE * i + PIX, :] = low
        cg_total += jnp.sum(low.astype(f32), axis=0, keepdims=True)
    edge = actp[48:64, :].astype(f32)
    row = lax.broadcasted_iota(jnp.int32, edge.shape, 0)
    actp[48:64, :] = jnp.where((row >= 1) & (row < 4), -act_mean, edge).astype(bf16)
    high, middle, rest = split(cg_total)
    edge = cg_ref[48:64, :].astype(f32)
    cg_ref[48:64, :] = (edge + rows_of(4, [jnp.zeros_like(high), high, middle, rest], edge.shape)).astype(bf16)
    send_ref[...] = half_grad(actp, cg_ref, 1 - core).astype(bf16)


def half_grad(actp, cg_ref, half):
    columns = actp[:, pl.ds(pl.multiple_of(half * HALF, HALF), HALF)]
    return lax.dot_general(columns, cg_ref[...], (((0,), (0,)), ((), ())), preferred_element_type=f32)


def keep_kernel(place_ref, actp, cg_ref, keep_ref):
    keep_ref[...] = half_grad(actp, cg_ref, place_ref[0])


def back_kernel(cg_ref, w_ref, out_ref):
    back = lax.dot_general(cg_ref[...], w_ref[...], (((1,), (1,)), ((), ())), preferred_element_type=f32)
    for i in range(IMG):
        out_ref[i] = back[STRIDE * i : STRIDE * i + PIX].astype(bf16)


def pair_kernel(keep_ref, got_ref, out_ref):
    out_ref[...] = (keep_ref[...] + got_ref[...].astype(f32)).astype(bf16)


def line_kernel(got_ref, out_ref):
    total = jnp.sum(got_ref[...].astype(f32), axis=0).reshape(N_Z, 8, COUT)
    for y in range(N_Y):
        out_ref[y] = total[:, :, 128 * y : 128 * y + 128].astype(bf16)


def block_kernel(got_ref, line_ref, master_ref, vel_ref, out_ref):
    total = jnp.sum(got_ref[...].astype(f32), axis=0) * (1.0 / BATCH)
    master = master_ref[...]
    decayed = master - momentum * vel_ref[...]
    decayed = jnp.concatenate([decayed[:8], decayed[8:]], axis=1)
    norm = jnp.sum(jnp.sum(master * master, axis=1, keepdims=True), axis=0, keepdims=True)
    square = jnp.sum(jnp.sum(total * total, axis=1, keepdims=True), axis=0, keepdims=True)
    norms = split(jnp.broadcast_to(norm, (8, 128))) + split(jnp.broadcast_to(square, (8, 128)))[:2]
    extra = rows_of(8, split(line_ref[...]) + norms, (8, 128))
    block = jnp.concatenate([total, decayed, extra], axis=0).astype(bf16)
    out_ref[...] = jnp.broadcast_to(block[None], out_ref.shape)


def plane_kernel(got_ref, out_ref):
    extra = jnp.sum(got_ref[:, 16:24, :].astype(f32).reshape(N_Y, N_Z, 8, 128), axis=0)
    lines = []
    norm = jnp.zeros((1, 128), f32)
    square = jnp.zeros((1, 128), f32)
    for z in range(N_Z):
        lines += split(extra[z, 0:1] + extra[z, 1:2] + extra[z, 2:3])
        norm += extra[z, 3:4] + extra[z, 4:5] + extra[z, 5:6]
        square += extra[z, 6:7] + extra[z, 7:8]
    lines += split(norm) + split(square)
    extra = jnp.concatenate(lines + [jnp.zeros((2, 128), f32)], axis=0).astype(bf16)
    grad = got_ref[:, 0:8, :].astype(f32).reshape(512, 128).astype(bf16)
    decayed = got_ref[:, 8:16, :].astype(f32).reshape(512, 128).astype(bf16)
    for p in range(N_X):
        out_ref[p, 0:512, :] = grad
        out_ref[p, 512:1024, :] = decayed
        out_ref[p, 1024:1056, :] = extra


def update_kernel(
    place_ref, mine_ref, other_ref, w_ref, master_ref, vel_ref, bn_ref, bnv_ref,
    new_master_ref, new_vel_ref, new_w_hbm, new_bn_ref, new_bnv_ref, new_w, sems,
):
    core, row, layer = place_ref[0], place_ref[1], place_ref[3]

    def run(parts):
        square = jnp.zeros((1, 128), f32)
        norm = jnp.zeros((1, 128), f32)
        totals = []
        for part in parts:
            extra = jnp.zeros((32, 128), f32)
            for x in range(N_X):
                extra += part[x, 1024:1056, :].astype(f32)
            line = [extra[3 * z : 3 * z + 1] + extra[3 * z + 1 : 3 * z + 2] + extra[3 * z + 2 : 3 * z + 3] for z in range(N_Z)]
            norm += extra[24:25] + extra[25:26] + extra[26:27]
            square += extra[27:28] + extra[28:29] + extra[29:30]
            totals.append(jnp.concatenate(line, axis=1))
        wnorm = jnp.sqrt(norm[:, 0:1])
        gnorm = jnp.sqrt(square[:, 0:1])
        rate = learn_rate * (trust_coef * wnorm / (gnorm + weight_decay * wnorm))
        stores = []
        for x in range(N_X):
            tiles = [part[x, 512:1024, :].astype(f32).reshape(N_Y, N_Z, 8, 128) for part in parts]
            rows = slice(128 * x, 128 * x + 128)
            h, strip = x // 2, x % 2 * 2
            for z in range(N_Z):
                columns = slice(128 * z, 128 * z + 128)
                even, odd = [tile[:, z] for tile in tiles]
                top = jnp.concatenate([even[:, :, :64], odd[:, :, :64]], axis=2)
                bottom = jnp.concatenate([even[:, :, 64:], odd[:, :, 64:]], axis=2)
                decayed = jnp.stack([top, bottom], axis=1).reshape(128, 128)
                lines = slice(64 * z, 64 * z + 64)
                step = jnp.concatenate([parts[h][strip, lines, :], parts[h][strip + 1, lines, :]], axis=0).astype(f32)
                step += weight_decay * w_ref[rows, columns].astype(f32)
                new_w[rows, columns] = (decayed - rate * step).astype(bf16)
            stores.append(pltpu.make_async_copy(new_w.at[rows], new_w_hbm.at[rows], sems.at[x]))
            stores[-1].start()
        bn_grad = jnp.concatenate([totals[1], totals[0]], axis=0) * (1.0 / BATCH)
        new_bnv = momentum * bnv_ref[...] + learn_rate * bn_grad
        new_bnv_ref[...] = new_bnv
        new_bn_ref[...] = bn_ref[...] - new_bnv
        for h in range(2):

            @pl.when(row // 16 == h)
            def _():
                start = pl.multiple_of(layer * 64 + row % 4 * 16, 16)
                pair = parts[h][row % 16 // 4, pl.ds(start, 16), :].astype(f32)
                own = jnp.where(core == 0, pair[:, :64], pair[:, 64:])
                new_vel = momentum * vel_ref[...] + rate * (own + weight_decay * master_ref[...])
                new_vel_ref[...] = new_vel
                new_master_ref[...] = master_ref[...] - new_vel

        for copy in stores:
            copy.wait()

    @pl.when(core == 0)
    def _():
        run((mine_ref, other_ref))

    @pl.when(core == 1)
    def _():
        run((other_ref, mine_ref))


def shape(dims, kind):
    return jax.ShapeDtypeStruct(dims, kind)


SMEM = pl.BlockSpec(memory_space=pltpu.SMEM)
VMEM = pl.BlockSpec(memory_space=pltpu.VMEM)
HBM = pl.BlockSpec(memory_space=pltpu.HBM)


def body(activations, pre_activation, pooled_grad, weights, master, velocity, bn_params, bn_velocity):
    core = lax.axis_index("core").astype(jnp.int32)
    layer = lax.axis_index("z").astype(jnp.int32)
    row = (lax.axis_index("x") * 8 + lax.axis_index("y")).astype(jnp.int32)
    place = jnp.stack([core, row, layer * 2 + core, layer])
    msg = pl.pallas_call(
        stats_kernel,
        out_shape=shape((STAT_ROWS, 128), f32),
        in_specs=[HBM] * 4,
        out_specs=VMEM,
        scratch_shapes=[
            pltpu.VMEM((IMG, PIX, CIN), bf16),
            pltpu.VMEM((IMG, PIX, COUT), bf16),
            pltpu.VMEM((IMG, COUT), f32),
            pltpu.VMEM((CIN, COUT), bf16),
            pltpu.VMEM((ROWS, CIN), bf16),
            pltpu.VMEM((ROWS, COUT), bf16),
            pltpu.SemaphoreType.DMA((4, PARTS)),
        ],
        compiler_params=params(60),
        name="conv_stats",
    )(activations, pre_activation, pooled_grad, weights)
    chip = pl.pallas_call(
        chip_kernel,
        out_shape=shape((N_Z, STAT_ROWS, 128), f32),
        in_specs=[VMEM],
        out_specs=VMEM,
        compiler_params=params(),
        name="chip_stats",
    )(lax.all_gather(msg, "core"))
    stats = lax.all_to_all(chip, "z", 0, 0)
    conv_grad, act, send, line = pl.pallas_call(
        grad_kernel,
        out_shape=(
            shape((ROWS, COUT), bf16),
            shape((ROWS, CIN), bf16),
            shape((HALF, COUT), bf16),
            shape((8, 128), f32),
        ),
        in_specs=[SMEM] + [VMEM] * 6,
        out_specs=(VMEM,) * 4,
        scratch_shapes=[pltpu.VMEM((ROWS, COUT), bf16), pltpu.VMEM((16, 128), f32)],
        compiler_params=params(),
        name="conv_grad",
    )(place, stats, weights, activations, pre_activation, pooled_grad, bn_params)
    swap = [(0, 1), (1, 0)]
    got = lax.ppermute(send, "core", swap)
    keep = pl.pallas_call(
        keep_kernel,
        out_shape=shape((HALF, COUT), f32),
        in_specs=[SMEM] + [VMEM] * 2,
        out_specs=VMEM,
        compiler_params=params(),
        cost_estimate=pl.CostEstimate(flops=2 * ROWS * HALF * COUT, bytes_accessed=4 << 20, transcendentals=0),
        name="keep_grad",
    )(place, act, conv_grad)
    input_grad = pl.pallas_call(
        back_kernel,
        out_shape=shape((IMG, PIX, CIN), bf16),
        in_specs=[VMEM] * 2,
        out_specs=VMEM,
        compiler_params=params(),
        cost_estimate=pl.CostEstimate(flops=2 * ROWS * CIN * COUT, bytes_accessed=4 << 20, transcendentals=0),
        name="input_grad",
    )(conv_grad, weights)
    halves = pl.pallas_call(
        pair_kernel,
        out_shape=shape((HALF, COUT), bf16),
        in_specs=[VMEM] * 2,
        out_specs=VMEM,
        compiler_params=params(),
        name="pair_sum",
    )(keep, got)
    arrived = lax.all_to_all(halves.reshape(N_X, HALF // N_X, COUT), "x", 0, 0)
    lines = pl.pallas_call(
        line_kernel,
        out_shape=shape((N_Y, N_Z, 8, 128), bf16),
        in_specs=[VMEM],
        out_specs=VMEM,
        compiler_params=params(),
        name="line_sum",
    )(arrived)
    arrived = lax.all_to_all(lines.reshape(N_Y * N_Z, 8, 128), PLANE, 0, 0)
    block = pl.pallas_call(
        block_kernel,
        out_shape=shape((N_Y * N_Z, SIDE_ROWS, 128), bf16),
        in_specs=[VMEM] * 4,
        out_specs=VMEM,
        compiler_params=params(),
        name="block_sum",
    )(arrived, line, master, velocity)
    wide = pl.pallas_call(
        plane_kernel,
        out_shape=shape((N_X, WIDE_ROWS, 128), bf16),
        in_specs=[VMEM],
        out_specs=VMEM,
        compiler_params=params(),
        name="plane_join",
    )(lax.all_to_all(block, PLANE, 0, 0))
    mine = lax.all_to_all(wide, "x", 0, 0)
    other = lax.ppermute(mine, "core", swap)
    new_master, new_velocity, new_weights, new_bn, new_bn_velocity = pl.pallas_call(
        update_kernel,
        out_shape=(
            shape((16, 64), f32),
            shape((16, 64), f32),
            shape((CIN, COUT), bf16),
            shape((2, COUT), f32),
            shape((2, COUT), f32),
        ),
        in_specs=[SMEM] + [VMEM] * 7,
        out_specs=(VMEM, VMEM, HBM, VMEM, VMEM),
        scratch_shapes=[pltpu.VMEM((CIN, COUT), bf16), pltpu.SemaphoreType.DMA((N_X,))],
        compiler_params=params(),
        name="update",
    )(place, mine, other, weights, master, velocity, bn_params, bn_velocity)
    return input_grad, new_master, new_velocity, new_weights, new_bn, new_bn_velocity


def solution(mesh):
    fine = Mesh(mesh.devices.reshape(4, 8, 8, 2), ALL)
    block = P(("x", "y"), ("z", "core"))
    return jax.shard_map(
        body,
        mesh=fine,
        in_specs=(P(ALL, None, None), P(ALL, None, None), P(ALL, None), P(), block, block, P(), P()),
        out_specs=(P(ALL, None, None), block, block, P(), P(), P()),
        check_vma=False,
    )
```

```python
import jax
import jax.numpy as jnp
from jax import lax
from jax.experimental import pallas as pl
from jax.experimental.pallas import tpu as pltpu
from jax.sharding import Mesh, PartitionSpec as P

epsilon = 1e-05
trust_coef = 0.001
weight_decay = 0.0001
momentum = 0.9
learn_rate = 12.0

IMG, PIX, STRIDE = 12, 49, 64
CIN, COUT = 512, 1024
ROWS = IMG * STRIDE
HALF = CIN // 2
N_ROW, N_COL = 32, 16
N_X, N_Y, N_Z = 4, 8, 8
M = PIX * IMG * N_COL
BATCH = IMG * N_ROW * N_COL
CHUNKS = COUT // 128
PLANE, ALL = ("y", "z"), ("x", "y", "z", "core")
STAT_ROWS = 40
SIDE_ROWS = 24
WIDE_ROWS = 1056
PARTS = 2
STRIP = 512
bf16, f32 = jnp.bfloat16, jnp.float32


def params(megabytes=20):
    return pltpu.CompilerParams(vmem_limit_bytes=megabytes << 20)


def fold(line):
    return jnp.concatenate([line[:, 128 * k : 128 * k + 128] for k in range(line.shape[1] // 128)], axis=0)


def unfold(block):
    return jnp.concatenate([block[k : k + 1] for k in range(block.shape[0])], axis=1)


def split(line):
    high = line.astype(bf16).astype(f32)
    middle = (line - high).astype(bf16).astype(f32)
    return high, middle, line - high - middle


def rows_of(count, lines, dims):
    row = lax.broadcasted_iota(jnp.int32, dims, 0)
    block = jnp.zeros(dims, f32)
    for k in range(count):
        block = jnp.where(row == k, jnp.broadcast_to(lines[k], dims), block)
    return block


def stats_kernel(act_hbm, pre_hbm, pool_hbm, w_hbm, msg_ref, act, pre, pool, w, actp, conv, sem_in):
    step = IMG // PARTS
    loads = []
    for k in range(PARTS):
        part = pl.ds(step * k, step)
        strip = pl.ds(CIN // PARTS * k, CIN // PARTS)
        loads.append(pltpu.make_async_copy(w_hbm.at[strip], w.at[strip], sem_in.at[0, k]))
        loads.append(pltpu.make_async_copy(act_hbm.at[part], act.at[part], sem_in.at[1, k]))
    for copy in loads:
        copy.start()
    later = [pltpu.make_async_copy(pool_hbm, pool, sem_in.at[3, 0])]
    for k in range(PARTS):
        part = pl.ds(step * k, step)
        later.append(pltpu.make_async_copy(pre_hbm.at[part], pre.at[part], sem_in.at[2, k]))
    for copy in later:
        copy.start()
    actp[...] = jnp.zeros_like(actp)
    for copy in loads:
        copy.wait()
    for i in range(IMG):
        actp[STRIDE * i : STRIDE * i + PIX, :] = act[i]
    act_total = jnp.sum(actp[...].astype(f32), axis=0, keepdims=True)
    strips = [slice(STRIP * k, STRIP * k + STRIP) for k in range(COUT // STRIP)]
    lines = []
    for strip in strips:
        value = jnp.dot(actp[...], w[:, strip], preferred_element_type=f32).astype(bf16)
        conv[:, strip] = value
        value = value.astype(f32)
        total = jnp.sum(value, axis=0, keepdims=True)
        square = jnp.sum(value * value, axis=0, keepdims=True)
        lines.append([total, square])
    for copy in later:
        copy.wait()
    for k, strip in enumerate(strips):
        up = jnp.zeros((1, STRIP), f32)
        up_conv = jnp.zeros((1, STRIP), f32)
        for i in range(IMG):
            value = conv[STRIDE * i : STRIDE * i + STRIDE, strip].astype(f32)[:PIX]
            passed = pre[i, :, strip].astype(f32) > 0
            share = pool[i : i + 1, strip] / PIX
            up += share * jnp.sum(jnp.where(passed, 1.0, 0.0), axis=0, keepdims=True)
            up_conv += share * jnp.sum(jnp.where(passed, value, 0.0), axis=0, keepdims=True)
        lines[k] += [up, up_conv]
    sums = [fold(jnp.concatenate([line[q] for line in lines], axis=1)) for q in range(4)]
    msg = jnp.concatenate(sums + [fold(act_total), jnp.zeros((4, 128), f32)], axis=0)
    msg_ref[...] = msg


def chip_kernel(got_ref, out_ref):
    out_ref[...] = jnp.broadcast_to((got_ref[0] + got_ref[1])[None], out_ref.shape)


def grad_kernel(
    stat_ref, w_ref, act_ref, pre_ref, pool_ref, bn_ref, cg_ref, actp, send_ref, line_ref, conv_ref, lines
):
    core, layer = core_of(), lax.axis_index("z").astype(jnp.int32)
    sums = jnp.sum(stat_ref[...], axis=0)
    sum_up = sums[16:24]
    act_mean = (unfold(sums[32:36]) / M).astype(bf16).astype(f32)
    mean = sums[0:8] / M
    variance = sums[8:16] / M - mean * mean
    rstd = lax.rsqrt(variance + epsilon)
    sum_upx = rstd * (sums[24:32] - mean * sum_up)
    lines[0:8, :] = sum_up
    lines[8:16, :] = sum_upx
    line_ref[...] = jnp.broadcast_to(lines[pl.ds(core * 8 + layer, 1), :], (8, 128))
    scale = fold(bn_ref[0:1, :]) * rstd
    shift = unfold(scale * (sum_up / M))
    slope = unfold(scale * (sum_upx / M) * rstd)
    mean = unfold(mean)
    scale = unfold(scale)
    actp[...] = jnp.zeros_like(actp)
    for i in range(IMG):
        actp[STRIDE * i : STRIDE * i + PIX, :] = act_ref[i]
    conv_ref[...] = jnp.dot(actp[...], w_ref[...], preferred_element_type=f32).astype(bf16)
    cg_ref[...] = jnp.zeros_like(cg_ref)
    cg_total = jnp.zeros((1, COUT), f32)
    for i in range(IMG):
        conv = conv_ref[STRIDE * i : STRIDE * i + STRIDE, :].astype(f32)[:PIX]
        on = scale * (pool_ref[i : i + 1, :] / PIX) - shift
        low = (jnp.where(pre_ref[i].astype(f32) > 0, on, -shift) - slope * (conv - mean)).astype(bf16)
        cg_ref[STRIDE * i : STRIDE * i + PIX, :] = low
        cg_total += jnp.sum(low.astype(f32), axis=0, keepdims=True)
    edge = actp[48:64, :].astype(f32)
    row = lax.broadcasted_iota(jnp.int32, edge.shape, 0)
    actp[48:64, :] = jnp.where((row >= 1) & (row < 4), -act_mean, edge).astype(bf16)
    high, middle, rest = split(cg_total)
    edge = cg_ref[48:64, :].astype(f32)
    cg_ref[48:64, :] = (edge + rows_of(4, [jnp.zeros_like(high), high, middle, rest], edge.shape)).astype(bf16)
    send_ref[...] = half_grad(actp, cg_ref, 1 - core).astype(bf16)


def core_of():
    return lax.axis_index("core").astype(jnp.int32)


def half_grad(actp, cg_ref, half):
    columns = actp[:, pl.ds(pl.multiple_of(half * HALF, HALF), HALF)]
    return lax.dot_general(columns, cg_ref[...], (((0,), (0,)), ((), ())), preferred_element_type=f32)


def keep_kernel(actp, cg_ref, keep_ref):
    keep_ref[...] = half_grad(actp, cg_ref, core_of())


def back_kernel(cg_ref, w_ref, out_ref):
    back = lax.dot_general(cg_ref[...], w_ref[...], (((1,), (1,)), ((), ())), preferred_element_type=f32)
    for i in range(IMG):
        out_ref[i] = back[STRIDE * i : STRIDE * i + PIX].astype(bf16)


def pair_kernel(keep_ref, got_ref, out_ref):
    out_ref[...] = (keep_ref[...] + got_ref[...].astype(f32)).astype(bf16)


def line_kernel(got_ref, out_ref):
    total = jnp.sum(got_ref[...].astype(f32), axis=0).reshape(N_Z, 8, COUT)
    for y in range(N_Y):
        out_ref[y] = total[:, :, 128 * y : 128 * y + 128].astype(bf16)


def block_kernel(got_ref, line_ref, master_ref, vel_ref, out_ref):
    total = jnp.sum(got_ref[...].astype(f32), axis=0) * (1.0 / BATCH)
    master = master_ref[...]
    decayed = master - momentum * vel_ref[...]
    decayed = jnp.concatenate([decayed[:8], decayed[8:]], axis=1)
    norm = jnp.sum(jnp.sum(master * master, axis=1, keepdims=True), axis=0, keepdims=True)
    square = jnp.sum(jnp.sum(total * total, axis=1, keepdims=True), axis=0, keepdims=True)
    norms = split(jnp.broadcast_to(norm, (8, 128))) + split(jnp.broadcast_to(square, (8, 128)))[:2]
    extra = rows_of(8, split(line_ref[...]) + norms, (8, 128))
    block = jnp.concatenate([total, decayed, extra], axis=0).astype(bf16)
    out_ref[...] = jnp.broadcast_to(block[None], out_ref.shape)


def plane_kernel(got_ref, out_ref):
    extra = jnp.sum(got_ref[:, 16:24, :].astype(f32).reshape(N_Y, N_Z, 8, 128), axis=0)
    lines = []
    norm = jnp.zeros((1, 128), f32)
    square = jnp.zeros((1, 128), f32)
    for z in range(N_Z):
        lines += split(extra[z, 0:1] + extra[z, 1:2] + extra[z, 2:3])
        norm += extra[z, 3:4] + extra[z, 4:5] + extra[z, 5:6]
        square += extra[z, 6:7] + extra[z, 7:8]
    lines += split(norm) + split(square)
    extra = jnp.concatenate(lines + [jnp.zeros((2, 128), f32)], axis=0).astype(bf16)
    grad = got_ref[:, 0:8, :].astype(f32).reshape(512, 128).astype(bf16)
    decayed = got_ref[:, 8:16, :].astype(f32).reshape(512, 128).astype(bf16)
    for p in range(N_X):
        out_ref[p, 0:512, :] = grad
        out_ref[p, 512:1024, :] = decayed
        out_ref[p, 1024:1056, :] = extra


def update_kernel(
    mine_ref, other_ref, w_ref, master_ref, vel_ref, bn_ref, bnv_ref,
    new_master_ref, new_vel_ref, new_w_hbm, new_bn_ref, new_bnv_ref, new_w, sems,
):
    core, layer = core_of(), lax.axis_index("z").astype(jnp.int32)
    row = (lax.axis_index("x") * N_Y + lax.axis_index("y")).astype(jnp.int32)

    def run(parts):
        square = jnp.zeros((1, 128), f32)
        norm = jnp.zeros((1, 128), f32)
        totals = []
        for part in parts:
            extra = jnp.zeros((32, 128), f32)
            for x in range(N_X):
                extra += part[x, 1024:1056, :].astype(f32)
            line = [extra[3 * z : 3 * z + 1] + extra[3 * z + 1 : 3 * z + 2] + extra[3 * z + 2 : 3 * z + 3] for z in range(N_Z)]
            norm += extra[24:25] + extra[25:26] + extra[26:27]
            square += extra[27:28] + extra[28:29] + extra[29:30]
            totals.append(jnp.concatenate(line, axis=1))
        wnorm = jnp.sqrt(norm[:, 0:1])
        gnorm = jnp.sqrt(square[:, 0:1])
        rate = learn_rate * (trust_coef * wnorm / (gnorm + weight_decay * wnorm))
        stores = []
        for x in range(N_X):
            tiles = [part[x, 512:1024, :].astype(f32).reshape(N_Y, N_Z, 8, 128) for part in parts]
            rows = slice(128 * x, 128 * x + 128)
            h, strip = x // 2, x % 2 * 2
            for z in range(N_Z):
                columns = slice(128 * z, 128 * z + 128)
                even, odd = [tile[:, z] for tile in tiles]
                top = jnp.concatenate([even[:, :, :64], odd[:, :, :64]], axis=2)
                bottom = jnp.concatenate([even[:, :, 64:], odd[:, :, 64:]], axis=2)
                decayed = jnp.stack([top, bottom], axis=1).reshape(128, 128)
                lines = slice(64 * z, 64 * z + 64)
                step = jnp.concatenate([parts[h][strip, lines, :], parts[h][strip + 1, lines, :]], axis=0).astype(f32)
                step += weight_decay * w_ref[rows, columns].astype(f32)
                new_w[rows, columns] = (decayed - rate * step).astype(bf16)
            stores.append(pltpu.make_async_copy(new_w.at[rows], new_w_hbm.at[rows], sems.at[x]))
            stores[-1].start()
        bn_grad = jnp.concatenate([totals[1], totals[0]], axis=0) * (1.0 / BATCH)
        new_bnv = momentum * bnv_ref[...] + learn_rate * bn_grad
        new_bnv_ref[...] = new_bnv
        new_bn_ref[...] = bn_ref[...] - new_bnv
        for h in range(2):

            @pl.when(row // 16 == h)
            def _():
                start = pl.multiple_of(layer * 64 + row % 4 * 16, 16)
                pair = parts[h][row % 16 // 4, pl.ds(start, 16), :].astype(f32)
                own = jnp.where(core == 0, pair[:, :64], pair[:, 64:])
                new_vel = momentum * vel_ref[...] + rate * (own + weight_decay * master_ref[...])
                new_vel_ref[...] = new_vel
                new_master_ref[...] = master_ref[...] - new_vel

        for copy in stores:
            copy.wait()

    @pl.when(core == 0)
    def _():
        run((mine_ref, other_ref))

    @pl.when(core == 1)
    def _():
        run((other_ref, mine_ref))


def shape(dims, kind):
    return jax.ShapeDtypeStruct(dims, kind)


VMEM = pl.BlockSpec(memory_space=pltpu.VMEM)
HBM = pl.BlockSpec(memory_space=pltpu.HBM)


def body(activations, pre_activation, pooled_grad, weights, master, velocity, bn_params, bn_velocity):
    msg = pl.pallas_call(
        stats_kernel,
        out_shape=shape((STAT_ROWS, 128), f32),
        in_specs=[HBM] * 4,
        out_specs=VMEM,
        scratch_shapes=[
            pltpu.VMEM((IMG, PIX, CIN), bf16),
            pltpu.VMEM((IMG, PIX, COUT), bf16),
            pltpu.VMEM((IMG, COUT), f32),
            pltpu.VMEM((CIN, COUT), bf16),
            pltpu.VMEM((ROWS, CIN), bf16),
            pltpu.VMEM((ROWS, COUT), bf16),
            pltpu.SemaphoreType.DMA((4, PARTS)),
        ],
        compiler_params=params(60),
        name="conv_stats",
    )(activations, pre_activation, pooled_grad, weights)
    chip = pl.pallas_call(
        chip_kernel,
        out_shape=shape((N_Z, STAT_ROWS, 128), f32),
        in_specs=[VMEM],
        out_specs=VMEM,
        compiler_params=params(),
        name="chip_stats",
    )(lax.all_gather(msg, "core"))
    stats = lax.all_to_all(chip, "z", 0, 0)
    conv_grad, act, send, line = pl.pallas_call(
        grad_kernel,
        out_shape=(
            shape((ROWS, COUT), bf16),
            shape((ROWS, CIN), bf16),
            shape((HALF, COUT), bf16),
            shape((8, 128), f32),
        ),
        in_specs=[VMEM] * 6,
        out_specs=(VMEM,) * 4,
        scratch_shapes=[pltpu.VMEM((ROWS, COUT), bf16), pltpu.VMEM((16, 128), f32)],
        compiler_params=params(),
        name="conv_grad",
    )(stats, weights, activations, pre_activation, pooled_grad, bn_params)
    swap = [(0, 1), (1, 0)]
    got = lax.ppermute(send, "core", swap)
    keep = pl.pallas_call(
        keep_kernel,
        out_shape=shape((HALF, COUT), f32),
        in_specs=[VMEM] * 2,
        out_specs=VMEM,
        compiler_params=params(),
        cost_estimate=pl.CostEstimate(flops=2 * ROWS * HALF * COUT, bytes_accessed=4 << 20, transcendentals=0),
        name="keep_grad",
    )(act, conv_grad)
    input_grad = pl.pallas_call(
        back_kernel,
        out_shape=shape((IMG, PIX, CIN), bf16),
        in_specs=[VMEM] * 2,
        out_specs=VMEM,
        compiler_params=params(),
        cost_estimate=pl.CostEstimate(flops=2 * ROWS * CIN * COUT, bytes_accessed=4 << 20, transcendentals=0),
        name="input_grad",
    )(conv_grad, weights)
    halves = pl.pallas_call(
        pair_kernel,
        out_shape=shape((HALF, COUT), bf16),
        in_specs=[VMEM] * 2,
        out_specs=VMEM,
        compiler_params=params(),
        name="pair_sum",
    )(keep, got)
    arrived = lax.all_to_all(halves.reshape(N_X, HALF // N_X, COUT), "x", 0, 0)
    lines = pl.pallas_call(
        line_kernel,
        out_shape=shape((N_Y, N_Z, 8, 128), bf16),
        in_specs=[VMEM],
        out_specs=VMEM,
        compiler_params=params(),
        name="line_sum",
    )(arrived)
    arrived = lax.all_to_all(lines.reshape(N_Y * N_Z, 8, 128), PLANE, 0, 0)
    block = pl.pallas_call(
        block_kernel,
        out_shape=shape((N_Y * N_Z, SIDE_ROWS, 128), bf16),
        in_specs=[VMEM] * 4,
        out_specs=VMEM,
        compiler_params=params(),
        name="block_sum",
    )(arrived, line, master, velocity)
    wide = pl.pallas_call(
        plane_kernel,
        out_shape=shape((N_X, WIDE_ROWS, 128), bf16),
        in_specs=[VMEM],
        out_specs=VMEM,
        compiler_params=params(),
        name="plane_join",
    )(lax.all_to_all(block, PLANE, 0, 0))
    mine = lax.all_to_all(wide, "x", 0, 0)
    other = lax.ppermute(mine, "core", swap)
    new_master, new_velocity, new_weights, new_bn, new_bn_velocity = pl.pallas_call(
        update_kernel,
        out_shape=(
            shape((16, 64), f32),
            shape((16, 64), f32),
            shape((CIN, COUT), bf16),
            shape((2, COUT), f32),
            shape((2, COUT), f32),
        ),
        in_specs=[VMEM] * 7,
        out_specs=(VMEM, VMEM, HBM, VMEM, VMEM),
        scratch_shapes=[pltpu.VMEM((CIN, COUT), bf16), pltpu.SemaphoreType.DMA((N_X,))],
        compiler_params=params(),
        name="update",
    )(mine, other, weights, master, velocity, bn_params, bn_velocity)
    return input_grad, new_master, new_velocity, new_weights, new_bn, new_bn_velocity


def solution(mesh):
    fine = Mesh(mesh.devices.reshape(4, 8, 8, 2), ALL)
    block = P(("x", "y"), ("z", "core"))
    return jax.shard_map(
        body,
        mesh=fine,
        in_specs=(P(ALL, None, None), P(ALL, None, None), P(ALL, None), P(), block, block, P(), P()),
        out_specs=(P(ALL, None, None), block, block, P(), P(), P()),
        check_vma=False,
    )
```

```python
import jax
import jax.numpy as jnp
from jax import lax
from jax.experimental import pallas as pl
from jax.experimental.pallas import tpu as pltpu
from jax.sharding import Mesh, PartitionSpec as P

epsilon = 1e-05
trust_coef = 0.001
weight_decay = 0.0001
momentum = 0.9
learn_rate = 12.0

IMG, PIX, STRIDE = 12, 49, 64
CIN, COUT = 512, 1024
ROWS = IMG * STRIDE
HALF = CIN // 2
N_ROW, N_COL = 32, 16
N_X, N_Y, N_Z = 4, 8, 8
M = PIX * IMG * N_COL
BATCH = IMG * N_ROW * N_COL
CHUNKS = COUT // 128
PLANE, ALL = ("y", "z"), ("x", "y", "z", "core")
STAT_ROWS = 40
SIDE_ROWS = 24
WIDE_ROWS = 1056
PARTS = 2
STRIP = 512
bf16, f32 = jnp.bfloat16, jnp.float32


def params(megabytes=20):
    return pltpu.CompilerParams(vmem_limit_bytes=megabytes << 20)


def fold(line):
    return jnp.concatenate([line[:, 128 * k : 128 * k + 128] for k in range(line.shape[1] // 128)], axis=0)


def unfold(block):
    return jnp.concatenate([block[k : k + 1] for k in range(block.shape[0])], axis=1)


def split(line):
    high = line.astype(bf16).astype(f32)
    middle = (line - high).astype(bf16).astype(f32)
    return high, middle, line - high - middle


def rows_of(count, lines, dims):
    row = lax.broadcasted_iota(jnp.int32, dims, 0)
    block = jnp.zeros(dims, f32)
    for k in range(count):
        block = jnp.where(row == k, jnp.broadcast_to(lines[k], dims), block)
    return block


def stats_kernel(act_hbm, pre_hbm, pool_hbm, w_hbm, msg_ref, act, pre, pool, w, actp, conv, sem_in):
    step = IMG // PARTS
    loads = []
    for k in range(PARTS):
        part = pl.ds(step * k, step)
        strip = pl.ds(CIN // PARTS * k, CIN // PARTS)
        loads.append(pltpu.make_async_copy(w_hbm.at[strip], w.at[strip], sem_in.at[0, k]))
        loads.append(pltpu.make_async_copy(act_hbm.at[part], act.at[part], sem_in.at[1, k]))
    for copy in loads:
        copy.start()
    later = [pltpu.make_async_copy(pool_hbm, pool, sem_in.at[3, 0])]
    for k in range(PARTS):
        part = pl.ds(step * k, step)
        later.append(pltpu.make_async_copy(pre_hbm.at[part], pre.at[part], sem_in.at[2, k]))
    for copy in later:
        copy.start()
    actp[...] = jnp.zeros_like(actp)
    for copy in loads:
        copy.wait()
    for i in range(IMG):
        actp[STRIDE * i : STRIDE * i + PIX, :] = act[i]
    act_total = jnp.sum(actp[...].astype(f32), axis=0, keepdims=True)
    strips = [slice(STRIP * k, STRIP * k + STRIP) for k in range(COUT // STRIP)]
    lines = []
    for strip in strips:
        value = jnp.dot(actp[...], w[:, strip], preferred_element_type=f32).astype(bf16)
        conv[:, strip] = value
        value = value.astype(f32)
        total = jnp.sum(value, axis=0, keepdims=True)
        square = jnp.sum(value * value, axis=0, keepdims=True)
        lines.append([total, square])
    for copy in later:
        copy.wait()
    for k, strip in enumerate(strips):
        up = jnp.zeros((1, STRIP), f32)
        up_conv = jnp.zeros((1, STRIP), f32)
        for i in range(IMG):
            value = conv[STRIDE * i : STRIDE * i + STRIDE, strip].astype(f32)[:PIX]
            passed = pre[i, :, strip].astype(f32) > 0
            share = pool[i : i + 1, strip] / PIX
            up += share * jnp.sum(jnp.where(passed, 1.0, 0.0), axis=0, keepdims=True)
            up_conv += share * jnp.sum(jnp.where(passed, value, 0.0), axis=0, keepdims=True)
        lines[k] += [up, up_conv]
    sums = [fold(jnp.concatenate([line[q] for line in lines], axis=1)) for q in range(4)]
    msg = jnp.concatenate(sums + [fold(act_total), jnp.zeros((4, 128), f32)], axis=0)
    msg_ref[...] = msg


def chip_kernel(got_ref, out_ref):
    out_ref[...] = jnp.broadcast_to((got_ref[0] + got_ref[1])[None], out_ref.shape)


def grad_kernel(
    stat_ref, w_ref, act_ref, pre_ref, pool_ref, bn_ref, cg_ref, actp, send_ref, line_ref, conv_ref, lines
):
    core, layer = core_of(), lax.axis_index("z").astype(jnp.int32)
    sums = jnp.sum(stat_ref[...], axis=0)
    sum_up = sums[16:24]
    act_mean = (unfold(sums[32:36]) / M).astype(bf16).astype(f32)
    mean = sums[0:8] / M
    variance = sums[8:16] / M - mean * mean
    rstd = lax.rsqrt(variance + epsilon)
    sum_upx = rstd * (sums[24:32] - mean * sum_up)
    lines[0:8, :] = sum_up
    lines[8:16, :] = sum_upx
    line_ref[...] = jnp.broadcast_to(lines[pl.ds(core * 8 + layer, 1), :], (8, 128))
    scale = fold(bn_ref[0:1, :]) * rstd
    shift = unfold(scale * (sum_up / M))
    slope = unfold(scale * (sum_upx / M) * rstd)
    mean = unfold(mean)
    scale = unfold(scale)
    actp[...] = jnp.zeros_like(actp)
    for i in range(IMG):
        actp[STRIDE * i : STRIDE * i + PIX, :] = act_ref[i]
    conv_ref[...] = jnp.dot(actp[...], w_ref[...], preferred_element_type=f32).astype(bf16)
    cg_ref[...] = jnp.zeros_like(cg_ref)
    cg_total = jnp.zeros((1, COUT), f32)
    for i in range(IMG):
        conv = conv_ref[STRIDE * i : STRIDE * i + STRIDE, :].astype(f32)[:PIX]
        on = scale * (pool_ref[i : i + 1, :] / PIX) - shift
        low = (jnp.where(pre_ref[i].astype(f32) > 0, on, -shift) - slope * (conv - mean)).astype(bf16)
        cg_ref[STRIDE * i : STRIDE * i + PIX, :] = low
        cg_total += jnp.sum(low.astype(f32), axis=0, keepdims=True)
    edge = actp[48:64, :].astype(f32)
    row = lax.broadcasted_iota(jnp.int32, edge.shape, 0)
    actp[48:64, :] = jnp.where((row >= 1) & (row < 4), -act_mean, edge).astype(bf16)
    high, middle, rest = split(cg_total)
    edge = cg_ref[48:64, :].astype(f32)
    cg_ref[48:64, :] = (edge + rows_of(4, [jnp.zeros_like(high), high, middle, rest], edge.shape)).astype(bf16)
    send_ref[...] = half_grad(actp, cg_ref, 1 - core).astype(bf16)


def core_of():
    return lax.axis_index("core").astype(jnp.int32)


def half_grad(actp, cg_ref, half):
    columns = actp[:, pl.ds(pl.multiple_of(half * HALF, HALF), HALF)]
    return lax.dot_general(columns, cg_ref[...], (((0,), (0,)), ((), ())), preferred_element_type=f32)


def keep_kernel(actp, cg_ref, keep_ref):
    keep_ref[...] = half_grad(actp, cg_ref, core_of())


def back_kernel(cg_ref, w_ref, out_ref):
    back = lax.dot_general(cg_ref[...], w_ref[...], (((1,), (1,)), ((), ())), preferred_element_type=f32)
    for i in range(IMG):
        out_ref[i] = back[STRIDE * i : STRIDE * i + PIX].astype(bf16)


def pair_kernel(keep_ref, got_ref, out_ref):
    out_ref[...] = (keep_ref[...] + got_ref[...].astype(f32)).astype(bf16)


def line_kernel(got_ref, out_ref):
    total = jnp.sum(got_ref[...].astype(f32), axis=0).reshape(N_Z, 8, COUT)
    for y in range(N_Y):
        out_ref[y] = total[:, :, 128 * y : 128 * y + 128].astype(bf16)


def block_kernel(got_ref, line_ref, master_ref, vel_ref, out_ref):
    total = jnp.sum(got_ref[...].astype(f32), axis=0) * (1.0 / BATCH)
    master = master_ref[...]
    decayed = master - momentum * vel_ref[...]
    decayed = jnp.concatenate([decayed[:8], decayed[8:]], axis=1)
    norm = jnp.sum(jnp.sum(master * master, axis=1, keepdims=True), axis=0, keepdims=True)
    square = jnp.sum(jnp.sum(total * total, axis=1, keepdims=True), axis=0, keepdims=True)
    norms = split(jnp.broadcast_to(norm, (8, 128))) + split(jnp.broadcast_to(square, (8, 128)))[:2]
    extra = rows_of(8, split(line_ref[...]) + norms, (8, 128))
    block = jnp.concatenate([total, decayed, extra], axis=0).astype(bf16)
    out_ref[...] = jnp.broadcast_to(block[None], out_ref.shape)


def plane_kernel(got_ref, out_ref):
    got = got_ref[...].astype(f32)
    extra = jnp.sum(got[:, 16:24, :].reshape(N_Y, N_Z, 8, 128), axis=0)
    lines = []
    norm = jnp.zeros((1, 128), f32)
    square = jnp.zeros((1, 128), f32)
    for z in range(N_Z):
        lines += split(extra[z, 0:1] + extra[z, 1:2] + extra[z, 2:3])
        norm += extra[z, 3:4] + extra[z, 4:5] + extra[z, 5:6]
        square += extra[z, 6:7] + extra[z, 7:8]
    lines += split(norm) + split(square)
    extra = jnp.concatenate(lines + [jnp.zeros((2, 128), f32)], axis=0).astype(bf16)
    grad = got[:, 0:8, :].reshape(512, 128).astype(bf16)
    decayed = got[:, 8:16, :].reshape(512, 128).astype(bf16)
    for p in range(N_X):
        out_ref[p, 0:512, :] = grad
        out_ref[p, 512:1024, :] = decayed
        out_ref[p, 1024:1056, :] = extra


def update_kernel(
    mine_ref, other_ref, w_ref, master_ref, vel_ref, bn_ref, bnv_ref,
    new_master_ref, new_vel_ref, new_w_hbm, new_bn_ref, new_bnv_ref, new_w, sems,
):
    core, layer = core_of(), lax.axis_index("z").astype(jnp.int32)
    row = (lax.axis_index("x") * N_Y + lax.axis_index("y")).astype(jnp.int32)

    def run(parts):
        square = jnp.zeros((1, 128), f32)
        norm = jnp.zeros((1, 128), f32)
        totals = []
        for part in parts:
            extra = jnp.zeros((32, 128), f32)
            for x in range(N_X):
                extra += part[x, 1024:1056, :].astype(f32)
            line = [extra[3 * z : 3 * z + 1] + extra[3 * z + 1 : 3 * z + 2] + extra[3 * z + 2 : 3 * z + 3] for z in range(N_Z)]
            norm += extra[24:25] + extra[25:26] + extra[26:27]
            square += extra[27:28] + extra[28:29] + extra[29:30]
            totals.append(jnp.concatenate(line, axis=1))
        wnorm = jnp.sqrt(norm[:, 0:1])
        gnorm = jnp.sqrt(square[:, 0:1])
        rate = learn_rate * (trust_coef * wnorm / (gnorm + weight_decay * wnorm))
        stores = []
        for x in range(N_X):
            tiles = [part[x, 512:1024, :].astype(f32).reshape(N_Y, N_Z, 8, 128) for part in parts]
            rows = slice(128 * x, 128 * x + 128)
            h, strip = x // 2, x % 2 * 2
            for z in range(N_Z):
                columns = slice(128 * z, 128 * z + 128)
                even, odd = [tile[:, z] for tile in tiles]
                top = jnp.concatenate([even[:, :, :64], odd[:, :, :64]], axis=2)
                bottom = jnp.concatenate([even[:, :, 64:], odd[:, :, 64:]], axis=2)
                decayed = jnp.stack([top, bottom], axis=1).reshape(128, 128)
                lines = slice(64 * z, 64 * z + 64)
                step = jnp.concatenate([parts[h][strip, lines, :], parts[h][strip + 1, lines, :]], axis=0).astype(f32)
                step += weight_decay * w_ref[rows, columns].astype(f32)
                new_w[rows, columns] = (decayed - rate * step).astype(bf16)
            stores.append(pltpu.make_async_copy(new_w.at[rows], new_w_hbm.at[rows], sems.at[x]))
            stores[-1].start()
        bn_grad = jnp.concatenate([totals[1], totals[0]], axis=0) * (1.0 / BATCH)
        new_bnv = momentum * bnv_ref[...] + learn_rate * bn_grad
        new_bnv_ref[...] = new_bnv
        new_bn_ref[...] = bn_ref[...] - new_bnv
        for h in range(2):

            @pl.when(row // 16 == h)
            def _():
                start = pl.multiple_of(layer * 64 + row % 4 * 16, 16)
                pair = parts[h][row % 16 // 4, pl.ds(start, 16), :].astype(f32)
                own = jnp.where(core == 0, pair[:, :64], pair[:, 64:])
                new_vel = momentum * vel_ref[...] + rate * (own + weight_decay * master_ref[...])
                new_vel_ref[...] = new_vel
                new_master_ref[...] = master_ref[...] - new_vel

        for copy in stores:
            copy.wait()

    @pl.when(core == 0)
    def _():
        run((mine_ref, other_ref))

    @pl.when(core == 1)
    def _():
        run((other_ref, mine_ref))


def shape(dims, kind):
    return jax.ShapeDtypeStruct(dims, kind)


VMEM = pl.BlockSpec(memory_space=pltpu.VMEM)
HBM = pl.BlockSpec(memory_space=pltpu.HBM)


def body(activations, pre_activation, pooled_grad, weights, master, velocity, bn_params, bn_velocity):
    msg = pl.pallas_call(
        stats_kernel,
        out_shape=shape((STAT_ROWS, 128), f32),
        in_specs=[HBM] * 4,
        out_specs=VMEM,
        scratch_shapes=[
            pltpu.VMEM((IMG, PIX, CIN), bf16),
            pltpu.VMEM((IMG, PIX, COUT), bf16),
            pltpu.VMEM((IMG, COUT), f32),
            pltpu.VMEM((CIN, COUT), bf16),
            pltpu.VMEM((ROWS, CIN), bf16),
            pltpu.VMEM((ROWS, COUT), bf16),
            pltpu.SemaphoreType.DMA((4, PARTS)),
        ],
        compiler_params=params(60),
        name="conv_stats",
    )(activations, pre_activation, pooled_grad, weights)
    chip = pl.pallas_call(
        chip_kernel,
        out_shape=shape((N_Z, STAT_ROWS, 128), f32),
        in_specs=[VMEM],
        out_specs=VMEM,
        compiler_params=params(),
        name="chip_stats",
    )(lax.all_gather(msg, "core"))
    stats = lax.all_to_all(chip, "z", 0, 0)
    conv_grad, act, send, line = pl.pallas_call(
        grad_kernel,
        out_shape=(
            shape((ROWS, COUT), bf16),
            shape((ROWS, CIN), bf16),
            shape((HALF, COUT), bf16),
            shape((8, 128), f32),
        ),
        in_specs=[VMEM] * 6,
        out_specs=(VMEM,) * 4,
        scratch_shapes=[pltpu.VMEM((ROWS, COUT), bf16), pltpu.VMEM((16, 128), f32)],
        compiler_params=params(),
        name="conv_grad",
    )(stats, weights, activations, pre_activation, pooled_grad, bn_params)
    swap = [(0, 1), (1, 0)]
    got = lax.ppermute(send, "core", swap)
    keep = pl.pallas_call(
        keep_kernel,
        out_shape=shape((HALF, COUT), f32),
        in_specs=[VMEM] * 2,
        out_specs=VMEM,
        compiler_params=params(),
        cost_estimate=pl.CostEstimate(flops=2 * ROWS * HALF * COUT, bytes_accessed=4 << 20, transcendentals=0),
        name="keep_grad",
    )(act, conv_grad)
    input_grad = pl.pallas_call(
        back_kernel,
        out_shape=shape((IMG, PIX, CIN), bf16),
        in_specs=[VMEM] * 2,
        out_specs=VMEM,
        compiler_params=params(),
        cost_estimate=pl.CostEstimate(flops=2 * ROWS * CIN * COUT, bytes_accessed=4 << 20, transcendentals=0),
        name="input_grad",
    )(conv_grad, weights)
    halves = pl.pallas_call(
        pair_kernel,
        out_shape=shape((HALF, COUT), bf16),
        in_specs=[VMEM] * 2,
        out_specs=VMEM,
        compiler_params=params(),
        name="pair_sum",
    )(keep, got)
    arrived = lax.all_to_all(halves.reshape(N_X, HALF // N_X, COUT), "x", 0, 0)
    lines = pl.pallas_call(
        line_kernel,
        out_shape=shape((N_Y, N_Z, 8, 128), bf16),
        in_specs=[VMEM],
        out_specs=VMEM,
        compiler_params=params(),
        name="line_sum",
    )(arrived)
    arrived = lax.all_to_all(lines.reshape(N_Y * N_Z, 8, 128), PLANE, 0, 0)
    block = pl.pallas_call(
        block_kernel,
        out_shape=shape((N_Y * N_Z, SIDE_ROWS, 128), bf16),
        in_specs=[VMEM] * 4,
        out_specs=VMEM,
        compiler_params=params(),
        name="block_sum",
    )(arrived, line, master, velocity)
    wide = pl.pallas_call(
        plane_kernel,
        out_shape=shape((N_X, WIDE_ROWS, 128), bf16),
        in_specs=[VMEM],
        out_specs=VMEM,
        compiler_params=params(),
        name="plane_join",
    )(lax.all_to_all(block, PLANE, 0, 0))
    mine = lax.all_to_all(wide, "x", 0, 0)
    other = lax.ppermute(mine, "core", swap)
    new_master, new_velocity, new_weights, new_bn, new_bn_velocity = pl.pallas_call(
        update_kernel,
        out_shape=(
            shape((16, 64), f32),
            shape((16, 64), f32),
            shape((CIN, COUT), bf16),
            shape((2, COUT), f32),
            shape((2, COUT), f32),
        ),
        in_specs=[VMEM] * 7,
        out_specs=(VMEM, VMEM, HBM, VMEM, VMEM),
        scratch_shapes=[pltpu.VMEM((CIN, COUT), bf16), pltpu.SemaphoreType.DMA((N_X,))],
        compiler_params=params(),
        name="update",
    )(mine, other, weights, master, velocity, bn_params, bn_velocity)
    return input_grad, new_master, new_velocity, new_weights, new_bn, new_bn_velocity


def solution(mesh):
    fine = Mesh(mesh.devices.reshape(4, 8, 8, 2), ALL)
    block = P(("x", "y"), ("z", "core"))
    return jax.shard_map(
        body,
        mesh=fine,
        in_specs=(P(ALL, None, None), P(ALL, None, None), P(ALL, None), P(), block, block, P(), P()),
        out_specs=(P(ALL, None, None), block, block, P(), P(), P()),
        check_vma=False,
    )
```

```python
import jax
import jax.numpy as jnp
from jax import lax
from jax.experimental import pallas as pl
from jax.experimental.pallas import tpu as pltpu
from jax.sharding import Mesh, PartitionSpec as P

epsilon = 1e-05
trust_coef = 0.001
weight_decay = 0.0001
momentum = 0.9
learn_rate = 12.0

IMG, PIX, STRIDE = 12, 49, 64
CIN, COUT = 512, 1024
ROWS = IMG * STRIDE
HALF = CIN // 2
N_ROW, N_COL = 32, 16
N_X, N_Y, N_Z = 4, 8, 8
M = PIX * IMG * N_COL
BATCH = IMG * N_ROW * N_COL
CHUNKS = COUT // 128
PLANE, ALL = ("y", "z"), ("x", "y", "z", "core")
STAT_ROWS = 40
SIDE_ROWS = 24
WIDE_ROWS = 1056
PARTS = 2
STRIP = 512
bf16, f32 = jnp.bfloat16, jnp.float32


def params(megabytes=20):
    return pltpu.CompilerParams(vmem_limit_bytes=megabytes << 20)


def fold(line):
    return jnp.concatenate([line[:, 128 * k : 128 * k + 128] for k in range(line.shape[1] // 128)], axis=0)


def unfold(block):
    return jnp.concatenate([block[k : k + 1] for k in range(block.shape[0])], axis=1)


def split(line):
    high = line.astype(bf16).astype(f32)
    middle = (line - high).astype(bf16).astype(f32)
    return high, middle, line - high - middle


def rows_of(count, lines, dims):
    row = lax.broadcasted_iota(jnp.int32, dims, 0)
    block = jnp.zeros(dims, f32)
    for k in range(count):
        block = jnp.where(row == k, jnp.broadcast_to(lines[k], dims), block)
    return block


def stats_kernel(act_hbm, pre_hbm, pool_hbm, w_hbm, msg_ref, act, pre, pool, w, actp, conv, sem_in):
    step = IMG // PARTS
    loads = []
    for k in range(PARTS):
        part = pl.ds(step * k, step)
        strip = pl.ds(CIN // PARTS * k, CIN // PARTS)
        loads.append(pltpu.make_async_copy(w_hbm.at[strip], w.at[strip], sem_in.at[0, k]))
        loads.append(pltpu.make_async_copy(act_hbm.at[part], act.at[part], sem_in.at[1, k]))
    for copy in loads:
        copy.start()
    later = [pltpu.make_async_copy(pool_hbm, pool, sem_in.at[3, 0])]
    for k in range(PARTS):
        part = pl.ds(step * k, step)
        later.append(pltpu.make_async_copy(pre_hbm.at[part], pre.at[part], sem_in.at[2, k]))
    for copy in later:
        copy.start()
    actp[...] = jnp.zeros_like(actp)
    for copy in loads:
        copy.wait()
    for i in range(IMG):
        actp[STRIDE * i : STRIDE * i + PIX, :] = act[i]
    act_total = jnp.sum(actp[...].astype(f32), axis=0, keepdims=True)
    strips = [slice(STRIP * k, STRIP * k + STRIP) for k in range(COUT // STRIP)]
    lines = []
    for strip in strips:
        value = jnp.dot(actp[...], w[:, strip], preferred_element_type=f32).astype(bf16)
        conv[:, strip] = value
        value = value.astype(f32)
        total = jnp.sum(value, axis=0, keepdims=True)
        square = jnp.sum(value * value, axis=0, keepdims=True)
        lines.append([total, square])
    for copy in later:
        copy.wait()
    for k, strip in enumerate(strips):
        up = jnp.zeros((1, STRIP), f32)
        up_conv = jnp.zeros((1, STRIP), f32)
        for i in range(IMG):
            value = conv[STRIDE * i : STRIDE * i + STRIDE, strip].astype(f32)[:PIX]
            passed = pre[i, :, strip].astype(f32) > 0
            share = pool[i : i + 1, strip] / PIX
            up += share * jnp.sum(jnp.where(passed, 1.0, 0.0), axis=0, keepdims=True)
            up_conv += share * jnp.sum(jnp.where(passed, value, 0.0), axis=0, keepdims=True)
        lines[k] += [up, up_conv]
    sums = [fold(jnp.concatenate([line[q] for line in lines], axis=1)) for q in range(4)]
    msg = jnp.concatenate(sums + [fold(act_total), jnp.zeros((4, 128), f32)], axis=0)
    msg_ref[...] = msg


def chip_kernel(got_ref, out_ref):
    out_ref[...] = jnp.broadcast_to((got_ref[0] + got_ref[1])[None], out_ref.shape)


def grad_kernel(
    stat_ref, w_ref, act_ref, pre_ref, pool_ref, bn_ref, cg_ref, actp, send_ref, line_ref, conv_ref, lines
):
    core, layer = core_of(), lax.axis_index("z").astype(jnp.int32)
    sums = jnp.sum(stat_ref[...], axis=0)
    sum_up = sums[16:24]
    act_mean = (unfold(sums[32:36]) / M).astype(bf16).astype(f32)
    mean = sums[0:8] / M
    variance = sums[8:16] / M - mean * mean
    rstd = lax.rsqrt(variance + epsilon)
    sum_upx = rstd * (sums[24:32] - mean * sum_up)
    lines[0:8, :] = sum_up
    lines[8:16, :] = sum_upx
    line_ref[...] = jnp.broadcast_to(lines[pl.ds(core * 8 + layer, 1), :], (8, 128))
    scale = fold(bn_ref[0:1, :]) * rstd
    shift = unfold(scale * (sum_up / M))
    slope = unfold(scale * (sum_upx / M) * rstd)
    mean = unfold(mean)
    scale = unfold(scale)
    actp[...] = jnp.zeros_like(actp)
    for i in range(IMG):
        actp[STRIDE * i : STRIDE * i + PIX, :] = act_ref[i]
    conv_ref[...] = jnp.dot(actp[...], w_ref[...], preferred_element_type=f32).astype(bf16)
    cg_ref[...] = jnp.zeros_like(cg_ref)
    cg_total = jnp.zeros((1, COUT), f32)
    for i in range(IMG):
        conv = conv_ref[STRIDE * i : STRIDE * i + STRIDE, :].astype(f32)[:PIX]
        on = scale * (pool_ref[i : i + 1, :] / PIX) - shift
        low = (jnp.where(pre_ref[i].astype(f32) > 0, on, -shift) - slope * (conv - mean)).astype(bf16)
        cg_ref[STRIDE * i : STRIDE * i + PIX, :] = low
        cg_total += jnp.sum(low.astype(f32), axis=0, keepdims=True)
    edge = actp[48:64, :].astype(f32)
    row = lax.broadcasted_iota(jnp.int32, edge.shape, 0)
    actp[48:64, :] = jnp.where((row >= 1) & (row < 4), -act_mean, edge).astype(bf16)
    high, middle, rest = split(cg_total)
    edge = cg_ref[48:64, :].astype(f32)
    cg_ref[48:64, :] = (edge + rows_of(4, [jnp.zeros_like(high), high, middle, rest], edge.shape)).astype(bf16)
    send_ref[...] = half_grad(actp, cg_ref, 1 - core).astype(bf16)


def core_of():
    return lax.axis_index("core").astype(jnp.int32)


def half_grad(actp, cg_ref, half):
    columns = actp[:, pl.ds(pl.multiple_of(half * HALF, HALF), HALF)]
    return lax.dot_general(columns, cg_ref[...], (((0,), (0,)), ((), ())), preferred_element_type=f32)


def keep_kernel(actp, cg_ref, keep_ref):
    keep_ref[...] = half_grad(actp, cg_ref, core_of())


def back_kernel(cg_ref, w_ref, out_ref):
    back = lax.dot_general(cg_ref[...], w_ref[...], (((1,), (1,)), ((), ())), preferred_element_type=f32)
    for i in range(IMG):
        out_ref[i] = back[STRIDE * i : STRIDE * i + PIX].astype(bf16)


def pair_kernel(keep_ref, got_ref, out_ref):
    out_ref[...] = (keep_ref[...] + got_ref[...].astype(f32)).astype(bf16)


def line_kernel(got_ref, out_ref):
    total = jnp.sum(got_ref[...].astype(f32), axis=0).reshape(N_Z, 8, COUT)
    for y in range(N_Y):
        out_ref[y] = total[:, :, 128 * y : 128 * y + 128].astype(bf16)


def block_kernel(got_ref, line_ref, master_ref, vel_ref, out_ref):
    total = jnp.sum(got_ref[...].astype(f32), axis=0) * (1.0 / BATCH)
    master = master_ref[...]
    decayed = master - momentum * vel_ref[...]
    decayed = jnp.concatenate([decayed[:8], decayed[8:]], axis=1)
    norm = jnp.sum(jnp.sum(master * master, axis=1, keepdims=True), axis=0, keepdims=True)
    square = jnp.sum(jnp.sum(total * total, axis=1, keepdims=True), axis=0, keepdims=True)
    norms = split(jnp.broadcast_to(norm, (8, 128))) + split(jnp.broadcast_to(square, (8, 128)))[:2]
    extra = rows_of(8, split(line_ref[...]) + norms, (8, 128))
    block = jnp.concatenate([total, decayed, extra], axis=0).astype(bf16)
    out_ref[...] = jnp.broadcast_to(block[None], out_ref.shape)


def plane_kernel(got_ref, out_ref):
    got = got_ref[...].astype(f32)
    extra = jnp.sum(got[:, 16:24, :].reshape(N_Y, N_Z, 8, 128), axis=0)
    lines = []
    norm = jnp.zeros((1, 128), f32)
    square = jnp.zeros((1, 128), f32)
    for z in range(N_Z):
        lines += split(extra[z, 0:1] + extra[z, 1:2] + extra[z, 2:3])
        norm += extra[z, 3:4] + extra[z, 4:5] + extra[z, 5:6]
        square += extra[z, 6:7] + extra[z, 7:8]
    lines += split(norm) + split(square)
    extra = jnp.concatenate(lines + [jnp.zeros((2, 128), f32)], axis=0).astype(bf16)
    grad = got[:, 0:8, :].reshape(512, 128).astype(bf16)
    decayed = got[:, 8:16, :].reshape(512, 128).astype(bf16)
    for p in range(N_X):
        out_ref[p, 0:512, :] = grad
        out_ref[p, 512:1024, :] = decayed
        out_ref[p, 1024:1056, :] = extra


def update_kernel(
    mine_ref, other_ref, w_ref, master_ref, vel_ref, bn_ref, bnv_ref,
    new_master_hbm, new_vel_hbm, new_w_hbm, new_bn_hbm, new_bnv_hbm,
    new_master_ref, new_vel_ref, new_w, new_bn_ref, new_bnv_ref, sems, small_sems,
):
    core, layer = core_of(), lax.axis_index("z").astype(jnp.int32)
    row = (lax.axis_index("x") * N_Y + lax.axis_index("y")).astype(jnp.int32)

    def run(parts):
        square = jnp.zeros((1, 128), f32)
        norm = jnp.zeros((1, 128), f32)
        totals = []
        for part in parts:
            extra = jnp.zeros((32, 128), f32)
            for x in range(N_X):
                extra += part[x, 1024:1056, :].astype(f32)
            line = [extra[3 * z : 3 * z + 1] + extra[3 * z + 1 : 3 * z + 2] + extra[3 * z + 2 : 3 * z + 3] for z in range(N_Z)]
            norm += extra[24:25] + extra[25:26] + extra[26:27]
            square += extra[27:28] + extra[28:29] + extra[29:30]
            totals.append(jnp.concatenate(line, axis=1))
        wnorm = jnp.sqrt(norm[:, 0:1])
        gnorm = jnp.sqrt(square[:, 0:1])
        rate = learn_rate * (trust_coef * wnorm / (gnorm + weight_decay * wnorm))
        bn_grad = jnp.concatenate([totals[1], totals[0]], axis=0) * (1.0 / BATCH)
        new_bnv = momentum * bnv_ref[...] + learn_rate * bn_grad
        new_bnv_ref[...] = new_bnv
        new_bn_ref[...] = bn_ref[...] - new_bnv
        for h in range(2):

            @pl.when(row // 16 == h)
            def _():
                start = pl.multiple_of(layer * 64 + row % 4 * 16, 16)
                pair = parts[h][row % 16 // 4, pl.ds(start, 16), :].astype(f32)
                own = jnp.where(core == 0, pair[:, :64], pair[:, 64:])
                new_vel = momentum * vel_ref[...] + rate * (own + weight_decay * master_ref[...])
                new_vel_ref[...] = new_vel
                new_master_ref[...] = master_ref[...] - new_vel

        small_pairs = (
            (new_master_ref, new_master_hbm),
            (new_vel_ref, new_vel_hbm),
            (new_bn_ref, new_bn_hbm),
            (new_bnv_ref, new_bnv_hbm),
        )
        stores = [pltpu.make_async_copy(here, there, small_sems.at[k]) for k, (here, there) in enumerate(small_pairs)]
        for copy in stores:
            copy.start()
        for x in range(N_X):
            tiles = [part[x, 512:1024, :].astype(f32).reshape(N_Y, N_Z, 8, 128) for part in parts]
            rows = slice(128 * x, 128 * x + 128)
            h, strip = x // 2, x % 2 * 2
            for z in range(N_Z):
                columns = slice(128 * z, 128 * z + 128)
                even, odd = [tile[:, z] for tile in tiles]
                top = jnp.concatenate([even[:, :, :64], odd[:, :, :64]], axis=2)
                bottom = jnp.concatenate([even[:, :, 64:], odd[:, :, 64:]], axis=2)
                decayed = jnp.stack([top, bottom], axis=1).reshape(128, 128)
                lines = slice(64 * z, 64 * z + 64)
                step = jnp.concatenate([parts[h][strip, lines, :], parts[h][strip + 1, lines, :]], axis=0).astype(f32)
                step += weight_decay * w_ref[rows, columns].astype(f32)
                new_w[rows, columns] = (decayed - rate * step).astype(bf16)
            stores.append(pltpu.make_async_copy(new_w.at[rows], new_w_hbm.at[rows], sems.at[x]))
            stores[-1].start()
        for copy in stores:
            copy.wait()

    @pl.when(core == 0)
    def _():
        run((mine_ref, other_ref))

    @pl.when(core == 1)
    def _():
        run((other_ref, mine_ref))


def shape(dims, kind):
    return jax.ShapeDtypeStruct(dims, kind)


VMEM = pl.BlockSpec(memory_space=pltpu.VMEM)
HBM = pl.BlockSpec(memory_space=pltpu.HBM)


def body(activations, pre_activation, pooled_grad, weights, master, velocity, bn_params, bn_velocity):
    msg = pl.pallas_call(
        stats_kernel,
        out_shape=pltpu.VMEM((STAT_ROWS, 128), f32),
        in_specs=[HBM] * 4,
        out_specs=VMEM,
        scratch_shapes=[
            pltpu.VMEM((IMG, PIX, CIN), bf16),
            pltpu.VMEM((IMG, PIX, COUT), bf16),
            pltpu.VMEM((IMG, COUT), f32),
            pltpu.VMEM((CIN, COUT), bf16),
            pltpu.VMEM((ROWS, CIN), bf16),
            pltpu.VMEM((ROWS, COUT), bf16),
            pltpu.SemaphoreType.DMA((4, PARTS)),
        ],
        compiler_params=params(60),
        name="conv_stats",
    )(activations, pre_activation, pooled_grad, weights)
    chip = pl.pallas_call(
        chip_kernel,
        out_shape=shape((N_Z, STAT_ROWS, 128), f32),
        in_specs=[VMEM],
        out_specs=VMEM,
        compiler_params=params(),
        name="chip_stats",
    )(lax.all_gather(msg, "core"))
    stats = lax.all_to_all(chip, "z", 0, 0)
    conv_grad, act, send, line = pl.pallas_call(
        grad_kernel,
        out_shape=(
            shape((ROWS, COUT), bf16),
            shape((ROWS, CIN), bf16),
            shape((HALF, COUT), bf16),
            shape((8, 128), f32),
        ),
        in_specs=[VMEM] * 6,
        out_specs=(VMEM,) * 4,
        scratch_shapes=[pltpu.VMEM((ROWS, COUT), bf16), pltpu.VMEM((16, 128), f32)],
        compiler_params=params(),
        name="conv_grad",
    )(stats, weights, activations, pre_activation, pooled_grad, bn_params)
    swap = [(0, 1), (1, 0)]
    got = lax.ppermute(send, "core", swap)
    keep = pl.pallas_call(
        keep_kernel,
        out_shape=shape((HALF, COUT), f32),
        in_specs=[VMEM] * 2,
        out_specs=VMEM,
        compiler_params=params(),
        cost_estimate=pl.CostEstimate(flops=2 * ROWS * HALF * COUT, bytes_accessed=4 << 20, transcendentals=0),
        name="keep_grad",
    )(act, conv_grad)
    input_grad = pl.pallas_call(
        back_kernel,
        out_shape=shape((IMG, PIX, CIN), bf16),
        in_specs=[VMEM] * 2,
        out_specs=VMEM,
        compiler_params=params(),
        cost_estimate=pl.CostEstimate(flops=2 * ROWS * CIN * COUT, bytes_accessed=4 << 20, transcendentals=0),
        name="input_grad",
    )(conv_grad, weights)
    halves = pl.pallas_call(
        pair_kernel,
        out_shape=shape((HALF, COUT), bf16),
        in_specs=[VMEM] * 2,
        out_specs=VMEM,
        compiler_params=params(),
        name="pair_sum",
    )(keep, got)
    arrived = lax.all_to_all(halves.reshape(N_X, HALF // N_X, COUT), "x", 0, 0)
    lines = pl.pallas_call(
        line_kernel,
        out_shape=shape((N_Y, N_Z, 8, 128), bf16),
        in_specs=[VMEM],
        out_specs=VMEM,
        compiler_params=params(),
        name="line_sum",
    )(arrived)
    arrived = lax.all_to_all(lines.reshape(N_Y * N_Z, 8, 128), PLANE, 0, 0)
    block = pl.pallas_call(
        block_kernel,
        out_shape=shape((N_Y * N_Z, SIDE_ROWS, 128), bf16),
        in_specs=[VMEM] * 4,
        out_specs=VMEM,
        compiler_params=params(),
        name="block_sum",
    )(arrived, line, master, velocity)
    wide = pl.pallas_call(
        plane_kernel,
        out_shape=shape((N_X, WIDE_ROWS, 128), bf16),
        in_specs=[VMEM],
        out_specs=VMEM,
        compiler_params=params(),
        name="plane_join",
    )(lax.all_to_all(block, PLANE, 0, 0))
    mine = lax.all_to_all(wide, "x", 0, 0)
    other = lax.ppermute(mine, "core", swap)
    new_master, new_velocity, new_weights, new_bn, new_bn_velocity = pl.pallas_call(
        update_kernel,
        out_shape=(
            shape((16, 64), f32),
            shape((16, 64), f32),
            shape((CIN, COUT), bf16),
            shape((2, COUT), f32),
            shape((2, COUT), f32),
        ),
        in_specs=[VMEM] * 7,
        out_specs=(HBM,) * 5,
        scratch_shapes=[
            pltpu.VMEM((16, 64), f32),
            pltpu.VMEM((16, 64), f32),
            pltpu.VMEM((CIN, COUT), bf16),
            pltpu.VMEM((2, COUT), f32),
            pltpu.VMEM((2, COUT), f32),
            pltpu.SemaphoreType.DMA((N_X,)),
            pltpu.SemaphoreType.DMA((4,)),
        ],
        compiler_params=params(),
        name="update",
    )(mine, other, weights, master, velocity, bn_params, bn_velocity)
    return input_grad, new_master, new_velocity, new_weights, new_bn, new_bn_velocity


def solution(mesh):
    fine = Mesh(mesh.devices.reshape(4, 8, 8, 2), ALL)
    block = P(("x", "y"), ("z", "core"))
    return jax.shard_map(
        body,
        mesh=fine,
        in_specs=(P(ALL, None, None), P(ALL, None, None), P(ALL, None), P(), block, block, P(), P()),
        out_specs=(P(ALL, None, None), block, block, P(), P(), P()),
        check_vma=False,
    )
```

```python
import jax
import jax.numpy as jnp
from jax import lax
from jax.experimental import pallas as pl
from jax.experimental.pallas import tpu as pltpu
from jax.sharding import Mesh, PartitionSpec as P

epsilon = 1e-05
trust_coef = 0.001
weight_decay = 0.0001
momentum = 0.9
learn_rate = 12.0

IMG, PIX, STRIDE = 12, 49, 64
CIN, COUT = 512, 1024
ROWS = IMG * STRIDE
HALF = CIN // 2
N_ROW, N_COL = 32, 16
N_X, N_Y, N_Z = 4, 8, 8
M = PIX * IMG * N_COL
BATCH = IMG * N_ROW * N_COL
CHUNKS = COUT // 128
PLANE, ALL = ("y", "z"), ("x", "y", "z", "core")
STAT_ROWS = 40
SIDE_ROWS = 24
WIDE_ROWS = 1056
PARTS = 2
STRIP = 512
bf16, f32 = jnp.bfloat16, jnp.float32


def params(megabytes=20):
    return pltpu.CompilerParams(vmem_limit_bytes=megabytes << 20)


def fold(line):
    return jnp.concatenate([line[:, 128 * k : 128 * k + 128] for k in range(line.shape[1] // 128)], axis=0)


def unfold(block):
    return jnp.concatenate([block[k : k + 1] for k in range(block.shape[0])], axis=1)


def split(line):
    high = line.astype(bf16).astype(f32)
    middle = (line - high).astype(bf16).astype(f32)
    return high, middle, line - high - middle


def rows_of(count, lines, dims):
    row = lax.broadcasted_iota(jnp.int32, dims, 0)
    block = jnp.zeros(dims, f32)
    for k in range(count):
        block = jnp.where(row == k, jnp.broadcast_to(lines[k], dims), block)
    return block


def stats_kernel(act_hbm, pre_hbm, pool_hbm, w_hbm, msg_ref, conv, actp, pre, pool, act, w, sem_in):
    step = IMG // PARTS
    loads = []
    for k in range(PARTS):
        part = pl.ds(step * k, step)
        strip = pl.ds(CIN // PARTS * k, CIN // PARTS)
        loads.append(pltpu.make_async_copy(w_hbm.at[strip], w.at[strip], sem_in.at[0, k]))
        loads.append(pltpu.make_async_copy(act_hbm.at[part], act.at[part], sem_in.at[1, k]))
    for copy in loads:
        copy.start()
    later = [pltpu.make_async_copy(pool_hbm, pool, sem_in.at[3, 0])]
    for k in range(PARTS):
        part = pl.ds(step * k, step)
        later.append(pltpu.make_async_copy(pre_hbm.at[part], pre.at[part], sem_in.at[2, k]))
    for copy in later:
        copy.start()
    actp[...] = jnp.zeros_like(actp)
    for copy in loads:
        copy.wait()
    for i in range(IMG):
        actp[STRIDE * i : STRIDE * i + PIX, :] = act[i]
    act_total = jnp.sum(actp[...].astype(f32), axis=0, keepdims=True)
    strips = [slice(STRIP * k, STRIP * k + STRIP) for k in range(COUT // STRIP)]
    lines = []
    for strip in strips:
        value = jnp.dot(actp[...], w[:, strip], preferred_element_type=f32).astype(bf16)
        conv[:, strip] = value
        value = value.astype(f32)
        total = jnp.sum(value, axis=0, keepdims=True)
        square = jnp.sum(value * value, axis=0, keepdims=True)
        lines.append([total, square])
    for copy in later:
        copy.wait()
    for k, strip in enumerate(strips):
        up = jnp.zeros((1, STRIP), f32)
        up_conv = jnp.zeros((1, STRIP), f32)
        for i in range(IMG):
            value = conv[STRIDE * i : STRIDE * i + STRIDE, strip].astype(f32)[:PIX]
            passed = pre[i, :, strip].astype(f32) > 0
            share = pool[i : i + 1, strip] / PIX
            up += share * jnp.sum(jnp.where(passed, 1.0, 0.0), axis=0, keepdims=True)
            up_conv += share * jnp.sum(jnp.where(passed, value, 0.0), axis=0, keepdims=True)
        lines[k] += [up, up_conv]
    sums = [fold(jnp.concatenate([line[q] for line in lines], axis=1)) for q in range(4)]
    msg = jnp.concatenate(sums + [fold(act_total), jnp.zeros((4, 128), f32)], axis=0)
    msg_ref[...] = msg


def chip_kernel(got_ref, out_ref):
    out_ref[...] = jnp.broadcast_to((got_ref[0] + got_ref[1])[None], out_ref.shape)


def grad_kernel(
    stat_ref, msg_ref, conv_ref, act_ref, pre_ref, pool_ref, bn_ref, cg_ref, actp, send_ref, line_ref, lines
):
    core, layer = core_of(), lax.axis_index("z").astype(jnp.int32)
    sums = jnp.sum(stat_ref[...], axis=0)
    sum_up = sums[16:24]
    act_mean = (unfold(sums[32:36]) / M).astype(bf16).astype(f32)
    mean = sums[0:8] / M
    variance = sums[8:16] / M - mean * mean
    rstd = lax.rsqrt(variance + epsilon)
    sum_upx = rstd * (sums[24:32] - mean * sum_up)
    lines[0:8, :] = sum_up
    lines[8:16, :] = sum_upx
    line_ref[...] = jnp.broadcast_to(lines[pl.ds(core * 8 + layer, 1), :], (8, 128))
    scale = fold(bn_ref[0:1, :]) * rstd
    shift = scale * (sum_up / M)
    slope = scale * (sum_upx / M) * rstd
    local = IMG * PIX
    cg_total = unfold(scale * msg_ref[16:24, :] - local * shift - slope * (msg_ref[0:8, :] - local * mean))
    mean, scale, shift, slope = unfold(mean), unfold(scale), unfold(shift), unfold(slope)
    actp[...] = act_ref[...]
    for i in range(IMG):
        cg_ref[STRIDE * i + 48 : STRIDE * i + 64, :] = jnp.zeros((16, COUT), bf16)
        conv = conv_ref[STRIDE * i : STRIDE * i + STRIDE, :].astype(f32)[:PIX]
        on = scale * (pool_ref[i : i + 1, :] / PIX) - shift
        cg = jnp.where(pre_ref[i].astype(f32) > 0, on, -shift) - slope * (conv - mean)
        cg_ref[STRIDE * i : STRIDE * i + PIX, :] = cg.astype(bf16)
    edge = actp[48:64, :].astype(f32)
    row = lax.broadcasted_iota(jnp.int32, edge.shape, 0)
    actp[48:64, :] = jnp.where((row >= 1) & (row < 4), -act_mean, edge).astype(bf16)
    high, middle, rest = split(cg_total)
    edge = cg_ref[48:64, :].astype(f32)
    cg_ref[48:64, :] = (edge + rows_of(4, [jnp.zeros_like(high), high, middle, rest], edge.shape)).astype(bf16)
    send_ref[...] = half_grad(actp, cg_ref, 1 - core).astype(bf16)


def core_of():
    return lax.axis_index("core").astype(jnp.int32)


def half_grad(actp, cg_ref, half):
    columns = actp[:, pl.ds(pl.multiple_of(half * HALF, HALF), HALF)]
    return lax.dot_general(columns, cg_ref[...], (((0,), (0,)), ((), ())), preferred_element_type=f32)


def keep_kernel(actp, cg_ref, keep_ref):
    keep_ref[...] = half_grad(actp, cg_ref, core_of())


def back_kernel(cg_ref, w_ref, out_ref):
    back = lax.dot_general(cg_ref[...], w_ref[...], (((1,), (1,)), ((), ())), preferred_element_type=f32)
    for i in range(IMG):
        out_ref[i] = back[STRIDE * i : STRIDE * i + PIX].astype(bf16)


def pair_kernel(keep_ref, got_ref, out_ref):
    out_ref[...] = (keep_ref[...] + got_ref[...].astype(f32)).astype(bf16)


def line_kernel(got_ref, out_ref):
    total = jnp.sum(got_ref[...].astype(f32), axis=0).reshape(N_Z, 8, COUT)
    for y in range(N_Y):
        out_ref[y] = total[:, :, 128 * y : 128 * y + 128].astype(bf16)


def block_kernel(got_ref, line_ref, master_ref, vel_ref, out_ref):
    total = jnp.sum(got_ref[...].astype(f32), axis=0) * (1.0 / BATCH)
    master = master_ref[...]
    decayed = master - momentum * vel_ref[...]
    decayed = jnp.concatenate([decayed[:8], decayed[8:]], axis=1)
    norm = jnp.sum(jnp.sum(master * master, axis=1, keepdims=True), axis=0, keepdims=True)
    square = jnp.sum(jnp.sum(total * total, axis=1, keepdims=True), axis=0, keepdims=True)
    norms = split(jnp.broadcast_to(norm, (8, 128))) + split(jnp.broadcast_to(square, (8, 128)))[:2]
    extra = rows_of(8, split(line_ref[...]) + norms, (8, 128))
    block = jnp.concatenate([total, decayed, extra], axis=0).astype(bf16)
    out_ref[...] = jnp.broadcast_to(block[None], out_ref.shape)


def plane_kernel(got_ref, out_ref):
    got = got_ref[...].astype(f32)
    extra = jnp.sum(got[:, 16:24, :].reshape(N_Y, N_Z, 8, 128), axis=0)
    lines = []
    norm = jnp.zeros((1, 128), f32)
    square = jnp.zeros((1, 128), f32)
    for z in range(N_Z):
        lines += split(extra[z, 0:1] + extra[z, 1:2] + extra[z, 2:3])
        norm += extra[z, 3:4] + extra[z, 4:5] + extra[z, 5:6]
        square += extra[z, 6:7] + extra[z, 7:8]
    lines += split(norm) + split(square)
    extra = jnp.concatenate(lines + [jnp.zeros((2, 128), f32)], axis=0).astype(bf16)
    grad = got[:, 0:8, :].reshape(512, 128).astype(bf16)
    decayed = got[:, 8:16, :].reshape(512, 128).astype(bf16)
    for p in range(N_X):
        out_ref[p, 0:512, :] = grad
        out_ref[p, 512:1024, :] = decayed
        out_ref[p, 1024:1056, :] = extra


def update_kernel(
    mine_ref, other_ref, w_ref, master_ref, vel_ref, bn_ref, bnv_ref,
    new_master_hbm, new_vel_hbm, new_w_hbm, new_bn_hbm, new_bnv_hbm,
    new_master_ref, new_vel_ref, new_w, new_bn_ref, new_bnv_ref, sems, small_sems,
):
    core, layer = core_of(), lax.axis_index("z").astype(jnp.int32)
    row = (lax.axis_index("x") * N_Y + lax.axis_index("y")).astype(jnp.int32)

    def run(parts):
        square = jnp.zeros((1, 128), f32)
        norm = jnp.zeros((1, 128), f32)
        totals = []
        for part in parts:
            extra = jnp.zeros((32, 128), f32)
            for x in range(N_X):
                extra += part[x, 1024:1056, :].astype(f32)
            line = [extra[3 * z : 3 * z + 1] + extra[3 * z + 1 : 3 * z + 2] + extra[3 * z + 2 : 3 * z + 3] for z in range(N_Z)]
            norm += extra[24:25] + extra[25:26] + extra[26:27]
            square += extra[27:28] + extra[28:29] + extra[29:30]
            totals.append(jnp.concatenate(line, axis=1))
        wnorm = jnp.sqrt(norm[:, 0:1])
        gnorm = jnp.sqrt(square[:, 0:1])
        rate = learn_rate * (trust_coef * wnorm / (gnorm + weight_decay * wnorm))
        bn_grad = jnp.concatenate([totals[1], totals[0]], axis=0) * (1.0 / BATCH)
        new_bnv = momentum * bnv_ref[...] + learn_rate * bn_grad
        new_bnv_ref[...] = new_bnv
        new_bn_ref[...] = bn_ref[...] - new_bnv
        for h in range(2):

            @pl.when(row // 16 == h)
            def _():
                start = pl.multiple_of(layer * 64 + row % 4 * 16, 16)
                pair = parts[h][row % 16 // 4, pl.ds(start, 16), :].astype(f32)
                own = jnp.where(core == 0, pair[:, :64], pair[:, 64:])
                new_vel = momentum * vel_ref[...] + rate * (own + weight_decay * master_ref[...])
                new_vel_ref[...] = new_vel
                new_master_ref[...] = master_ref[...] - new_vel

        small_pairs = (
            (new_master_ref, new_master_hbm),
            (new_vel_ref, new_vel_hbm),
            (new_bn_ref, new_bn_hbm),
            (new_bnv_ref, new_bnv_hbm),
        )
        stores = [pltpu.make_async_copy(here, there, small_sems.at[k]) for k, (here, there) in enumerate(small_pairs)]
        for copy in stores:
            copy.start()
        for x in range(N_X):
            tiles = [part[x, 512:1024, :].astype(f32).reshape(N_Y, N_Z, 8, 128) for part in parts]
            rows = slice(128 * x, 128 * x + 128)
            h, strip = x // 2, x % 2 * 2
            for z in range(N_Z):
                columns = slice(128 * z, 128 * z + 128)
                even, odd = [tile[:, z] for tile in tiles]
                top = jnp.concatenate([even[:, :, :64], odd[:, :, :64]], axis=2)
                bottom = jnp.concatenate([even[:, :, 64:], odd[:, :, 64:]], axis=2)
                decayed = jnp.stack([top, bottom], axis=1).reshape(128, 128)
                lines = slice(64 * z, 64 * z + 64)
                step = jnp.concatenate([parts[h][strip, lines, :], parts[h][strip + 1, lines, :]], axis=0).astype(f32)
                step += weight_decay * w_ref[rows, columns].astype(f32)
                new_w[rows, columns] = (decayed - rate * step).astype(bf16)
            stores.append(pltpu.make_async_copy(new_w.at[rows], new_w_hbm.at[rows], sems.at[x]))
            stores[-1].start()
        for copy in stores:
            copy.wait()

    @pl.when(core == 0)
    def _():
        run((mine_ref, other_ref))

    @pl.when(core == 1)
    def _():
        run((other_ref, mine_ref))


def shape(dims, kind):
    return jax.ShapeDtypeStruct(dims, kind)


VMEM = pl.BlockSpec(memory_space=pltpu.VMEM)
HBM = pl.BlockSpec(memory_space=pltpu.HBM)


def body(activations, pre_activation, pooled_grad, weights, master, velocity, bn_params, bn_velocity):
    msg, conv, act, pre, pool = pl.pallas_call(
        stats_kernel,
        out_shape=(
            pltpu.VMEM((STAT_ROWS, 128), f32),
            pltpu.VMEM((ROWS, COUT), bf16),
            pltpu.VMEM((ROWS, CIN), bf16),
            pltpu.VMEM((IMG, PIX, COUT), bf16),
            pltpu.VMEM((IMG, COUT), f32),
        ),
        in_specs=[HBM] * 4,
        out_specs=(VMEM,) * 5,
        scratch_shapes=[
            pltpu.VMEM((IMG, PIX, CIN), bf16),
            pltpu.VMEM((CIN, COUT), bf16),
            pltpu.SemaphoreType.DMA((4, PARTS)),
        ],
        compiler_params=params(60),
        name="conv_stats",
    )(activations, pre_activation, pooled_grad, weights)
    chip = pl.pallas_call(
        chip_kernel,
        out_shape=shape((N_Z, STAT_ROWS, 128), f32),
        in_specs=[VMEM],
        out_specs=VMEM,
        compiler_params=params(),
        name="chip_stats",
    )(lax.all_gather(msg, "core"))
    stats = lax.all_to_all(chip, "z", 0, 0)
    conv_grad, act, send, line = pl.pallas_call(
        grad_kernel,
        out_shape=(
            shape((ROWS, COUT), bf16),
            shape((ROWS, CIN), bf16),
            shape((HALF, COUT), bf16),
            shape((8, 128), f32),
        ),
        in_specs=[VMEM] * 7,
        out_specs=(VMEM,) * 4,
        scratch_shapes=[pltpu.VMEM((16, 128), f32)],
        compiler_params=params(),
        name="conv_grad",
    )(stats, msg, conv, act, pre, pool, bn_params)
    swap = [(0, 1), (1, 0)]
    got = lax.ppermute(send, "core", swap)
    keep = pl.pallas_call(
        keep_kernel,
        out_shape=shape((HALF, COUT), f32),
        in_specs=[VMEM] * 2,
        out_specs=VMEM,
        compiler_params=params(),
        cost_estimate=pl.CostEstimate(flops=2 * ROWS * HALF * COUT, bytes_accessed=4 << 20, transcendentals=0),
        name="keep_grad",
    )(act, conv_grad)
    input_grad = pl.pallas_call(
        back_kernel,
        out_shape=shape((IMG, PIX, CIN), bf16),
        in_specs=[VMEM] * 2,
        out_specs=VMEM,
        compiler_params=params(),
        cost_estimate=pl.CostEstimate(flops=2 * ROWS * CIN * COUT, bytes_accessed=4 << 20, transcendentals=0),
        name="input_grad",
    )(conv_grad, weights)
    halves = pl.pallas_call(
        pair_kernel,
        out_shape=shape((HALF, COUT), bf16),
        in_specs=[VMEM] * 2,
        out_specs=VMEM,
        compiler_params=params(),
        name="pair_sum",
    )(keep, got)
    arrived = lax.all_to_all(halves.reshape(N_X, HALF // N_X, COUT), "x", 0, 0)
    lines = pl.pallas_call(
        line_kernel,
        out_shape=shape((N_Y, N_Z, 8, 128), bf16),
        in_specs=[VMEM],
        out_specs=VMEM,
        compiler_params=params(),
        name="line_sum",
    )(arrived)
    arrived = lax.all_to_all(lines.reshape(N_Y * N_Z, 8, 128), PLANE, 0, 0)
    block = pl.pallas_call(
        block_kernel,
        out_shape=shape((N_Y * N_Z, SIDE_ROWS, 128), bf16),
        in_specs=[VMEM] * 4,
        out_specs=VMEM,
        compiler_params=params(),
        name="block_sum",
    )(arrived, line, master, velocity)
    wide = pl.pallas_call(
        plane_kernel,
        out_shape=shape((N_X, WIDE_ROWS, 128), bf16),
        in_specs=[VMEM],
        out_specs=VMEM,
        compiler_params=params(),
        name="plane_join",
    )(lax.all_to_all(block, PLANE, 0, 0))
    mine = lax.all_to_all(wide, "x", 0, 0)
    other = lax.ppermute(mine, "core", swap)
    new_master, new_velocity, new_weights, new_bn, new_bn_velocity = pl.pallas_call(
        update_kernel,
        out_shape=(
            shape((16, 64), f32),
            shape((16, 64), f32),
            shape((CIN, COUT), bf16),
            shape((2, COUT), f32),
            shape((2, COUT), f32),
        ),
        in_specs=[VMEM] * 7,
        out_specs=(HBM,) * 5,
        scratch_shapes=[
            pltpu.VMEM((16, 64), f32),
            pltpu.VMEM((16, 64), f32),
            pltpu.VMEM((CIN, COUT), bf16),
            pltpu.VMEM((2, COUT), f32),
            pltpu.VMEM((2, COUT), f32),
            pltpu.SemaphoreType.DMA((N_X,)),
            pltpu.SemaphoreType.DMA((4,)),
        ],
        compiler_params=params(),
        name="update",
    )(mine, other, weights, master, velocity, bn_params, bn_velocity)
    return input_grad, new_master, new_velocity, new_weights, new_bn, new_bn_velocity


def solution(mesh):
    fine = Mesh(mesh.devices.reshape(4, 8, 8, 2), ALL)
    block = P(("x", "y"), ("z", "core"))
    return jax.shard_map(
        body,
        mesh=fine,
        in_specs=(P(ALL, None, None), P(ALL, None, None), P(ALL, None), P(), block, block, P(), P()),
        out_specs=(P(ALL, None, None), block, block, P(), P(), P()),
        check_vma=False,
    )
```

```python
import jax
import jax.numpy as jnp
from jax import lax
from jax.experimental import pallas as pl
from jax.experimental.pallas import tpu as pltpu
from jax.sharding import Mesh, PartitionSpec as P

epsilon = 1e-05
trust_coef = 0.001
weight_decay = 0.0001
momentum = 0.9
learn_rate = 12.0

IMG, PIX, STRIDE = 12, 49, 64
CIN, COUT = 512, 1024
ROWS = IMG * STRIDE
HALF = CIN // 2
N_ROW, N_COL = 32, 16
N_X, N_Y, N_Z = 4, 8, 8
M = PIX * IMG * N_COL
BATCH = IMG * N_ROW * N_COL
CHUNKS = COUT // 128
PLANE, ALL = ("y", "z"), ("x", "y", "z", "core")
STAT_ROWS = 40
SIDE_ROWS = 24
WIDE_ROWS = 1056
PARTS = 2
STRIP = 256
bf16, f32 = jnp.bfloat16, jnp.float32


def params(megabytes=20):
    return pltpu.CompilerParams(vmem_limit_bytes=megabytes << 20)


def fold(line):
    return jnp.concatenate([line[:, 128 * k : 128 * k + 128] for k in range(line.shape[1] // 128)], axis=0)


def unfold(block):
    return jnp.concatenate([block[k : k + 1] for k in range(block.shape[0])], axis=1)


def split(line):
    high = line.astype(bf16).astype(f32)
    middle = (line - high).astype(bf16).astype(f32)
    return high, middle, line - high - middle


def rows_of(count, lines, dims):
    row = lax.broadcasted_iota(jnp.int32, dims, 0)
    block = jnp.zeros(dims, f32)
    for k in range(count):
        block = jnp.where(row == k, jnp.broadcast_to(lines[k], dims), block)
    return block


def stats_kernel(act_hbm, pre_hbm, pool_hbm, w_hbm, msg_ref, conv, actp, pre, pool, act, w, sem_in):
    step = IMG // PARTS
    loads = []
    for k in range(PARTS):
        part = pl.ds(step * k, step)
        strip = pl.ds(CIN // PARTS * k, CIN // PARTS)
        loads.append(pltpu.make_async_copy(w_hbm.at[strip], w.at[strip], sem_in.at[0, k]))
        loads.append(pltpu.make_async_copy(act_hbm.at[part], act.at[part], sem_in.at[1, k]))
    for copy in loads:
        copy.start()
    later = [pltpu.make_async_copy(pool_hbm, pool, sem_in.at[3, 0])]
    for k in range(PARTS):
        part = pl.ds(step * k, step)
        later.append(pltpu.make_async_copy(pre_hbm.at[part], pre.at[part], sem_in.at[2, k]))
    for copy in later:
        copy.start()
    actp[...] = jnp.zeros_like(actp)
    for copy in loads:
        copy.wait()
    for i in range(IMG):
        actp[STRIDE * i : STRIDE * i + PIX, :] = act[i]
    act_total = jnp.sum(actp[...].astype(f32), axis=0, keepdims=True)
    strips = [slice(STRIP * k, STRIP * k + STRIP) for k in range(COUT // STRIP)]
    lines = []
    for strip in strips:
        value = jnp.dot(actp[...], w[:, strip], preferred_element_type=f32).astype(bf16)
        conv[:, strip] = value
        value = value.astype(f32).reshape(IMG, STRIDE, STRIP)[:, :56]
        total = jnp.sum(jnp.sum(value, axis=0), axis=0, keepdims=True)
        square = jnp.sum(jnp.sum(value * value, axis=0), axis=0, keepdims=True)
        lines.append([total, square])
    for copy in later:
        copy.wait()
    for k, strip in enumerate(strips):
        wide, last = (8, STRIP), (1, STRIP)
        up, up_conv = jnp.zeros(wide, f32), jnp.zeros(wide, f32)
        up_last, up_conv_last = jnp.zeros(last, f32), jnp.zeros(last, f32)
        for i in range(IMG):
            value = conv[STRIDE * i : STRIDE * i + STRIDE, strip].astype(f32)[:PIX]
            passed = pre[i, :, strip].astype(f32) > 0
            share = pool[i : i + 1, strip] / PIX
            ones = jnp.where(passed, 1.0, 0.0)
            value = jnp.where(passed, value, 0.0)
            up += share * jnp.sum(ones[:48].reshape(6, 8, STRIP), axis=0)
            up_conv += share * jnp.sum(value[:48].reshape(6, 8, STRIP), axis=0)
            up_last += share * ones[48:49]
            up_conv_last += share * value[48:49]
        up = jnp.sum(up, axis=0, keepdims=True) + up_last
        up_conv = jnp.sum(up_conv, axis=0, keepdims=True) + up_conv_last
        lines[k] += [up, up_conv]
    sums = [fold(jnp.concatenate([line[q] for line in lines], axis=1)) for q in range(4)]
    msg = jnp.concatenate(sums + [fold(act_total), jnp.zeros((4, 128), f32)], axis=0)
    msg_ref[...] = msg


def chip_kernel(got_ref, out_ref):
    out_ref[...] = jnp.broadcast_to((got_ref[0] + got_ref[1])[None], out_ref.shape)


def grad_kernel(
    stat_ref, msg_ref, conv_ref, act_ref, pre_ref, pool_ref, bn_ref, cg_ref, actp, send_ref, line_ref, lines
):
    core, layer = core_of(), lax.axis_index("z").astype(jnp.int32)
    sums = jnp.sum(stat_ref[...], axis=0)
    sum_up = sums[16:24]
    act_mean = (unfold(sums[32:36]) / M).astype(bf16).astype(f32)
    mean = sums[0:8] / M
    variance = sums[8:16] / M - mean * mean
    rstd = lax.rsqrt(variance + epsilon)
    sum_upx = rstd * (sums[24:32] - mean * sum_up)
    lines[0:8, :] = sum_up
    lines[8:16, :] = sum_upx
    line_ref[...] = jnp.broadcast_to(lines[pl.ds(core * 8 + layer, 1), :], (8, 128))
    scale = fold(bn_ref[0:1, :]) * rstd
    shift = scale * (sum_up / M)
    slope = scale * (sum_upx / M) * rstd
    local = IMG * PIX
    cg_total = unfold(scale * msg_ref[16:24, :] - local * shift - slope * (msg_ref[0:8, :] - local * mean))
    mean, scale, shift, slope = unfold(mean), unfold(scale), unfold(shift), unfold(slope)
    actp[...] = act_ref[...]
    for i in range(IMG):
        cg_ref[STRIDE * i + 48 : STRIDE * i + 64, :] = jnp.zeros((16, COUT), bf16)
        conv = conv_ref[STRIDE * i : STRIDE * i + STRIDE, :].astype(f32)[:PIX]
        on = scale * (pool_ref[i : i + 1, :] / PIX) - shift
        cg = jnp.where(pre_ref[i].astype(f32) > 0, on, -shift) - slope * (conv - mean)
        cg_ref[STRIDE * i : STRIDE * i + PIX, :] = cg.astype(bf16)
    edge = actp[48:64, :].astype(f32)
    row = lax.broadcasted_iota(jnp.int32, edge.shape, 0)
    actp[48:64, :] = jnp.where((row >= 1) & (row < 4), -act_mean, edge).astype(bf16)
    high, middle, rest = split(cg_total)
    edge = cg_ref[48:64, :].astype(f32)
    cg_ref[48:64, :] = (edge + rows_of(4, [jnp.zeros_like(high), high, middle, rest], edge.shape)).astype(bf16)
    send_ref[...] = half_grad(actp, cg_ref, 1 - core).astype(bf16)


def core_of():
    return lax.axis_index("core").astype(jnp.int32)


def half_grad(actp, cg_ref, half):
    columns = actp[:, pl.ds(pl.multiple_of(half * HALF, HALF), HALF)]
    return lax.dot_general(columns, cg_ref[...], (((0,), (0,)), ((), ())), preferred_element_type=f32)


def keep_kernel(actp, cg_ref, keep_ref):
    keep_ref[...] = half_grad(actp, cg_ref, core_of())


def back_kernel(cg_ref, w_ref, out_ref):
    back = lax.dot_general(cg_ref[...], w_ref[...], (((1,), (1,)), ((), ())), preferred_element_type=f32)
    for i in range(IMG):
        out_ref[i] = back[STRIDE * i : STRIDE * i + PIX].astype(bf16)


def pair_kernel(keep_ref, got_ref, out_ref):
    out_ref[...] = (keep_ref[...] + got_ref[...].astype(f32)).astype(bf16)


def line_kernel(got_ref, out_ref):
    total = jnp.sum(got_ref[...].astype(f32), axis=0).reshape(N_Z, 8, COUT)
    for y in range(N_Y):
        out_ref[y] = total[:, :, 128 * y : 128 * y + 128].astype(bf16)


def block_kernel(got_ref, line_ref, master_ref, vel_ref, out_ref):
    total = jnp.sum(got_ref[...].astype(f32), axis=0) * (1.0 / BATCH)
    master = master_ref[...]
    decayed = master - momentum * vel_ref[...]
    decayed = jnp.concatenate([decayed[:8], decayed[8:]], axis=1)
    norm = jnp.sum(jnp.sum(master * master, axis=1, keepdims=True), axis=0, keepdims=True)
    square = jnp.sum(jnp.sum(total * total, axis=1, keepdims=True), axis=0, keepdims=True)
    norms = split(jnp.broadcast_to(norm, (8, 128))) + split(jnp.broadcast_to(square, (8, 128)))[:2]
    extra = rows_of(8, split(line_ref[...]) + norms, (8, 128))
    block = jnp.concatenate([total, decayed, extra], axis=0).astype(bf16)
    out_ref[...] = jnp.broadcast_to(block[None], out_ref.shape)


def plane_kernel(got_ref, out_ref):
    got = got_ref[...].astype(f32)
    extra = jnp.sum(got[:, 16:24, :].reshape(N_Y, N_Z, 8, 128), axis=0)
    lines = []
    norm = jnp.zeros((1, 128), f32)
    square = jnp.zeros((1, 128), f32)
    for z in range(N_Z):
        lines += split(extra[z, 0:1] + extra[z, 1:2] + extra[z, 2:3])
        norm += extra[z, 3:4] + extra[z, 4:5] + extra[z, 5:6]
        square += extra[z, 6:7] + extra[z, 7:8]
    lines += split(norm) + split(square)
    extra = jnp.concatenate(lines + [jnp.zeros((2, 128), f32)], axis=0).astype(bf16)
    grad = got[:, 0:8, :].reshape(512, 128).astype(bf16)
    decayed = got[:, 8:16, :].reshape(512, 128).astype(bf16)
    for p in range(N_X):
        out_ref[p, 0:512, :] = grad
        out_ref[p, 512:1024, :] = decayed
        out_ref[p, 1024:1056, :] = extra


def update_kernel(
    mine_ref, other_ref, w_ref, master_ref, vel_ref, bn_ref, bnv_ref,
    new_master_hbm, new_vel_hbm, new_w_hbm, new_bn_hbm, new_bnv_hbm,
    new_master_ref, new_vel_ref, new_w, new_bn_ref, new_bnv_ref, sems, small_sems,
):
    core, layer = core_of(), lax.axis_index("z").astype(jnp.int32)
    row = (lax.axis_index("x") * N_Y + lax.axis_index("y")).astype(jnp.int32)

    def run(parts):
        square = jnp.zeros((1, 128), f32)
        norm = jnp.zeros((1, 128), f32)
        totals = []
        for part in parts:
            extra = jnp.zeros((32, 128), f32)
            for x in range(N_X):
                extra += part[x, 1024:1056, :].astype(f32)
            line = [extra[3 * z : 3 * z + 1] + extra[3 * z + 1 : 3 * z + 2] + extra[3 * z + 2 : 3 * z + 3] for z in range(N_Z)]
            norm += extra[24:25] + extra[25:26] + extra[26:27]
            square += extra[27:28] + extra[28:29] + extra[29:30]
            totals.append(jnp.concatenate(line, axis=1))
        wnorm = jnp.sqrt(norm[:, 0:1])
        gnorm = jnp.sqrt(square[:, 0:1])
        rate = learn_rate * (trust_coef * wnorm / (gnorm + weight_decay * wnorm))
        bn_grad = jnp.concatenate([totals[1], totals[0]], axis=0) * (1.0 / BATCH)
        new_bnv = momentum * bnv_ref[...] + learn_rate * bn_grad
        new_bnv_ref[...] = new_bnv
        new_bn_ref[...] = bn_ref[...] - new_bnv
        for h in range(2):

            @pl.when(row // 16 == h)
            def _():
                start = pl.multiple_of(layer * 64 + row % 4 * 16, 16)
                pair = parts[h][row % 16 // 4, pl.ds(start, 16), :].astype(f32)
                own = jnp.where(core == 0, pair[:, :64], pair[:, 64:])
                new_vel = momentum * vel_ref[...] + rate * (own + weight_decay * master_ref[...])
                new_vel_ref[...] = new_vel
                new_master_ref[...] = master_ref[...] - new_vel

        small_pairs = (
            (new_master_ref, new_master_hbm),
            (new_vel_ref, new_vel_hbm),
            (new_bn_ref, new_bn_hbm),
            (new_bnv_ref, new_bnv_hbm),
        )
        stores = [pltpu.make_async_copy(here, there, small_sems.at[k]) for k, (here, there) in enumerate(small_pairs)]
        for copy in stores:
            copy.start()
        for x in range(N_X):
            tiles = [part[x, 512:1024, :].astype(f32).reshape(N_Y, N_Z, 8, 128) for part in parts]
            rows = slice(128 * x, 128 * x + 128)
            h, strip = x // 2, x % 2 * 2
            for z in range(N_Z):
                columns = slice(128 * z, 128 * z + 128)
                even, odd = [tile[:, z] for tile in tiles]
                top = jnp.concatenate([even[:, :, :64], odd[:, :, :64]], axis=2)
                bottom = jnp.concatenate([even[:, :, 64:], odd[:, :, 64:]], axis=2)
                decayed = jnp.stack([top, bottom], axis=1).reshape(128, 128)
                lines = slice(64 * z, 64 * z + 64)
                step = jnp.concatenate([parts[h][strip, lines, :], parts[h][strip + 1, lines, :]], axis=0).astype(f32)
                step += weight_decay * w_ref[rows, columns].astype(f32)
                new_w[rows, columns] = (decayed - rate * step).astype(bf16)
            stores.append(pltpu.make_async_copy(new_w.at[rows], new_w_hbm.at[rows], sems.at[x]))
            stores[-1].start()
        for copy in stores:
            copy.wait()

    @pl.when(core == 0)
    def _():
        run((mine_ref, other_ref))

    @pl.when(core == 1)
    def _():
        run((other_ref, mine_ref))


def shape(dims, kind):
    return jax.ShapeDtypeStruct(dims, kind)


VMEM = pl.BlockSpec(memory_space=pltpu.VMEM)
HBM = pl.BlockSpec(memory_space=pltpu.HBM)


def body(activations, pre_activation, pooled_grad, weights, master, velocity, bn_params, bn_velocity):
    msg, conv, act, pre, pool = pl.pallas_call(
        stats_kernel,
        out_shape=(
            pltpu.VMEM((STAT_ROWS, 128), f32),
            pltpu.VMEM((ROWS, COUT), bf16),
            pltpu.VMEM((ROWS, CIN), bf16),
            pltpu.VMEM((IMG, PIX, COUT), bf16),
            pltpu.VMEM((IMG, COUT), f32),
        ),
        in_specs=[HBM] * 4,
        out_specs=(VMEM,) * 5,
        scratch_shapes=[
            pltpu.VMEM((IMG, PIX, CIN), bf16),
            pltpu.VMEM((CIN, COUT), bf16),
            pltpu.SemaphoreType.DMA((4, PARTS)),
        ],
        compiler_params=params(60),
        name="conv_stats",
    )(activations, pre_activation, pooled_grad, weights)
    chip = pl.pallas_call(
        chip_kernel,
        out_shape=shape((N_Z, STAT_ROWS, 128), f32),
        in_specs=[VMEM],
        out_specs=VMEM,
        compiler_params=params(),
        name="chip_stats",
    )(lax.all_gather(msg, "core"))
    stats = lax.all_to_all(chip, "z", 0, 0)
    conv_grad, act, send, line = pl.pallas_call(
        grad_kernel,
        out_shape=(
            shape((ROWS, COUT), bf16),
            shape((ROWS, CIN), bf16),
            shape((HALF, COUT), bf16),
            shape((8, 128), f32),
        ),
        in_specs=[VMEM] * 7,
        out_specs=(VMEM,) * 4,
        scratch_shapes=[pltpu.VMEM((16, 128), f32)],
        compiler_params=params(),
        name="conv_grad",
    )(stats, msg, conv, act, pre, pool, bn_params)
    swap = [(0, 1), (1, 0)]
    got = lax.ppermute(send, "core", swap)
    keep = pl.pallas_call(
        keep_kernel,
        out_shape=shape((HALF, COUT), f32),
        in_specs=[VMEM] * 2,
        out_specs=VMEM,
        compiler_params=params(),
        cost_estimate=pl.CostEstimate(flops=2 * ROWS * HALF * COUT, bytes_accessed=4 << 20, transcendentals=0),
        name="keep_grad",
    )(act, conv_grad)
    input_grad = pl.pallas_call(
        back_kernel,
        out_shape=shape((IMG, PIX, CIN), bf16),
        in_specs=[VMEM] * 2,
        out_specs=VMEM,
        compiler_params=params(),
        cost_estimate=pl.CostEstimate(flops=2 * ROWS * CIN * COUT, bytes_accessed=4 << 20, transcendentals=0),
        name="input_grad",
    )(conv_grad, weights)
    halves = pl.pallas_call(
        pair_kernel,
        out_shape=shape((HALF, COUT), bf16),
        in_specs=[VMEM] * 2,
        out_specs=VMEM,
        compiler_params=params(),
        name="pair_sum",
    )(keep, got)
    arrived = lax.all_to_all(halves.reshape(N_X, HALF // N_X, COUT), "x", 0, 0)
    lines = pl.pallas_call(
        line_kernel,
        out_shape=shape((N_Y, N_Z, 8, 128), bf16),
        in_specs=[VMEM],
        out_specs=VMEM,
        compiler_params=params(),
        name="line_sum",
    )(arrived)
    arrived = lax.all_to_all(lines.reshape(N_Y * N_Z, 8, 128), PLANE, 0, 0)
    block = pl.pallas_call(
        block_kernel,
        out_shape=shape((N_Y * N_Z, SIDE_ROWS, 128), bf16),
        in_specs=[VMEM] * 4,
        out_specs=VMEM,
        compiler_params=params(),
        name="block_sum",
    )(arrived, line, master, velocity)
    wide = pl.pallas_call(
        plane_kernel,
        out_shape=shape((N_X, WIDE_ROWS, 128), bf16),
        in_specs=[VMEM],
        out_specs=VMEM,
        compiler_params=params(),
        name="plane_join",
    )(lax.all_to_all(block, PLANE, 0, 0))
    mine = lax.all_to_all(wide, "x", 0, 0)
    other = lax.ppermute(mine, "core", swap)
    new_master, new_velocity, new_weights, new_bn, new_bn_velocity = pl.pallas_call(
        update_kernel,
        out_shape=(
            shape((16, 64), f32),
            shape((16, 64), f32),
            shape((CIN, COUT), bf16),
            shape((2, COUT), f32),
            shape((2, COUT), f32),
        ),
        in_specs=[VMEM] * 7,
        out_specs=(HBM,) * 5,
        scratch_shapes=[
            pltpu.VMEM((16, 64), f32),
            pltpu.VMEM((16, 64), f32),
            pltpu.VMEM((CIN, COUT), bf16),
            pltpu.VMEM((2, COUT), f32),
            pltpu.VMEM((2, COUT), f32),
            pltpu.SemaphoreType.DMA((N_X,)),
            pltpu.SemaphoreType.DMA((4,)),
        ],
        compiler_params=params(),
        name="update",
    )(mine, other, weights, master, velocity, bn_params, bn_velocity)
    return input_grad, new_master, new_velocity, new_weights, new_bn, new_bn_velocity


def solution(mesh):
    fine = Mesh(mesh.devices.reshape(4, 8, 8, 2), ALL)
    block = P(("x", "y"), ("z", "core"))
    return jax.shard_map(
        body,
        mesh=fine,
        in_specs=(P(ALL, None, None), P(ALL, None, None), P(ALL, None), P(), block, block, P(), P()),
        out_specs=(P(ALL, None, None), block, block, P(), P(), P()),
        check_vma=False,
    )
```

```python
import jax
import jax.numpy as jnp
from jax import lax
from jax.experimental import pallas as pl
from jax.experimental.pallas import tpu as pltpu
from jax.sharding import Mesh, PartitionSpec as P

epsilon = 1e-05
trust_coef = 0.001
weight_decay = 0.0001
momentum = 0.9
learn_rate = 12.0

IMG, PIX, STRIDE = 12, 49, 64
CIN, COUT = 512, 1024
ROWS = IMG * STRIDE
WIDE = COUT // 2
N_ROW, N_COL = 32, 16
N_X, N_Y, N_Z = 4, 8, 8
M = PIX * IMG * N_COL
BATCH = IMG * N_ROW * N_COL
CHUNKS = COUT // 128
PLANE, ALL = ("y", "z"), ("x", "y", "z", "core")
STAT_ROWS = 40
SIDE_ROWS = 24
WIDE_ROWS = 1056
PARTS = 2
STRIP = 256
bf16, f32 = jnp.bfloat16, jnp.float32


def params(megabytes=20):
    return pltpu.CompilerParams(vmem_limit_bytes=megabytes << 20)


def fold(line):
    return jnp.concatenate([line[:, 128 * k : 128 * k + 128] for k in range(line.shape[1] // 128)], axis=0)


def unfold(block):
    return jnp.concatenate([block[k : k + 1] for k in range(block.shape[0])], axis=1)


def split(line):
    high = line.astype(bf16).astype(f32)
    middle = (line - high).astype(bf16).astype(f32)
    return high, middle, line - high - middle


def rows_of(count, lines, dims):
    row = lax.broadcasted_iota(jnp.int32, dims, 0)
    block = jnp.zeros(dims, f32)
    for k in range(count):
        block = jnp.where(row == k, jnp.broadcast_to(lines[k], dims), block)
    return block


def stats_kernel(act_hbm, pre_hbm, pool_hbm, w_hbm, msg_ref, conv, actp, pre, pool, act, w, sem_in):
    step = IMG // PARTS
    loads = []
    for k in range(PARTS):
        part = pl.ds(step * k, step)
        strip = pl.ds(CIN // PARTS * k, CIN // PARTS)
        loads.append(pltpu.make_async_copy(w_hbm.at[strip], w.at[strip], sem_in.at[0, k]))
        loads.append(pltpu.make_async_copy(act_hbm.at[part], act.at[part], sem_in.at[1, k]))
    for copy in loads:
        copy.start()
    later = [pltpu.make_async_copy(pool_hbm, pool, sem_in.at[3, 0])]
    for k in range(PARTS):
        part = pl.ds(step * k, step)
        later.append(pltpu.make_async_copy(pre_hbm.at[part], pre.at[part], sem_in.at[2, k]))
    for copy in later:
        copy.start()
    actp[...] = jnp.zeros_like(actp)
    for copy in loads:
        copy.wait()
    for i in range(IMG):
        actp[STRIDE * i : STRIDE * i + PIX, :] = act[i]
    act_total = jnp.sum(actp[...].astype(f32), axis=0, keepdims=True)
    strips = [slice(STRIP * k, STRIP * k + STRIP) for k in range(COUT // STRIP)]
    lines = []
    for strip in strips:
        value = jnp.dot(actp[...], w[:, strip], preferred_element_type=f32).astype(bf16)
        conv[:, strip] = value
        value = value.astype(f32).reshape(IMG, STRIDE, STRIP)[:, :56]
        total = jnp.sum(jnp.sum(value, axis=0), axis=0, keepdims=True)
        square = jnp.sum(jnp.sum(value * value, axis=0), axis=0, keepdims=True)
        lines.append([total, square])
    for copy in later:
        copy.wait()
    for k, strip in enumerate(strips):
        wide, last = (8, STRIP), (1, STRIP)
        up, up_conv = jnp.zeros(wide, f32), jnp.zeros(wide, f32)
        up_last, up_conv_last = jnp.zeros(last, f32), jnp.zeros(last, f32)
        for i in range(IMG):
            value = conv[STRIDE * i : STRIDE * i + STRIDE, strip].astype(f32)[:PIX]
            passed = pre[i, :, strip].astype(f32) > 0
            share = pool[i : i + 1, strip] / PIX
            ones = jnp.where(passed, 1.0, 0.0)
            value = jnp.where(passed, value, 0.0)
            up += share * jnp.sum(ones[:48].reshape(6, 8, STRIP), axis=0)
            up_conv += share * jnp.sum(value[:48].reshape(6, 8, STRIP), axis=0)
            up_last += share * ones[48:49]
            up_conv_last += share * value[48:49]
        up = jnp.sum(up, axis=0, keepdims=True) + up_last
        up_conv = jnp.sum(up_conv, axis=0, keepdims=True) + up_conv_last
        lines[k] += [up, up_conv]
    sums = [fold(jnp.concatenate([line[q] for line in lines], axis=1)) for q in range(4)]
    msg = jnp.concatenate(sums + [fold(act_total), jnp.zeros((4, 128), f32)], axis=0)
    msg_ref[...] = msg


def chip_kernel(got_ref, out_ref):
    out_ref[...] = jnp.broadcast_to((got_ref[0] + got_ref[1])[None], out_ref.shape)


def fill(vectors, half, conv_ref, pre_ref, pool_ref, cg_ref):
    columns = pl.ds(pl.multiple_of(half * WIDE, WIDE), WIDE)
    mean, scale, shift, slope, cg_total = [
        unfold(jnp.where(half == 0, vectors[8 * k : 8 * k + 4], vectors[8 * k + 4 : 8 * k + 8])) for k in range(5)
    ]
    for i in range(IMG):
        cg_ref[STRIDE * i + 48 : STRIDE * i + 64, :] = jnp.zeros((16, WIDE), bf16)
        conv = conv_ref[STRIDE * i : STRIDE * i + STRIDE, columns].astype(f32)[:PIX]
        on = scale * (pool_ref[i : i + 1, columns] / PIX) - shift
        cg = jnp.where(pre_ref[i, :, columns].astype(f32) > 0, on, -shift) - slope * (conv - mean)
        cg_ref[STRIDE * i : STRIDE * i + PIX, :] = cg.astype(bf16)
    high, middle, rest = split(cg_total)
    edge = cg_ref[48:64, :].astype(f32)
    cg_ref[48:64, :] = (edge + rows_of(4, [jnp.zeros_like(high), high, middle, rest], edge.shape)).astype(bf16)


def product(actp, cg_ref):
    return lax.dot_general(actp[...], cg_ref[...], (((0,), (0,)), ((), ())), preferred_element_type=f32)


def core_of():
    return lax.axis_index("core").astype(jnp.int32)


def grad_kernel(
    stat_ref, msg_ref, conv_ref, act_ref, pre_ref, pool_ref, bn_ref, cg_ref, actp, send_ref, line_ref, vec_ref, lines
):
    core, layer = core_of(), lax.axis_index("z").astype(jnp.int32)
    sums = jnp.sum(stat_ref[...], axis=0)
    sum_up = sums[16:24]
    act_mean = (unfold(sums[32:36]) / M).astype(bf16).astype(f32)
    mean = sums[0:8] / M
    variance = sums[8:16] / M - mean * mean
    rstd = lax.rsqrt(variance + epsilon)
    sum_upx = rstd * (sums[24:32] - mean * sum_up)
    lines[0:8, :] = sum_up
    lines[8:16, :] = sum_upx
    line_ref[...] = jnp.broadcast_to(lines[pl.ds(core * 8 + layer, 1), :], (8, 128))
    scale = fold(bn_ref[0:1, :]) * rstd
    shift = scale * (sum_up / M)
    slope = scale * (sum_upx / M) * rstd
    local = IMG * PIX
    cg_total = scale * msg_ref[16:24, :] - local * shift - slope * (msg_ref[0:8, :] - local * mean)
    vectors = jnp.concatenate([mean, scale, shift, slope, cg_total], axis=0)
    vec_ref[...] = vectors
    actp[...] = act_ref[...]
    edge = actp[48:64, :].astype(f32)
    row = lax.broadcasted_iota(jnp.int32, edge.shape, 0)
    actp[48:64, :] = jnp.where((row >= 1) & (row < 4), -act_mean, edge).astype(bf16)
    fill(vectors, 1 - core, conv_ref, pre_ref, pool_ref, cg_ref)
    send_ref[...] = product(actp, cg_ref).astype(bf16)


def keep_kernel(vec_ref, conv_ref, pre_ref, pool_ref, actp, cg_ref, keep_ref):
    fill(vec_ref[...], core_of(), conv_ref, pre_ref, pool_ref, cg_ref)
    keep_ref[...] = product(actp, cg_ref)


def back_kernel(sent_ref, kept_ref, w_ref, out_ref):
    core = core_of()
    back = jnp.zeros((ROWS, CIN), f32)
    for half, cg_ref in ((1 - core, sent_ref), (core, kept_ref)):
        w = w_ref[:, pl.ds(pl.multiple_of(half * WIDE, WIDE), WIDE)]
        back += lax.dot_general(cg_ref[...], w, (((1,), (1,)), ((), ())), preferred_element_type=f32)
    for i in range(IMG):
        out_ref[i] = back[STRIDE * i : STRIDE * i + PIX].astype(bf16)


def pair_kernel(keep_ref, got_ref, out_ref):
    out_ref[...] = (keep_ref[...] + got_ref[...].astype(f32)).astype(bf16)


def line_kernel(got_ref, out_ref):
    total = jnp.sum(got_ref[...].astype(f32), axis=0).reshape(16, 8, WIDE)
    for j in range(4):
        out_ref[j] = total[:, :, 128 * j : 128 * j + 128].astype(bf16)


def block_kernel(got_ref, line_ref, master_ref, vel_ref, out_ref):
    total = jnp.sum(got_ref[...].astype(f32), axis=0) * (1.0 / BATCH)
    master = master_ref[...]
    decayed = master - momentum * vel_ref[...]
    decayed = jnp.concatenate([decayed[:8], decayed[8:]], axis=1)
    norm = jnp.sum(jnp.sum(master * master, axis=1, keepdims=True), axis=0, keepdims=True)
    square = jnp.sum(jnp.sum(total * total, axis=1, keepdims=True), axis=0, keepdims=True)
    norms = split(jnp.broadcast_to(norm, (8, 128))) + split(jnp.broadcast_to(square, (8, 128)))[:2]
    extra = rows_of(8, split(line_ref[...]) + norms, (8, 128))
    block = jnp.concatenate([total, decayed, extra], axis=0).astype(bf16)
    out_ref[...] = jnp.broadcast_to(block[None], out_ref.shape)


def plane_kernel(got_ref, out_ref):
    got = got_ref[...].astype(f32)
    extra = jnp.sum(got[:, 16:24, :].reshape(N_Y, N_Z, 8, 128), axis=0)
    lines = []
    norm = jnp.zeros((1, 128), f32)
    square = jnp.zeros((1, 128), f32)
    for z in range(N_Z):
        lines += split(extra[z, 0:1] + extra[z, 1:2] + extra[z, 2:3])
        norm += extra[z, 3:4] + extra[z, 4:5] + extra[z, 5:6]
        square += extra[z, 6:7] + extra[z, 7:8]
    lines += split(norm) + split(square)
    extra = jnp.concatenate(lines + [jnp.zeros((2, 128), f32)], axis=0).astype(bf16)
    grad = got[:, 0:8, :].reshape(512, 128).astype(bf16)
    decayed = got[:, 8:16, :].reshape(512, 128).astype(bf16)
    for p in range(N_X):
        out_ref[p, 0:512, :] = grad
        out_ref[p, 512:1024, :] = decayed
        out_ref[p, 1024:1056, :] = extra


def update_kernel(
    mine_ref, other_ref, w_ref, master_ref, vel_ref, bn_ref, bnv_ref,
    new_master_hbm, new_vel_hbm, new_w_hbm, new_bn_hbm, new_bnv_hbm,
    new_master_ref, new_vel_ref, new_w, new_bn_ref, new_bnv_ref, sems, small_sems,
):
    core, layer = core_of(), lax.axis_index("z").astype(jnp.int32)
    row = (lax.axis_index("x") * N_Y + lax.axis_index("y")).astype(jnp.int32)

    def run(parts):
        square = jnp.zeros((1, 128), f32)
        norm = jnp.zeros((1, 128), f32)
        totals = []
        for part in parts:
            extra = jnp.zeros((32, 128), f32)
            for x in range(N_X):
                extra += part[x, 1024:1056, :].astype(f32)
            line = [extra[3 * z : 3 * z + 1] + extra[3 * z + 1 : 3 * z + 2] + extra[3 * z + 2 : 3 * z + 3] for z in range(N_Z)]
            norm += extra[24:25] + extra[25:26] + extra[26:27]
            square += extra[27:28] + extra[28:29] + extra[29:30]
            totals.append(jnp.concatenate(line, axis=1))
        wnorm = jnp.sqrt(norm[:, 0:1])
        gnorm = jnp.sqrt(square[:, 0:1])
        rate = learn_rate * (trust_coef * wnorm / (gnorm + weight_decay * wnorm))
        bn_grad = jnp.concatenate([totals[1], totals[0]], axis=0) * (1.0 / BATCH)
        new_bnv = momentum * bnv_ref[...] + learn_rate * bn_grad
        new_bnv_ref[...] = new_bnv
        new_bn_ref[...] = bn_ref[...] - new_bnv
        for h in range(2):

            @pl.when(layer // 4 == h)
            def _():
                start = pl.multiple_of(layer % 4 * 128 + row % 8 * 16, 16)
                pair = parts[h][row // 8, pl.ds(start, 16), :].astype(f32)
                own = jnp.where(core == 0, pair[:, :64], pair[:, 64:])
                new_vel = momentum * vel_ref[...] + rate * (own + weight_decay * master_ref[...])
                new_vel_ref[...] = new_vel
                new_master_ref[...] = master_ref[...] - new_vel

        small_pairs = (
            (new_master_ref, new_master_hbm),
            (new_vel_ref, new_vel_hbm),
            (new_bn_ref, new_bn_hbm),
            (new_bnv_ref, new_bnv_hbm),
        )
        stores = [pltpu.make_async_copy(here, there, small_sems.at[k]) for k, (here, there) in enumerate(small_pairs)]
        for copy in stores:
            copy.start()
        for x in range(N_X):
            tiles = [part[x, 512:1024, :].astype(f32).reshape(N_Y, N_Z, 8, 128) for part in parts]
            rows = slice(128 * x, 128 * x + 128)
            for z in range(N_Z):
                columns = slice(128 * z, 128 * z + 128)
                even, odd = [tile[:, z] for tile in tiles]
                top = jnp.concatenate([even[:, :, :64], odd[:, :, :64]], axis=2)
                bottom = jnp.concatenate([even[:, :, 64:], odd[:, :, 64:]], axis=2)
                decayed = jnp.stack([top, bottom], axis=1).reshape(128, 128)
                lines = slice(128 * (z % 4), 128 * (z % 4) + 128)
                step = parts[z // 4][x, lines, :].astype(f32)
                step += weight_decay * w_ref[rows, columns].astype(f32)
                new_w[rows, columns] = (decayed - rate * step).astype(bf16)
            stores.append(pltpu.make_async_copy(new_w.at[rows], new_w_hbm.at[rows], sems.at[x]))
            stores[-1].start()
        for copy in stores:
            copy.wait()

    @pl.when(core == 0)
    def _():
        run((mine_ref, other_ref))

    @pl.when(core == 1)
    def _():
        run((other_ref, mine_ref))


def shape(dims, kind):
    return jax.ShapeDtypeStruct(dims, kind)


VMEM = pl.BlockSpec(memory_space=pltpu.VMEM)
HBM = pl.BlockSpec(memory_space=pltpu.HBM)


def body(activations, pre_activation, pooled_grad, weights, master, velocity, bn_params, bn_velocity):
    msg, conv, act, pre, pool = pl.pallas_call(
        stats_kernel,
        out_shape=(
            pltpu.VMEM((STAT_ROWS, 128), f32),
            pltpu.VMEM((ROWS, COUT), bf16),
            pltpu.VMEM((ROWS, CIN), bf16),
            pltpu.VMEM((IMG, PIX, COUT), bf16),
            pltpu.VMEM((IMG, COUT), f32),
        ),
        in_specs=[HBM] * 4,
        out_specs=(VMEM,) * 5,
        scratch_shapes=[
            pltpu.VMEM((IMG, PIX, CIN), bf16),
            pltpu.VMEM((CIN, COUT), bf16),
            pltpu.SemaphoreType.DMA((4, PARTS)),
        ],
        compiler_params=params(56),
        name="conv_stats",
    )(activations, pre_activation, pooled_grad, weights)
    chip = pl.pallas_call(
        chip_kernel,
        out_shape=shape((N_Z, STAT_ROWS, 128), f32),
        in_specs=[VMEM],
        out_specs=VMEM,
        compiler_params=params(),
        name="chip_stats",
    )(lax.all_gather(msg, "core"))
    stats = lax.all_to_all(chip, "z", 0, 0)
    sent, act, send, line, vectors = pl.pallas_call(
        grad_kernel,
        out_shape=(
            shape((ROWS, WIDE), bf16),
            shape((ROWS, CIN), bf16),
            shape((CIN, WIDE), bf16),
            shape((8, 128), f32),
            shape((40, 128), f32),
        ),
        in_specs=[VMEM] * 7,
        out_specs=(VMEM,) * 5,
        scratch_shapes=[pltpu.VMEM((16, 128), f32)],
        compiler_params=params(),
        name="conv_grad",
    )(stats, msg, conv, act, pre, pool, bn_params)
    swap = [(0, 1), (1, 0)]
    got = lax.ppermute(send, "core", swap)
    kept, keep = pl.pallas_call(
        keep_kernel,
        out_shape=(shape((ROWS, WIDE), bf16), shape((CIN, WIDE), f32)),
        in_specs=[VMEM] * 5,
        out_specs=(VMEM,) * 2,
        compiler_params=params(),
        cost_estimate=pl.CostEstimate(flops=2 * ROWS * CIN * WIDE, bytes_accessed=4 << 20, transcendentals=0),
        name="keep_grad",
    )(vectors, conv, pre, pool, act)
    input_grad = pl.pallas_call(
        back_kernel,
        out_shape=shape((IMG, PIX, CIN), bf16),
        in_specs=[VMEM] * 3,
        out_specs=VMEM,
        compiler_params=params(),
        cost_estimate=pl.CostEstimate(flops=2 * ROWS * CIN * COUT, bytes_accessed=4 << 20, transcendentals=0),
        name="input_grad",
    )(sent, kept, weights)
    halves = pl.pallas_call(
        pair_kernel,
        out_shape=shape((CIN, WIDE), bf16),
        in_specs=[VMEM] * 2,
        out_specs=VMEM,
        compiler_params=params(),
        name="pair_sum",
    )(keep, got)
    arrived = lax.all_to_all(halves.reshape(N_X, CIN // N_X, WIDE), "x", 0, 0)
    lines = pl.pallas_call(
        line_kernel,
        out_shape=shape((4, 16, 8, 128), bf16),
        in_specs=[VMEM],
        out_specs=VMEM,
        compiler_params=params(),
        name="line_sum",
    )(arrived)
    arrived = lax.all_to_all(lines.reshape(N_Y * N_Z, 8, 128), PLANE, 0, 0)
    block = pl.pallas_call(
        block_kernel,
        out_shape=shape((N_Y * N_Z, SIDE_ROWS, 128), bf16),
        in_specs=[VMEM] * 4,
        out_specs=VMEM,
        compiler_params=params(),
        name="block_sum",
    )(arrived, line, master, velocity)
    wide = pl.pallas_call(
        plane_kernel,
        out_shape=shape((N_X, WIDE_ROWS, 128), bf16),
        in_specs=[VMEM],
        out_specs=VMEM,
        compiler_params=params(),
        name="plane_join",
    )(lax.all_to_all(block, PLANE, 0, 0))
    mine = lax.all_to_all(wide, "x", 0, 0)
    other = lax.ppermute(mine, "core", swap)
    new_master, new_velocity, new_weights, new_bn, new_bn_velocity = pl.pallas_call(
        update_kernel,
        out_shape=(
            shape((16, 64), f32),
            shape((16, 64), f32),
            shape((CIN, COUT), bf16),
            shape((2, COUT), f32),
            shape((2, COUT), f32),
        ),
        in_specs=[VMEM] * 7,
        out_specs=(HBM,) * 5,
        scratch_shapes=[
            pltpu.VMEM((16, 64), f32),
            pltpu.VMEM((16, 64), f32),
            pltpu.VMEM((CIN, COUT), bf16),
            pltpu.VMEM((2, COUT), f32),
            pltpu.VMEM((2, COUT), f32),
            pltpu.SemaphoreType.DMA((N_X,)),
            pltpu.SemaphoreType.DMA((4,)),
        ],
        compiler_params=params(),
        name="update",
    )(mine, other, weights, master, velocity, bn_params, bn_velocity)
    return input_grad, new_master, new_velocity, new_weights, new_bn, new_bn_velocity


def solution(mesh):
    fine = Mesh(mesh.devices.reshape(4, 8, 8, 2), ALL)
    block = P(("x", "y"), ("z", "core"))
    return jax.shard_map(
        body,
        mesh=fine,
        in_specs=(P(ALL, None, None), P(ALL, None, None), P(ALL, None), P(), block, block, P(), P()),
        out_specs=(P(ALL, None, None), block, block, P(), P(), P()),
        check_vma=False,
    )
```

```python
import jax
import jax.numpy as jnp
from jax import lax
from jax.experimental import pallas as pl
from jax.experimental.pallas import tpu as pltpu
from jax.sharding import Mesh, PartitionSpec as P

epsilon = 1e-05
trust_coef = 0.001
weight_decay = 0.0001
momentum = 0.9
learn_rate = 12.0

IMG, PIX, STRIDE = 12, 49, 64
CIN, COUT = 512, 1024
ROWS = IMG * STRIDE
WIDE = COUT // 2
N_ROW, N_COL = 32, 16
N_X, N_Y, N_Z = 4, 8, 8
M = PIX * IMG * N_COL
BATCH = IMG * N_ROW * N_COL
CHUNKS = COUT // 128
PLANE, ALL = ("y", "z"), ("x", "y", "z", "core")
STAT_ROWS = 40
SIDE_ROWS = 24
WIDE_ROWS = 1056
PARTS = 2
STRIP = 256
bf16, f32 = jnp.bfloat16, jnp.float32


def params(megabytes=20):
    return pltpu.CompilerParams(vmem_limit_bytes=megabytes << 20)


def fold(line):
    return jnp.concatenate([line[:, 128 * k : 128 * k + 128] for k in range(line.shape[1] // 128)], axis=0)


def unfold(block):
    return jnp.concatenate([block[k : k + 1] for k in range(block.shape[0])], axis=1)


def split(line):
    high = line.astype(bf16).astype(f32)
    middle = (line - high).astype(bf16).astype(f32)
    return high, middle, line - high - middle


def rows_of(count, lines, dims):
    row = lax.broadcasted_iota(jnp.int32, dims, 0)
    block = jnp.zeros(dims, f32)
    for k in range(count):
        block = jnp.where(row == k, jnp.broadcast_to(lines[k], dims), block)
    return block


def stats_kernel(act_hbm, pre_hbm, pool_hbm, w_hbm, msg_ref, conv, actp, pre, pool, act, w, sem_in):
    step = IMG // PARTS
    loads = []
    for k in range(PARTS):
        part = pl.ds(step * k, step)
        strip = pl.ds(CIN // PARTS * k, CIN // PARTS)
        loads.append(pltpu.make_async_copy(w_hbm.at[strip], w.at[strip], sem_in.at[0, k]))
        loads.append(pltpu.make_async_copy(act_hbm.at[part], act.at[part], sem_in.at[1, k]))
    for copy in loads:
        copy.start()
    later = [pltpu.make_async_copy(pool_hbm, pool, sem_in.at[3, 0])]
    for k in range(PARTS):
        part = pl.ds(step * k, step)
        later.append(pltpu.make_async_copy(pre_hbm.at[part], pre.at[part], sem_in.at[2, k]))
    for copy in later:
        copy.start()
    actp[...] = jnp.zeros_like(actp)
    for copy in loads:
        copy.wait()
    for i in range(IMG):
        actp[STRIDE * i : STRIDE * i + PIX, :] = act[i]
    act_total = actp[...].astype(f32).reshape(IMG, STRIDE, CIN)[:, :56]
    act_total = jnp.sum(jnp.sum(act_total, axis=0), axis=0, keepdims=True)
    strips = [slice(STRIP * k, STRIP * k + STRIP) for k in range(COUT // STRIP)]
    lines = []
    for strip in strips:
        value = jnp.dot(actp[...], w[:, strip], preferred_element_type=f32).astype(bf16)
        conv[:, strip] = value
        value = value.astype(f32).reshape(IMG, STRIDE, STRIP)[:, :56]
        total = jnp.sum(jnp.sum(value, axis=0), axis=0, keepdims=True)
        square = jnp.sum(jnp.sum(value * value, axis=0), axis=0, keepdims=True)
        lines.append([total, square])
    for copy in later:
        copy.wait()
    for k, strip in enumerate(strips):
        wide, last = (8, STRIP), (1, STRIP)
        up, up_conv = jnp.zeros(wide, f32), jnp.zeros(wide, f32)
        up_last, up_conv_last = jnp.zeros(last, f32), jnp.zeros(last, f32)
        for i in range(IMG):
            value = conv[STRIDE * i : STRIDE * i + STRIDE, strip].astype(f32)[:PIX]
            passed = pre[i, :, strip].astype(f32) > 0
            share = pool[i : i + 1, strip] / PIX
            ones = jnp.where(passed, 1.0, 0.0)
            value = jnp.where(passed, value, 0.0)
            up += share * jnp.sum(ones[:48].reshape(6, 8, STRIP), axis=0)
            up_conv += share * jnp.sum(value[:48].reshape(6, 8, STRIP), axis=0)
            up_last += share * ones[48:49]
            up_conv_last += share * value[48:49]
        up = jnp.sum(up, axis=0, keepdims=True) + up_last
        up_conv = jnp.sum(up_conv, axis=0, keepdims=True) + up_conv_last
        lines[k] += [up, up_conv]
    sums = [fold(jnp.concatenate([line[q] for line in lines], axis=1)) for q in range(4)]
    msg = jnp.concatenate(sums + [fold(act_total), jnp.zeros((4, 128), f32)], axis=0)
    msg_ref[...] = msg


def chip_kernel(got_ref, out_ref):
    out_ref[...] = jnp.broadcast_to((got_ref[0] + got_ref[1])[None], out_ref.shape)


def fill(vectors, half, conv_ref, pre_ref, pool_ref, cg_ref):
    columns = pl.ds(pl.multiple_of(half * WIDE, WIDE), WIDE)
    mean, scale, shift, slope, cg_total = [
        unfold(jnp.where(half == 0, vectors[8 * k : 8 * k + 4], vectors[8 * k + 4 : 8 * k + 8])) for k in range(5)
    ]
    for i in range(IMG):
        cg_ref[STRIDE * i + 48 : STRIDE * i + 64, :] = jnp.zeros((16, WIDE), bf16)
        conv = conv_ref[STRIDE * i : STRIDE * i + STRIDE, columns].astype(f32)[:PIX]
        on = scale * (pool_ref[i : i + 1, columns] / PIX) - shift
        cg = jnp.where(pre_ref[i, :, columns].astype(f32) > 0, on, -shift) - slope * (conv - mean)
        cg_ref[STRIDE * i : STRIDE * i + PIX, :] = cg.astype(bf16)
    high, middle, rest = split(cg_total)
    edge = cg_ref[48:64, :].astype(f32)
    cg_ref[48:64, :] = (edge + rows_of(4, [jnp.zeros_like(high), high, middle, rest], edge.shape)).astype(bf16)


def product(actp, cg_ref):
    return lax.dot_general(actp[...], cg_ref[...], (((0,), (0,)), ((), ())), preferred_element_type=f32)


def core_of():
    return lax.axis_index("core").astype(jnp.int32)


def grad_kernel(
    stat_ref, msg_ref, conv_ref, act_ref, pre_ref, pool_ref, bn_ref, cg_ref, actp, send_ref, line_ref, vec_ref, lines
):
    core, layer = core_of(), lax.axis_index("z").astype(jnp.int32)
    sums = jnp.sum(stat_ref[...], axis=0)
    sum_up = sums[16:24]
    act_mean = (unfold(sums[32:36]) / M).astype(bf16).astype(f32)
    mean = sums[0:8] / M
    variance = sums[8:16] / M - mean * mean
    rstd = lax.rsqrt(variance + epsilon)
    sum_upx = rstd * (sums[24:32] - mean * sum_up)
    lines[0:8, :] = sum_up
    lines[8:16, :] = sum_upx
    line_ref[...] = jnp.broadcast_to(lines[pl.ds(core * 8 + layer, 1), :], (8, 128))
    scale = fold(bn_ref[0:1, :]) * rstd
    shift = scale * (sum_up / M)
    slope = scale * (sum_upx / M) * rstd
    local = IMG * PIX
    cg_total = scale * msg_ref[16:24, :] - local * shift - slope * (msg_ref[0:8, :] - local * mean)
    vectors = jnp.concatenate([mean, scale, shift, slope, cg_total], axis=0)
    vec_ref[...] = vectors
    actp[...] = act_ref[...]
    edge = actp[48:64, :].astype(f32)
    row = lax.broadcasted_iota(jnp.int32, edge.shape, 0)
    actp[48:64, :] = jnp.where((row >= 1) & (row < 4), -act_mean, edge).astype(bf16)
    fill(vectors, 1 - core, conv_ref, pre_ref, pool_ref, cg_ref)
    send_ref[...] = product(actp, cg_ref).astype(bf16)


def keep_kernel(vec_ref, conv_ref, pre_ref, pool_ref, actp, cg_ref, keep_ref):
    fill(vec_ref[...], core_of(), conv_ref, pre_ref, pool_ref, cg_ref)
    keep_ref[...] = product(actp, cg_ref)


def back_kernel(sent_ref, kept_ref, w_ref, out_ref):
    core = core_of()
    back = jnp.zeros((ROWS, CIN), f32)
    for half, cg_ref in ((1 - core, sent_ref), (core, kept_ref)):
        w = w_ref[:, pl.ds(pl.multiple_of(half * WIDE, WIDE), WIDE)]
        back += lax.dot_general(cg_ref[...], w, (((1,), (1,)), ((), ())), preferred_element_type=f32)
    for i in range(IMG):
        out_ref[i] = back[STRIDE * i : STRIDE * i + PIX].astype(bf16)


def pair_kernel(keep_ref, got_ref, out_ref):
    out_ref[...] = (keep_ref[...] + got_ref[...].astype(f32)).astype(bf16)


def line_kernel(got_ref, out_ref):
    total = jnp.sum(got_ref[...].astype(f32), axis=0).reshape(16, 8, WIDE)
    for j in range(4):
        out_ref[j] = total[:, :, 128 * j : 128 * j + 128].astype(bf16)


def block_kernel(got_ref, line_ref, master_ref, vel_ref, out_ref):
    total = jnp.sum(got_ref[...].astype(f32), axis=0) * (1.0 / BATCH)
    master = master_ref[...]
    decayed = master - momentum * vel_ref[...]
    decayed = jnp.concatenate([decayed[:8], decayed[8:]], axis=1)
    norm = jnp.sum(jnp.sum(master * master, axis=1, keepdims=True), axis=0, keepdims=True)
    square = jnp.sum(jnp.sum(total * total, axis=1, keepdims=True), axis=0, keepdims=True)
    norms = split(jnp.broadcast_to(norm, (8, 128))) + split(jnp.broadcast_to(square, (8, 128)))[:2]
    extra = rows_of(8, split(line_ref[...]) + norms, (8, 128))
    block = jnp.concatenate([total, decayed, extra], axis=0).astype(bf16)
    out_ref[...] = jnp.broadcast_to(block[None], out_ref.shape)


def plane_kernel(got_ref, out_ref):
    got = got_ref[...].astype(f32)
    extra = jnp.sum(got[:, 16:24, :].reshape(N_Y, N_Z, 8, 128), axis=0)
    lines = []
    norm = jnp.zeros((1, 128), f32)
    square = jnp.zeros((1, 128), f32)
    for z in range(N_Z):
        lines += split(extra[z, 0:1] + extra[z, 1:2] + extra[z, 2:3])
        norm += extra[z, 3:4] + extra[z, 4:5] + extra[z, 5:6]
        square += extra[z, 6:7] + extra[z, 7:8]
    lines += split(norm) + split(square)
    extra = jnp.concatenate(lines + [jnp.zeros((2, 128), f32)], axis=0).astype(bf16)
    grad = got[:, 0:8, :].reshape(512, 128).astype(bf16)
    decayed = got[:, 8:16, :].reshape(512, 128).astype(bf16)
    for p in range(N_X):
        out_ref[p, 0:512, :] = grad
        out_ref[p, 512:1024, :] = decayed
        out_ref[p, 1024:1056, :] = extra


def update_kernel(
    mine_ref, other_ref, w_ref, master_ref, vel_ref, bn_ref, bnv_ref,
    new_master_hbm, new_vel_hbm, new_w_hbm, new_bn_hbm, new_bnv_hbm,
    new_master_ref, new_vel_ref, new_w, new_bn_ref, new_bnv_ref, sems, small_sems,
):
    core, layer = core_of(), lax.axis_index("z").astype(jnp.int32)
    row = (lax.axis_index("x") * N_Y + lax.axis_index("y")).astype(jnp.int32)

    def run(parts):
        square = jnp.zeros((1, 128), f32)
        norm = jnp.zeros((1, 128), f32)
        totals = []
        for part in parts:
            extra = jnp.zeros((32, 128), f32)
            for x in range(N_X):
                extra += part[x, 1024:1056, :].astype(f32)
            line = [extra[3 * z : 3 * z + 1] + extra[3 * z + 1 : 3 * z + 2] + extra[3 * z + 2 : 3 * z + 3] for z in range(N_Z)]
            norm += extra[24:25] + extra[25:26] + extra[26:27]
            square += extra[27:28] + extra[28:29] + extra[29:30]
            totals.append(jnp.concatenate(line, axis=1))
        wnorm = jnp.sqrt(norm[:, 0:1])
        gnorm = jnp.sqrt(square[:, 0:1])
        rate = learn_rate * (trust_coef * wnorm / (gnorm + weight_decay * wnorm))
        bn_grad = jnp.concatenate([totals[1], totals[0]], axis=0) * (1.0 / BATCH)
        new_bnv = momentum * bnv_ref[...] + learn_rate * bn_grad
        new_bnv_ref[...] = new_bnv
        new_bn_ref[...] = bn_ref[...] - new_bnv
        for h in range(2):

            @pl.when(layer // 4 == h)
            def _():
                start = pl.multiple_of(layer % 4 * 128 + row % 8 * 16, 16)
                pair = parts[h][row // 8, pl.ds(start, 16), :].astype(f32)
                own = jnp.where(core == 0, pair[:, :64], pair[:, 64:])
                new_vel = momentum * vel_ref[...] + rate * (own + weight_decay * master_ref[...])
                new_vel_ref[...] = new_vel
                new_master_ref[...] = master_ref[...] - new_vel

        small_pairs = (
            (new_master_ref, new_master_hbm),
            (new_vel_ref, new_vel_hbm),
            (new_bn_ref, new_bn_hbm),
            (new_bnv_ref, new_bnv_hbm),
        )
        stores = [pltpu.make_async_copy(here, there, small_sems.at[k]) for k, (here, there) in enumerate(small_pairs)]
        for copy in stores:
            copy.start()
        for x in range(N_X):
            tiles = [part[x, 512:1024, :].astype(f32).reshape(N_Y, N_Z, 8, 128) for part in parts]
            rows = slice(128 * x, 128 * x + 128)
            for z in range(N_Z):
                columns = slice(128 * z, 128 * z + 128)
                even, odd = [tile[:, z] for tile in tiles]
                top = jnp.concatenate([even[:, :, :64], odd[:, :, :64]], axis=2)
                bottom = jnp.concatenate([even[:, :, 64:], odd[:, :, 64:]], axis=2)
                decayed = jnp.stack([top, bottom], axis=1).reshape(128, 128)
                lines = slice(128 * (z % 4), 128 * (z % 4) + 128)
                step = parts[z // 4][x, lines, :].astype(f32)
                step += weight_decay * w_ref[rows, columns].astype(f32)
                new_w[rows, columns] = (decayed - rate * step).astype(bf16)
            stores.append(pltpu.make_async_copy(new_w.at[rows], new_w_hbm.at[rows], sems.at[x]))
            stores[-1].start()
        for copy in stores:
            copy.wait()

    @pl.when(core == 0)
    def _():
        run((mine_ref, other_ref))

    @pl.when(core == 1)
    def _():
        run((other_ref, mine_ref))


def shape(dims, kind):
    return jax.ShapeDtypeStruct(dims, kind)


VMEM = pl.BlockSpec(memory_space=pltpu.VMEM)
HBM = pl.BlockSpec(memory_space=pltpu.HBM)


def body(activations, pre_activation, pooled_grad, weights, master, velocity, bn_params, bn_velocity):
    msg, conv, act, pre, pool = pl.pallas_call(
        stats_kernel,
        out_shape=(
            pltpu.VMEM((STAT_ROWS, 128), f32),
            pltpu.VMEM((ROWS, COUT), bf16),
            pltpu.VMEM((ROWS, CIN), bf16),
            pltpu.VMEM((IMG, PIX, COUT), bf16),
            pltpu.VMEM((IMG, COUT), f32),
        ),
        in_specs=[HBM] * 4,
        out_specs=(VMEM,) * 5,
        scratch_shapes=[
            pltpu.VMEM((IMG, PIX, CIN), bf16),
            pltpu.VMEM((CIN, COUT), bf16),
            pltpu.SemaphoreType.DMA((4, PARTS)),
        ],
        compiler_params=params(56),
        name="conv_stats",
    )(activations, pre_activation, pooled_grad, weights)
    chip = pl.pallas_call(
        chip_kernel,
        out_shape=shape((N_Z, STAT_ROWS, 128), f32),
        in_specs=[VMEM],
        out_specs=VMEM,
        compiler_params=params(),
        name="chip_stats",
    )(lax.all_gather(msg, "core"))
    stats = lax.all_to_all(chip, "z", 0, 0)
    sent, act, send, line, vectors = pl.pallas_call(
        grad_kernel,
        out_shape=(
            shape((ROWS, WIDE), bf16),
            shape((ROWS, CIN), bf16),
            shape((CIN, WIDE), bf16),
            shape((8, 128), f32),
            shape((40, 128), f32),
        ),
        in_specs=[VMEM] * 7,
        out_specs=(VMEM,) * 5,
        scratch_shapes=[pltpu.VMEM((16, 128), f32)],
        compiler_params=params(),
        name="conv_grad",
    )(stats, msg, conv, act, pre, pool, bn_params)
    swap = [(0, 1), (1, 0)]
    got = lax.ppermute(send, "core", swap)
    kept, keep = pl.pallas_call(
        keep_kernel,
        out_shape=(shape((ROWS, WIDE), bf16), shape((CIN, WIDE), f32)),
        in_specs=[VMEM] * 5,
        out_specs=(VMEM,) * 2,
        compiler_params=params(),
        cost_estimate=pl.CostEstimate(flops=2 * ROWS * CIN * WIDE, bytes_accessed=4 << 20, transcendentals=0),
        name="keep_grad",
    )(vectors, conv, pre, pool, act)
    input_grad = pl.pallas_call(
        back_kernel,
        out_shape=shape((IMG, PIX, CIN), bf16),
        in_specs=[VMEM] * 3,
        out_specs=VMEM,
        compiler_params=params(),
        cost_estimate=pl.CostEstimate(flops=2 * ROWS * CIN * COUT, bytes_accessed=4 << 20, transcendentals=0),
        name="input_grad",
    )(sent, kept, weights)
    halves = pl.pallas_call(
        pair_kernel,
        out_shape=shape((CIN, WIDE), bf16),
        in_specs=[VMEM] * 2,
        out_specs=VMEM,
        compiler_params=params(),
        name="pair_sum",
    )(keep, got)
    arrived = lax.all_to_all(halves.reshape(N_X, CIN // N_X, WIDE), "x", 0, 0)
    lines = pl.pallas_call(
        line_kernel,
        out_shape=shape((4, 16, 8, 128), bf16),
        in_specs=[VMEM],
        out_specs=VMEM,
        compiler_params=params(),
        name="line_sum",
    )(arrived)
    arrived = lax.all_to_all(lines.reshape(N_Y * N_Z, 8, 128), PLANE, 0, 0)
    block = pl.pallas_call(
        block_kernel,
        out_shape=shape((N_Y * N_Z, SIDE_ROWS, 128), bf16),
        in_specs=[VMEM] * 4,
        out_specs=VMEM,
        compiler_params=params(),
        name="block_sum",
    )(arrived, line, master, velocity)
    wide = pl.pallas_call(
        plane_kernel,
        out_shape=shape((N_X, WIDE_ROWS, 128), bf16),
        in_specs=[VMEM],
        out_specs=VMEM,
        compiler_params=params(),
        name="plane_join",
    )(lax.all_to_all(block, PLANE, 0, 0))
    mine = lax.all_to_all(wide, "x", 0, 0)
    other = lax.ppermute(mine, "core", swap)
    new_master, new_velocity, new_weights, new_bn, new_bn_velocity = pl.pallas_call(
        update_kernel,
        out_shape=(
            shape((16, 64), f32),
            shape((16, 64), f32),
            shape((CIN, COUT), bf16),
            shape((2, COUT), f32),
            shape((2, COUT), f32),
        ),
        in_specs=[VMEM] * 7,
        out_specs=(HBM,) * 5,
        scratch_shapes=[
            pltpu.VMEM((16, 64), f32),
            pltpu.VMEM((16, 64), f32),
            pltpu.VMEM((CIN, COUT), bf16),
            pltpu.VMEM((2, COUT), f32),
            pltpu.VMEM((2, COUT), f32),
            pltpu.SemaphoreType.DMA((N_X,)),
            pltpu.SemaphoreType.DMA((4,)),
        ],
        compiler_params=params(),
        name="update",
    )(mine, other, weights, master, velocity, bn_params, bn_velocity)
    return input_grad, new_master, new_velocity, new_weights, new_bn, new_bn_velocity


def solution(mesh):
    fine = Mesh(mesh.devices.reshape(4, 8, 8, 2), ALL)
    block = P(("x", "y"), ("z", "core"))
    return jax.shard_map(
        body,
        mesh=fine,
        in_specs=(P(ALL, None, None), P(ALL, None, None), P(ALL, None), P(), block, block, P(), P()),
        out_specs=(P(ALL, None, None), block, block, P(), P(), P()),
        check_vma=False,
    )
```
